32 devices in a mesh: pool: 4 (over x, core), dp: 8 (over z, y).
Axes of the slice: x: 2, y: 2, z: 4, core: 2. Of those that a mesh axis runs over, the one named last changes fastest.
Arguments:
- activations: bfloat16 [4096, 8192], P('dp', 'pool')
- gradient: bfloat16 [8192, 28672], P('pool', 'dp')
- owner_slot: int32 [4, 4], replicated, may hold values from 0 to 15, as said below
Outputs:
- update: bfloat16 [8192, 28672], P('pool', 'dp')
- owned_roots: bfloat16 [4, 16, 512, 512], P('pool', 'dp')
The draws below stay inside these ranges and needn't reach their ends.
Inputs may be any that keep to these rules, and one draw needn't show every extreme that they name: `owner_slot`: in each row the 4 entries are distinct; entry e names slot e % 2 of the device e // 2 along dp within that group; in every row some device holds 2 of the row's blocks.
All inputs are finite; a program needn't handle non-finite values. Where the reference program divides by a largest or mean magnitude, that divisor is 1e-20 or more.
Results may differ from the reference program's by a relative error of at most 0.0053.
Values may be sent and summed in bfloat16 or wider, within the bound.
No kernel may reach another device: no remote copies, remote signals or barrier semaphores. Data moves between devices by JAX's collectives and lax.ppermute only.
A program may use at most 192 MiB of HBM per device.

```python
import math
import jax
import jax.numpy as jnp
from jax import lax

D = 8192
FF = 28672
BLK = 512
ITERS = 3
SLOTS = 2
GROUPS = 4
PEERS = 8
NSG = 4
TOKENS = 4096


def draw_activations(key, part):
    key = jax.random.fold_in(key, 11)
    first = jax.random.fold_in(key, 0)
    second = jax.random.fold_in(key, 1)
    third = jax.random.fold_in(key, 2)
    fifth = jax.random.fold_in(key, 4)
    sixth = jax.random.fold_in(key, 5)
    blocks = D // BLK
    lead = 2.0 * math.isqrt(BLK)
    mix_noise = jax.random.randint(fifth, (blocks, BLK, BLK), -2, 3).astype(jnp.float32)
    mixing = mix_noise + lead * jnp.eye(BLK, dtype=jnp.float32)[None]
    base = (jax.random.randint(first, (TOKENS, D), -6, 7) + jax.random.randint(sixth, (TOKENS, D), -6, 7)).astype(jnp.float32)
    base_var = 28.0
    column_scale = jnp.exp(jax.random.uniform(second, (1, D), jnp.float32) * math.log(10.0))
    mixed = jnp.einsum('tka,kab->tkb', base.reshape(TOKENS, blocks, BLK), mixing, precision=lax.Precision.HIGHEST, preferred_element_type=jnp.float32).reshape(TOKENS, D)
    normalizer = 1.0 / math.sqrt(base_var * (lead * lead + 2.0 * (BLK - 1)))
    block_number = (jnp.arange(D, dtype=jnp.int32) // BLK).astype(jnp.float32)[None, :]
    block_scale = jnp.exp(block_number * (math.log(10.0) / blocks))
    position = jnp.arange(TOKENS, dtype=jnp.float32)[:, None] / (TOKENS - 1)
    jitter = jnp.exp(jax.random.uniform(third, (TOKENS, 1), jnp.float32, -0.35, 0.35))
    row_scale = (1.0 + 2.0 * position) * jitter
    return (mixed * normalizer * column_scale * block_scale * row_scale).astype(jnp.bfloat16)


def draw_gradient(key, part):
    key = jax.random.fold_in(key, 17)
    first, second, third = jax.random.split(key, 3)
    shared = jax.random.normal(third, (1, FF), jnp.float32)
    ramp = 3.0 * jnp.arange(FF, dtype=jnp.float32)[None, :] / (FF - 1)
    base = jax.random.normal(first, (D, FF), jnp.float32)
    column_scale = jnp.exp(jax.random.uniform(second, (1, FF), jnp.float32) * math.log(4.0))
    base = base + ramp * shared
    position = jnp.arange(D, dtype=jnp.float32)[:, None] / (D - 1)
    return (base * column_scale * (1.0 + 2.0 * position)).astype(jnp.bfloat16)


def draw_owner_slot(key, part):
    key = jax.random.fold_in(key, 23)
    table_rows = []
    for group in range(GROUPS):
        group_key = jax.random.fold_in(key, group)
        pick_key, slot_key, order_key = jax.random.split(group_key, 3)
        devices = jax.random.permutation(pick_key, PEERS)[:NSG - 1].astype(jnp.int32)
        slot_draw = jax.random.randint(slot_key, (NSG,), 0, SLOTS).astype(jnp.int32)
        shared_base = devices[0] * SLOTS
        entries = jnp.concatenate([jnp.stack([shared_base, shared_base + 1]), devices[1:] * SLOTS + slot_draw[2:]])
        order = jax.random.permutation(order_key, NSG)
        table_rows.append(entries[order].astype(jnp.int32))
    return jnp.stack(table_rows).astype(jnp.int32)


def setup_inputs(seed: int = 0) -> dict:
    key_of = jax.random.split(jax.random.key(seed), 4)
    activations = draw_activations(jax.random.fold_in(key_of[3], 71), 0)
    gradient = draw_gradient(jax.random.fold_in(key_of[3], 71), 0)
    owner_slot = draw_owner_slot(jax.random.fold_in(key_of[3], 71), 0)
    return dict(activations=activations, gradient=gradient, owner_slot=owner_slot)


damping = 0.01

def full_dot(left, right):
    return jnp.dot(left, right, precision=lax.Precision.HIGHEST, preferred_element_type=jnp.float32)

def inverse_root(stat):
    identity = jnp.eye(BLK, dtype=jnp.float32)
    matrix = stat + damping * identity
    bound = jnp.max(lax.optimization_barrier(jnp.sum(jnp.abs(matrix), axis=1)))
    scale = 2.0 / bound
    iterate = scale * matrix
    estimate = jnp.sqrt(jnp.sqrt(scale)) * identity
    for step in range(ITERS):
        factor = (5.0 * identity - iterate) / 4.0
        estimate = full_dot(estimate, factor)
        square = full_dot(factor, factor)
        fourth = full_dot(square, square)
        iterate = full_dot(fourth, iterate)
    return estimate

def reference(activations, gradient, owner_slot):
    count = D // BLK
    roots = []
    for block in range(count):
        columns = activations[:, block * BLK:(block + 1) * BLK]
        stat = jnp.dot(columns.T, columns, preferred_element_type=jnp.float32) / TOKENS
        roots.append(inverse_root(stat).astype(jnp.bfloat16))
    owned = jnp.zeros((GROUPS, PEERS * SLOTS, BLK, BLK), jnp.bfloat16)
    for group in range(GROUPS):
        for inner in range(NSG):
            owned = owned.at[group, owner_slot[group, inner]].set(roots[group * NSG + inner])
    pieces = []
    usq = jnp.float32(0.0)
    for block in range(count):
        piece = jnp.dot(roots[block], gradient[block * BLK:(block + 1) * BLK], preferred_element_type=jnp.float32)
        usq = usq + jnp.sum(piece * piece)
        pieces.append(piece)
    gsq = jnp.sum(jnp.square(gradient.astype(jnp.float32)))
    ratio = jnp.sqrt(gsq / (usq + 1e-06))
    update = jnp.concatenate([(piece * ratio).astype(jnp.bfloat16) for piece in pieces], axis=0)
    return (update, owned)
```

```python
import functools

import jax
import jax.numpy as jnp
from jax import lax
from jax.experimental import pallas as pl
from jax.experimental.pallas import tpu as pltpu
from jax.sharding import PartitionSpec as P

BLK = 512
HALF = BLK // 2
TAIL = HALF + 16
ITERS = 3
SLOTS = 2
QUAD = 4

damping = 0.01
F32 = jnp.float32
BF16 = jnp.bfloat16
SMEM = pl.BlockSpec(memory_space=pltpu.SMEM)
VMEM = pl.BlockSpec(memory_space=pltpu.VMEM)


def params(mib):
    return pltpu.CompilerParams(vmem_limit_bytes=mib * 2**20)


def dot(left, right, dims=((1,), (0,))):
    return lax.dot_general(left, right, (dims, ((), ())), preferred_element_type=F32)


def places():
    row = lax.broadcasted_iota(jnp.int32, (HALF, HALF), 0)
    col = lax.broadcasted_iota(jnp.int32, (HALF, HALF), 1)
    return row, col


def fold(first, last):
    row, col = places()
    body = jnp.where(row <= col, first, last)
    diagonal = jnp.sum(jnp.where(row == col, last, 0.0), axis=0, keepdims=True)
    return body, jnp.broadcast_to(diagonal, (TAIL - HALF, HALF))


def unfold(body, diagonal):
    row, col = places()
    turned = body.T
    first = jnp.where(row <= col, body, turned)
    last = jnp.where(row > col, body, jnp.where(row < col, turned, diagonal))
    return first, last


def stat_kernel(order, x_ref, *out):
    for place in (3, 1, 2, 0):
        start = pl.multiple_of(order[place] * BLK, BLK)
        left = x_ref[:, pl.ds(start, HALF)]
        right = x_ref[:, pl.ds(pl.multiple_of(start + HALF, HALF), HALF)]
        along = ((0,), (0,))
        out[2 * place][...] = dot(left, right, along).astype(BF16)
        body, diagonal = fold(dot(left, left, along), dot(right, right, along))
        out[2 * place + 1][:HALF] = body.astype(BF16)
        out[2 * place + 1][HALF:] = diagonal.astype(BF16)


def statistics(order, activations):
    shapes = [
        jax.ShapeDtypeStruct((rows, HALF), BF16) for _ in range(QUAD) for rows in (HALF, TAIL)
    ]
    return pl.pallas_call(
        stat_kernel,
        out_shape=shapes,
        in_specs=[SMEM, VMEM],
        out_specs=[VMEM] * len(shapes),
        compiler_params=params(32),
        name="statistics",
    )(order, activations)


def gram_kernel(order, g_ref, gram_ref):
    tile = g_ref[...]
    term = dot(tile, tile, ((1,), (1,)))

    @pl.when(pl.program_id(1) == 0)
    def _():
        gram_ref[0] = term

    @pl.when(pl.program_id(1) > 0)
    def _():
        gram_ref[0] += term


def tile_width(columns):
    for width in (1792, 896, 512, 256, 128):
        if columns % width == 0:
            return width
    return columns


def gram(order, gradient):
    rows, columns = gradient.shape
    width = tile_width(columns)
    return pl.pallas_call(
        gram_kernel,
        out_shape=jax.ShapeDtypeStruct((QUAD, BLK, BLK), F32),
        grid_spec=pltpu.PrefetchScalarGridSpec(
            num_scalar_prefetch=1,
            grid=(QUAD, columns // width),
            in_specs=[pl.BlockSpec((BLK, width), lambda s, j, order: (order[s], j))],
            out_specs=pl.BlockSpec((1, BLK, BLK), lambda s, j, order: (s, 0, 0)),
        ),
        compiler_params=params(32),
        cost_estimate=pl.CostEstimate(
            flops=2 * rows * columns * BLK,
            bytes_accessed=2 * rows * columns + 4 * QUAD * BLK * BLK,
            transcendentals=0,
        ),
        name="gram",
    )(order, gradient)


def product(left, right):
    return dot(left.astype(BF16), right.astype(BF16))


def newton_kernel(tokens, mine0, mine1, other0, other1, root0, root1, held):
    cross = (mine0[...].astype(F32) + other0[...].astype(F32)) / tokens
    rest = (mine1[...].astype(F32) + other1[...].astype(F32)) / tokens
    first, last = unfold(rest[:HALF], rest[HALF : HALF + 1])
    held[:HALF, :HALF] = first
    held[:HALF, HALF:] = cross
    held[HALF:, :HALF] = cross.T
    held[HALF:, HALF:] = last
    row = lax.broadcasted_iota(jnp.int32, (BLK, BLK), 0)
    col = lax.broadcasted_iota(jnp.int32, (BLK, BLK), 1)
    identity = jnp.where(row == col, 1.0, 0.0).astype(F32)
    matrix = held[...] + damping * identity
    bound = jnp.max(jnp.sum(jnp.abs(matrix), axis=0, keepdims=True), axis=1, keepdims=True)
    scale = 2.0 / bound
    iterate = matrix * scale
    estimate = None
    for step in range(ITERS):
        error = (identity - iterate) * 0.25
        if estimate is None:
            estimate = error
        else:
            estimate = estimate + error + product(estimate, error)
        if step + 1 < ITERS:
            square = 2.0 * error + product(error, error)
            fourth = 2.0 * square + product(square, square)
            iterate = iterate + product(fourth, iterate)
    held[...] = (estimate + identity) * jnp.sqrt(jnp.sqrt(scale))
    root0[...] = held[:HALF, HALF:].astype(BF16)
    body, diagonal = fold(held[:HALF, :HALF], held[HALF:, HALF:])
    root1[:HALF] = body.astype(BF16)
    root1[HALF:] = diagonal.astype(BF16)


def newton(tokens, *halves):
    return pl.pallas_call(
        functools.partial(newton_kernel, tokens),
        out_shape=[jax.ShapeDtypeStruct((rows, HALF), BF16) for rows in (HALF, TAIL)],
        in_specs=[VMEM] * 4,
        out_specs=[VMEM] * 2,
        scratch_shapes=[pltpu.VMEM((BLK, BLK), F32)],
        compiler_params=params(32),
        name="newton",
    )(*halves)


def norm_kernel(half0, half1, gram_ref, root_ref, total_ref):
    cross = half0[...].astype(F32)
    rest = half1[...].astype(F32)
    first, last = unfold(rest[:HALF], rest[HALF : HALF + 1])
    root_ref[:HALF, :HALF] = first.astype(BF16)
    root_ref[:HALF, HALF:] = cross.astype(BF16)
    root_ref[HALF:, :HALF] = cross.T.astype(BF16)
    root_ref[HALF:, HALF:] = last.astype(BF16)
    root = root_ref[...]
    weighted = dot(root, root) * gram_ref[0]
    total_ref[...] = jnp.sum(weighted, axis=0, keepdims=True).reshape(1, BLK)


def norm(place, half0, half1, grams):
    whole = lambda rows: pl.BlockSpec((rows, HALF), lambda i: (0, 0))
    return pl.pallas_call(
        norm_kernel,
        out_shape=[jax.ShapeDtypeStruct((BLK, BLK), BF16), jax.ShapeDtypeStruct((1, BLK), F32)],
        grid=(1,),
        in_specs=[
            whole(HALF),
            whole(TAIL),
            pl.BlockSpec((1, BLK, BLK), lambda i: (place, 0, 0)),
        ],
        out_specs=[
            pl.BlockSpec((BLK, BLK), lambda i: (0, 0)),
            pl.BlockSpec((1, BLK), lambda i: (0, 0)),
        ],
        compiler_params=params(32),
        cost_estimate=pl.CostEstimate(
            flops=2 * BLK**3, bytes_accessed=8 * BLK * BLK, transcendentals=0
        ),
        name="norm",
    )(half0, half1, grams)


def apply_kernel(order, slots, ratio, r0, r1, r2, r3, g_ref, update_ref, owned_ref, root):
    place, column = pl.program_id(0), pl.program_id(1)

    @pl.when((place == 0) & (column == 0))
    def _():
        owned_ref[...] = jnp.zeros_like(owned_ref)

    for one, packed in enumerate((r0, r1, r2, r3)):

        @pl.when((place == one) & (column == 0))
        def _():
            root[...] = packed[...]

    for slot in range(SLOTS):

        @pl.when((column == 0) & (slots[place] == slot))
        def _():
            owned_ref[slot] = root[...]

    update_ref[...] = (dot(root[...], g_ref[...]) * ratio[0]).astype(BF16)


def apply(order, slots, ratio, roots, gradient):
    rows, columns = gradient.shape
    width = tile_width(columns)
    square = pl.BlockSpec((BLK, BLK), lambda s, j, order, slots: (0, 0))
    tile = pl.BlockSpec((BLK, width), lambda s, j, order, slots: (order[s], j))
    return pl.pallas_call(
        apply_kernel,
        out_shape=[
            jax.ShapeDtypeStruct((rows, columns), BF16),
            jax.ShapeDtypeStruct((SLOTS, BLK, BLK), BF16),
        ],
        grid_spec=pltpu.PrefetchScalarGridSpec(
            num_scalar_prefetch=2,
            grid=(QUAD, columns // width),
            in_specs=[SMEM] + [square] * QUAD + [tile],
            out_specs=[
                tile,
                pl.BlockSpec((SLOTS, BLK, BLK), lambda s, j, order, slots: (0, 0, 0)),
            ],
            scratch_shapes=[pltpu.VMEM((BLK, BLK), BF16)],
        ),
        compiler_params=params(40),
        name="apply",
    )(order, slots, ratio, *roots, gradient)


def swap(value, flip, axis="dp"):
    count = lax.axis_size(axis)
    return lax.ppermute(value, axis, [(i, i ^ flip) for i in range(count)])


def total(value, *axes):
    for axis in axes:
        flip = 1
        while flip < lax.axis_size(axis):
            value = value + swap(value, flip, axis)
            flip *= 2
    return value


def add(*values):
    return sum(value.astype(F32) for value in values).astype(BF16)


def per_device(activations, gradient, owner_slot):
    peer_count = lax.axis_size("dp")
    my_index = lax.axis_index("dp")
    group_index = lax.axis_index("pool")
    tokens_all = activations.shape[0] * peer_count
    owner_row = lax.dynamic_index_in_dim(owner_slot, group_index, 0, keepdims=False)
    order = (my_index % QUAD) ^ jnp.arange(QUAD, dtype=jnp.int32)
    slots = owner_row[order] - my_index * SLOTS

    a0, a1, b0, b1, c0, c1, d0, d1 = statistics(order, activations)
    from_y = swap(d0, 1)
    from_z = swap(d1, 2)
    y0 = swap(b0, 1)
    z1 = swap(c1, 2)
    y1 = swap(add(b1, from_z), 1)
    z0 = swap(add(c0, from_y), 2)
    mine0 = add(a0, y0, z0)
    mine1 = add(a1, y1, z1)
    flip = QUAD
    other0, other1 = swap(mine0, flip), swap(mine1, flip)
    while 2 * flip < peer_count:
        mine0, mine1 = add(mine0, other0), add(mine1, other1)
        flip *= 2
        other0, other1 = swap(mine0, flip), swap(mine1, flip)

    grams = gram(order, gradient)
    a0, a1 = newton(tokens_all, mine0, mine1, other0, other1)
    c0 = swap(a0, 2)
    b1 = swap(a1, 1)
    c1 = swap(a1, 2)
    b0 = swap(a0, 1)
    d0 = swap(c0, 1)
    d1 = swap(b1, 2)
    roots, totals = zip(
        *[norm(place, *pair, grams) for place, pair in enumerate(((a0, a1), (b0, b1), (c0, c1), (d0, d1)))]
    )
    grad_square = sum(jnp.trace(grams[place]) for place in range(QUAD))
    update_square = jnp.sum(sum(totals))
    both = total(jnp.stack([grad_square, update_square]), "pool", "dp")
    ratio = jnp.sqrt(both[0] / (both[1] + 1e-06))
    update, owned = apply(order, slots, ratio[None], roots, gradient)
    return (update, owned[None])


def solution(mesh):
    in_specs = (P("dp", "pool"), P("pool", "dp"), P())
    out_specs = (P("pool", "dp"), P("pool", "dp", None, None))
    return jax.shard_map(
        per_device, mesh=mesh, in_specs=in_specs, out_specs=out_specs, check_vma=False
    )
```

```python
import functools

import jax
import jax.numpy as jnp
from jax import lax
from jax.experimental import pallas as pl
from jax.experimental.pallas import tpu as pltpu
from jax.sharding import PartitionSpec as P

BLK = 512
HALF = BLK // 2
TAIL = HALF + 16
ITERS = 3
SLOTS = 2
QUAD = 4
ROWS = 8
LANES = 128

damping = 0.01
F32 = jnp.float32
BF16 = jnp.bfloat16
SMEM = pl.BlockSpec(memory_space=pltpu.SMEM)
VMEM = pl.BlockSpec(memory_space=pltpu.VMEM)


def params(mib):
    return pltpu.CompilerParams(vmem_limit_bytes=mib * 2**20)


def dot(left, right, dims=((1,), (0,))):
    return lax.dot_general(left, right, (dims, ((), ())), preferred_element_type=F32)


def places():
    row = lax.broadcasted_iota(jnp.int32, (HALF, HALF), 0)
    col = lax.broadcasted_iota(jnp.int32, (HALF, HALF), 1)
    return row, col


def fold(first, last):
    row, col = places()
    body = jnp.where(row <= col, first, last)
    diagonal = jnp.sum(jnp.where(row == col, last, 0.0), axis=0, keepdims=True)
    return body, jnp.broadcast_to(diagonal, (TAIL - HALF, HALF))


def unfold(body, diagonal):
    row, col = places()
    turned = body.T
    first = jnp.where(row <= col, body, turned)
    last = jnp.where(row > col, body, jnp.where(row < col, turned, diagonal))
    return first, last


def stat_kernel(order, x_ref, *out):
    for place in (3, 1, 2, 0):
        start = pl.multiple_of(order[place] * BLK, BLK)
        left = x_ref[:, pl.ds(start, HALF)]
        right = x_ref[:, pl.ds(pl.multiple_of(start + HALF, HALF), HALF)]
        along = ((0,), (0,))
        out[2 * place][...] = dot(left, right, along).astype(BF16)
        body, diagonal = fold(dot(left, left, along), dot(right, right, along))
        out[2 * place + 1][:HALF] = body.astype(BF16)
        out[2 * place + 1][HALF:] = diagonal.astype(BF16)


def statistics(order, activations):
    shapes = [
        jax.ShapeDtypeStruct((rows, HALF), BF16) for _ in range(QUAD) for rows in (HALF, TAIL)
    ]
    return pl.pallas_call(
        stat_kernel,
        out_shape=shapes,
        in_specs=[SMEM, VMEM],
        out_specs=[VMEM] * len(shapes),
        compiler_params=params(16),
        name="statistics",
    )(order, activations)


def tile_width(columns):
    for width in (1792, 896, 512, 256, 128):
        if columns % width == 0:
            return width
    return columns


def chunks(width):
    start = 0
    while width - start >= 2 * BLK:
        yield pl.ds(start, BLK)
        start += BLK
    yield pl.ds(start, width - start)


def gram_kernel(order, after0, after1, g_ref, gram_ref, norm_ref):
    @pl.when(pl.program_id(1) == 0)
    def _():
        gram_ref[...] = jnp.zeros_like(gram_ref)

    for part in chunks(g_ref.shape[1]):
        tile = g_ref[:, part]
        gram_ref[0] += dot(tile, tile, ((1,), (1,)))

    @pl.when(pl.program_id(1) == pl.num_programs(1) - 1)
    def _():
        row = lax.broadcasted_iota(jnp.int32, (BLK, BLK), 0)
        col = lax.broadcasted_iota(jnp.int32, (BLK, BLK), 1)
        squares = jnp.where(row == col, gram_ref[0], 0.0)
        norm_ref[0] = jnp.sum(squares, axis=0, keepdims=True)


def gram(order, gradient, *after):
    rows, columns = gradient.shape
    width = tile_width(columns)
    return pl.pallas_call(
        gram_kernel,
        out_shape=[
            jax.ShapeDtypeStruct((QUAD, BLK, BLK), F32),
            jax.ShapeDtypeStruct((QUAD, 1, BLK), F32),
        ],
        grid_spec=pltpu.PrefetchScalarGridSpec(
            num_scalar_prefetch=1,
            grid=(QUAD, columns // width),
            in_specs=[
                pl.BlockSpec(memory_space=pl.ANY),
                pl.BlockSpec(memory_space=pl.ANY),
                pl.BlockSpec((BLK, width), lambda s, j, order: (order[s], j)),
            ],
            out_specs=[
                pl.BlockSpec((1, BLK, BLK), lambda s, j, order: (s, 0, 0)),
                pl.BlockSpec((1, 1, BLK), lambda s, j, order: (s, 0, 0)),
            ],
        ),
        compiler_params=params(20),
        cost_estimate=pl.CostEstimate(
            flops=2 * rows * columns * BLK,
            bytes_accessed=2 * rows * columns + 4 * QUAD * BLK * BLK,
            transcendentals=0,
        ),
        name="gram",
    )(order, *after, gradient)


def product(left, right):
    return dot(left.astype(BF16), right.astype(BF16))


def newton_kernel(tokens, after, mine0, mine1, other0, other1, root0, root1, held):
    cross = (mine0[...].astype(F32) + other0[...].astype(F32)) / tokens
    rest = (mine1[...].astype(F32) + other1[...].astype(F32)) / tokens
    first, last = unfold(rest[:HALF], rest[HALF : HALF + 1])
    held[:HALF, :HALF] = first
    held[:HALF, HALF:] = cross
    held[HALF:, :HALF] = cross.T
    held[HALF:, HALF:] = last
    row = lax.broadcasted_iota(jnp.int32, (BLK, BLK), 0)
    col = lax.broadcasted_iota(jnp.int32, (BLK, BLK), 1)
    identity = jnp.where(row == col, 1.0, 0.0).astype(F32)
    matrix = held[...] + damping * identity
    bound = jnp.max(jnp.sum(jnp.abs(matrix), axis=0, keepdims=True), axis=1, keepdims=True)
    scale = 2.0 / bound
    iterate = matrix * scale
    estimate = None
    for step in range(ITERS):
        error = (identity - iterate) * 0.25
        if estimate is None:
            estimate = error
        else:
            estimate = estimate + error + product(estimate, error)
        if step + 1 < ITERS:
            square = 2.0 * error + product(error, error)
            fourth = 2.0 * square + product(square, square)
            iterate = iterate + product(fourth, iterate)
    held[...] = (estimate + identity) * jnp.sqrt(jnp.sqrt(scale))
    root0[...] = held[:HALF, HALF:].astype(BF16)
    body, diagonal = fold(held[:HALF, :HALF], held[HALF:, HALF:])
    root1[:HALF] = body.astype(BF16)
    root1[HALF:] = diagonal.astype(BF16)


def newton(tokens, after, *halves):
    return pl.pallas_call(
        functools.partial(newton_kernel, tokens),
        out_shape=[jax.ShapeDtypeStruct((rows, HALF), BF16) for rows in (HALF, TAIL)],
        in_specs=[pl.BlockSpec(memory_space=pl.ANY)] + [VMEM] * 4,
        out_specs=[VMEM] * 2,
        scratch_shapes=[pltpu.VMEM((BLK, BLK), F32)],
        compiler_params=params(16),
        name="newton",
    )(after, *halves)


def norm_kernel(half0, half1, gram_ref, square_ref, sums_ref, root_ref, total_ref):
    cross = half0[...].astype(F32)
    rest = half1[...].astype(F32)
    first, last = unfold(rest[:HALF], rest[HALF : HALF + 1])
    root_ref[:HALF, :HALF] = first.astype(BF16)
    root_ref[:HALF, HALF:] = cross.astype(BF16)
    root_ref[HALF:, :HALF] = cross.T.astype(BF16)
    root_ref[HALF:, HALF:] = last.astype(BF16)
    root = root_ref[...]
    weighted = dot(root, root) * gram_ref[0]
    new = jnp.sum(weighted, axis=0, keepdims=True)
    old = square_ref[0]
    lanes = lambda value: sum(value[:, i : i + LANES] for i in range(0, BLK, LANES))
    row = lax.broadcasted_iota(jnp.int32, sums_ref.shape, 0)
    total_ref[...] = sums_ref[...] + jnp.where(row == 0, lanes(old), jnp.where(row == 1, lanes(new), 0.0))


def norm(place, half0, half1, grams, squares, sums):
    whole = lambda rows: pl.BlockSpec((rows, HALF), lambda i: (0, 0))
    return pl.pallas_call(
        norm_kernel,
        out_shape=[
            jax.ShapeDtypeStruct((BLK, BLK), BF16),
            jax.ShapeDtypeStruct((ROWS, LANES), F32),
        ],
        grid=(1,),
        in_specs=[
            whole(HALF),
            whole(TAIL),
            pl.BlockSpec((1, BLK, BLK), lambda i: (place, 0, 0)),
            pl.BlockSpec((1, 1, BLK), lambda i: (place, 0, 0)),
            pl.BlockSpec((ROWS, LANES), lambda i: (0, 0)),
        ],
        out_specs=[
            pl.BlockSpec((BLK, BLK), lambda i: (0, 0)),
            pl.BlockSpec((ROWS, LANES), lambda i: (0, 0)),
        ],
        compiler_params=params(16),
        cost_estimate=pl.CostEstimate(
            flops=2 * BLK**3, bytes_accessed=8 * BLK * BLK, transcendentals=0
        ),
        name="norm",
    )(half0, half1, grams, squares, sums)


def apply_kernel(order, here, owner_slot, sums, r0, r1, r2, r3, g_ref, update_ref, owned_ref, root, ratio):
    place, column = pl.program_id(0), pl.program_id(1)

    @pl.when((place == 0) & (column == 0))
    def _():
        owned_ref[...] = jnp.zeros_like(owned_ref)
        both = jnp.sum(sums[...], axis=1, keepdims=True)
        ratio[...] = jnp.broadcast_to(jnp.sqrt(both[:1] / (both[1:2] + 1e-06)), ratio.shape)

    for one, packed in enumerate((r0, r1, r2, r3)):

        @pl.when((place == one) & (column == 0))
        def _():
            root[...] = packed[...]

    for slot in range(SLOTS):

        @pl.when((column == 0) & (owner_slot[here[0], order[place]] == here[1] + slot))
        def _():
            owned_ref[slot] = root[...]

    for part in chunks(g_ref.shape[1]):
        update_ref[:, part] = (dot(root[...], g_ref[:, part]) * ratio[:1, :1]).astype(BF16)


def apply(order, here, owner_slot, sums, roots, gradient):
    rows, columns = gradient.shape
    width = tile_width(columns)
    square = pl.BlockSpec((BLK, BLK), lambda s, j, order, *_: (0, 0))
    tile = pl.BlockSpec((BLK, width), lambda s, j, order, *_: (order[s], j))
    return pl.pallas_call(
        apply_kernel,
        out_shape=[
            jax.ShapeDtypeStruct((rows, columns), BF16),
            jax.ShapeDtypeStruct((SLOTS, BLK, BLK), BF16),
        ],
        grid_spec=pltpu.PrefetchScalarGridSpec(
            num_scalar_prefetch=3,
            grid=(QUAD, columns // width),
            in_specs=[pl.BlockSpec((ROWS, LANES), lambda s, j, order, *_: (0, 0))]
            + [square] * QUAD
            + [tile],
            out_specs=[
                tile,
                pl.BlockSpec((SLOTS, BLK, BLK), lambda s, j, order, *_: (0, 0, 0)),
            ],
            scratch_shapes=[pltpu.VMEM((BLK, BLK), BF16), pltpu.VMEM((ROWS, LANES), F32)],
        ),
        compiler_params=params(24),
        name="apply",
    )(order, here, owner_slot, sums, *roots, gradient)


def swap(value, flip, axis="dp"):
    count = lax.axis_size(axis)
    return lax.ppermute(value, axis, [(i, i ^ flip) for i in range(count)])


def total(value, *axes):
    for axis in axes:
        flip = 1
        while flip < lax.axis_size(axis):
            value = value + swap(value, flip, axis)
            flip *= 2
    return value


def add(*values):
    return sum(value.astype(F32) for value in values).astype(BF16)


def per_device(activations, gradient, owner_slot):
    peer_count = lax.axis_size("dp")
    my_index = lax.axis_index("dp")
    group_index = lax.axis_index("pool")
    tokens_all = activations.shape[0] * peer_count
    order = (my_index % QUAD) ^ jnp.arange(QUAD, dtype=jnp.int32)
    here = jnp.stack([group_index, my_index * SLOTS])

    a0, a1, b0, b1, c0, c1, d0, d1 = statistics(order, activations)
    from_y = swap(d0, 1)
    from_z = swap(d1, 2)
    y0 = swap(b0, 1)
    z1 = swap(c1, 2)
    y1 = swap(add(b1, from_z), 1)
    z0 = swap(add(c0, from_y), 2)
    mine0 = add(a0, y0, z0)
    mine1 = add(a1, y1, z1)
    flip = QUAD
    other0, other1 = swap(mine0, flip), swap(mine1, flip)
    while 2 * flip < peer_count:
        mine0, mine1 = add(mine0, other0), add(mine1, other1)
        flip *= 2
        other0, other1 = swap(mine0, flip), swap(mine1, flip)

    grams, squares = gram(order, gradient, mine0, mine1)
    a0, a1 = newton(tokens_all, squares, mine0, mine1, other0, other1)
    c0 = swap(a0, 2)
    b1 = swap(a1, 1)
    c1 = swap(a1, 2)
    b0 = swap(a0, 1)
    d0 = swap(c0, 1)
    d1 = swap(b1, 2)
    sums = jnp.zeros((ROWS, LANES), F32)
    roots = []
    for place, pair in enumerate(((a0, a1), (b0, b1), (c0, c1), (d0, d1))):
        root, sums = norm(place, *pair, grams, squares, sums)
        roots.append(root)
    sums = total(sums, "pool", "dp")
    update, owned = apply(order, here, owner_slot, sums, roots, gradient)
    return (update, owned[None])


def solution(mesh):
    in_specs = (P("dp", "pool"), P("pool", "dp"), P())
    out_specs = (P("pool", "dp"), P("pool", "dp", None, None))
    return jax.shard_map(
        per_device, mesh=mesh, in_specs=in_specs, out_specs=out_specs, check_vma=False
    )
```

```python
import functools

import jax
import jax.numpy as jnp
from jax import lax
from jax.experimental import pallas as pl
from jax.experimental.pallas import tpu as pltpu
from jax.sharding import PartitionSpec as P

BLK = 512
HALF = BLK // 2
FOLD = BLK + 16
ITERS = 3
SLOTS = 2
QUAD = 4
ROWS = 8
LANES = 128

damping = 0.01
F32 = jnp.float32
BF16 = jnp.bfloat16
SMEM = pl.BlockSpec(memory_space=pltpu.SMEM)
VMEM = pl.BlockSpec(memory_space=pltpu.VMEM)
ANY = pl.BlockSpec(memory_space=pl.ANY)


def params(mib):
    return pltpu.CompilerParams(vmem_limit_bytes=mib * 2**20)


def dot(left, right, dims=((1,), (0,))):
    return lax.dot_general(left, right, (dims, ((), ())), preferred_element_type=F32)


def places():
    row = lax.broadcasted_iota(jnp.int32, (HALF, HALF), 0)
    col = lax.broadcasted_iota(jnp.int32, (HALF, HALF), 1)
    return row, col


def fold(first, last):
    row, col = places()
    body = jnp.where(row <= col, first, last)
    diagonal = jnp.sum(jnp.where(row == col, last, 0.0), axis=0, keepdims=True)
    return body, jnp.broadcast_to(diagonal, (FOLD - BLK, HALF))


def unfold(body, diagonal):
    row, col = places()
    turned = body.T
    first = jnp.where(row <= col, body, turned)
    last = jnp.where(row > col, body, jnp.where(row < col, turned, diagonal))
    return first, last


def stat_kernel(order, x_ref, *out):
    for place in (1, 2, 3, 0):
        start = pl.multiple_of(order[place] * BLK, BLK)
        left = x_ref[:, pl.ds(start, HALF)]
        right = x_ref[:, pl.ds(pl.multiple_of(start + HALF, HALF), HALF)]
        along = ((0,), (0,))
        out[place][:HALF] = dot(left, right, along).astype(BF16)
        body, diagonal = fold(dot(left, left, along), dot(right, right, along))
        out[place][HALF:BLK] = body.astype(BF16)
        out[place][BLK:] = diagonal.astype(BF16)


def statistics(order, activations):
    return pl.pallas_call(
        stat_kernel,
        out_shape=[jax.ShapeDtypeStruct((FOLD, HALF), BF16)] * QUAD,
        in_specs=[SMEM, VMEM],
        out_specs=[VMEM] * QUAD,
        compiler_params=params(16),
        name="statistics",
    )(order, activations)


def chunks(width, size):
    start = 0
    while width - start >= 2 * size:
        yield pl.ds(start, size)
        start += size
    yield pl.ds(start, width - start)


def gram_kernel(order, after, g_ref, held_ref, top_ref, last_ref, norm_ref, arrived):
    parts = list(chunks(g_ref.shape[1], 1792))

    def copy(place, index):
        rows = pl.ds(pl.multiple_of(order[place] * BLK, BLK), BLK)
        return pltpu.make_async_copy(
            g_ref.at[rows, parts[index]],
            held_ref.at[place, :, parts[index]],
            arrived.at[place, index],
        )

    for place in range(QUAD):
        for index in range(len(parts)):
            copy(place, index).start()

    def block(place, _):
        for index, part in enumerate(parts):
            copy(place, index).wait()
            upper = held_ref[place, :HALF, part]
            lower = held_ref[place, HALF:, part]
            across = ((1,), (1,))
            terms = dot(upper, upper, across), dot(upper, lower, across), dot(lower, lower, across)
            if index == 0:
                top_ref[place, :, :HALF] = terms[0]
                top_ref[place, :, HALF:] = terms[1]
                last_ref[place] = terms[2]
            else:
                top_ref[place, :, :HALF] += terms[0]
                top_ref[place, :, HALF:] += terms[1]
                last_ref[place] += terms[2]
        row, col = places()
        squares = jnp.where(row == col, top_ref[place, :, :HALF] + last_ref[place], 0.0)
        norm_ref[place] = jnp.sum(squares, axis=0, keepdims=True)
        return _

    lax.fori_loop(0, QUAD, block, 0)


def gram(order, gradient, after):
    rows, columns = gradient.shape
    parts = len(list(chunks(columns, 1792)))
    return pl.pallas_call(
        gram_kernel,
        out_shape=[
            pltpu.VMEM((QUAD, BLK, columns), BF16),
            pltpu.VMEM((QUAD, HALF, BLK), F32),
            pltpu.VMEM((QUAD, HALF, HALF), F32),
            pltpu.VMEM((QUAD, 1, HALF), F32),
        ],
        in_specs=[SMEM, ANY, ANY],
        out_specs=[VMEM] * 4,
        scratch_shapes=[pltpu.SemaphoreType.DMA((QUAD, parts))],
        compiler_params=params(16),
        cost_estimate=pl.CostEstimate(
            flops=2 * rows * columns * BLK, bytes_accessed=4 * rows * columns, transcendentals=0
        ),
        name="gram",
    )(order, after, pltpu.with_memory_space_constraint(gradient, pltpu.HBM))


def product(left, right):
    return dot(left.astype(BF16), right.astype(BF16))


def newton_kernel(tokens, after, mine, other, root, held):
    total = (mine[...].astype(F32) + other[...].astype(F32)) / tokens
    cross = total[:HALF]
    first, last = unfold(total[HALF:BLK], total[BLK : BLK + 1])
    held[:HALF, :HALF] = first
    held[:HALF, HALF:] = cross
    held[HALF:, :HALF] = cross.T
    held[HALF:, HALF:] = last
    row = lax.broadcasted_iota(jnp.int32, (BLK, BLK), 0)
    col = lax.broadcasted_iota(jnp.int32, (BLK, BLK), 1)
    identity = jnp.where(row == col, 1.0, 0.0).astype(F32)
    matrix = held[...] + damping * identity
    bound = jnp.max(jnp.sum(jnp.abs(matrix), axis=0, keepdims=True), axis=1, keepdims=True)
    scale = 2.0 / bound
    iterate = matrix * scale
    estimate = None
    for step in range(ITERS):
        error = (identity - iterate) * 0.25
        if estimate is None:
            estimate = error
        else:
            estimate = estimate + error + product(estimate, error)
        if step + 1 < ITERS:
            square = 2.0 * error + product(error, error)
            fourth = 2.0 * square + product(square, square)
            iterate = iterate + product(fourth, iterate)
    held[...] = (estimate + identity) * jnp.sqrt(jnp.sqrt(scale))
    root[:HALF] = held[:HALF, HALF:].astype(BF16)
    body, diagonal = fold(held[:HALF, :HALF], held[HALF:, HALF:])
    root[HALF:BLK] = body.astype(BF16)
    root[BLK:] = diagonal.astype(BF16)


def newton(tokens, after, mine, other):
    return pl.pallas_call(
        functools.partial(newton_kernel, tokens),
        out_shape=jax.ShapeDtypeStruct((FOLD, HALF), BF16),
        in_specs=[ANY, VMEM, VMEM],
        out_specs=VMEM,
        scratch_shapes=[pltpu.VMEM((BLK, BLK), F32)],
        compiler_params=params(16),
        cost_estimate=pl.CostEstimate(
            flops=16 * BLK**3, bytes_accessed=8 * BLK * BLK, transcendentals=0
        ),
        name="newton",
    )(after, mine, other)


def norm_kernel(place, folded, top_ref, last_ref, square_ref, sums_ref, root_ref, total_ref):
    cross = folded[:HALF]
    rest = folded[HALF:].astype(F32)
    first, last = unfold(rest[:HALF], rest[HALF : HALF + 1])
    root_ref[:HALF, :HALF] = first.astype(BF16)
    root_ref[:HALF, HALF:] = cross
    root_ref[HALF:, :HALF] = cross.astype(F32).T.astype(BF16)
    root_ref[HALF:, HALF:] = last.astype(BF16)
    upper = dot(root_ref[:HALF], root_ref[...]) * top_ref[place]
    lower = dot(root_ref[HALF:], root_ref[:, HALF:]) * last_ref[place]
    new = jnp.sum(upper[:, :HALF] + 2.0 * upper[:, HALF:] + lower, axis=0, keepdims=True)
    old = square_ref[place]
    lanes = lambda value: sum(value[:, i : i + LANES] for i in range(0, HALF, LANES))
    row = lax.broadcasted_iota(jnp.int32, sums_ref.shape, 0)
    total_ref[...] = sums_ref[...] + jnp.where(row == 0, lanes(old), jnp.where(row == 1, lanes(new), 0.0))


def norm(place, folded, grams, sums):
    return pl.pallas_call(
        functools.partial(norm_kernel, place),
        out_shape=[
            jax.ShapeDtypeStruct((BLK, BLK), BF16),
            jax.ShapeDtypeStruct((ROWS, LANES), F32),
        ],
        in_specs=[VMEM] * 5,
        out_specs=[VMEM] * 2,
        compiler_params=params(16),
        cost_estimate=pl.CostEstimate(
            flops=2 * BLK**3, bytes_accessed=8 * BLK * BLK, transcendentals=0
        ),
        name="norm",
    )(folded, *grams, sums)


def multiply_kernel(place, after, root_ref, g_ref, u_ref):
    for part in chunks(g_ref.shape[2], BLK):
        u_ref[place, :, part] = dot(root_ref[...], g_ref[place, :, part]).astype(BF16)


def multiply(place, root, held, after):
    return pl.pallas_call(
        functools.partial(multiply_kernel, place),
        out_shape=pltpu.VMEM(held.shape, BF16),
        in_specs=[ANY, VMEM, VMEM],
        out_specs=VMEM,
        input_output_aliases={2: 0},
        compiler_params=params(16),
        cost_estimate=pl.CostEstimate(
            flops=2 * BLK * BLK * held.shape[2],
            bytes_accessed=4 * BLK * held.shape[2],
            transcendentals=0,
        ),
        name="multiply",
    )(after, root, held)


def owned_kernel(order, here, owner_slot, r0, r1, r2, r3, owned_ref):
    owned_ref[...] = jnp.zeros_like(owned_ref)
    for place, root in enumerate((r0, r1, r2, r3)):
        for slot in range(SLOTS):

            @pl.when(owner_slot[here[0], order[place]] == here[1] + slot)
            def _():
                owned_ref[slot] = root[...]


def owned_roots(order, here, owner_slot, roots):
    return pl.pallas_call(
        owned_kernel,
        out_shape=jax.ShapeDtypeStruct((SLOTS, BLK, BLK), BF16),
        grid_spec=pltpu.PrefetchScalarGridSpec(
            num_scalar_prefetch=3,
            grid=(1,),
            in_specs=[pl.BlockSpec((BLK, BLK), lambda i, *_: (0, 0))] * QUAD,
            out_specs=pl.BlockSpec((SLOTS, BLK, BLK), lambda i, *_: (0, 0, 0)),
        ),
        compiler_params=params(16),
        cost_estimate=pl.CostEstimate(
            flops=0, bytes_accessed=4 * SLOTS * BLK * BLK, transcendentals=0
        ),
        name="owned",
    )(order, here, owner_slot, *roots)


def scale_kernel(order, sums, u_ref, update_ref, scaled, sent):
    both = jnp.sum(sums[...], axis=1, keepdims=True)
    ratio = jnp.sqrt(both[:1] / (both[1:2] + 1e-06))
    parts = list(chunks(u_ref.shape[2], 1792))

    def copy(place, index):
        rows = pl.ds(pl.multiple_of(order[place] * BLK, BLK), BLK)
        return pltpu.make_async_copy(
            scaled.at[place, :, parts[index]],
            update_ref.at[rows, parts[index]],
            sent.at[place, index],
        )

    def block(place, _):
        for index, part in enumerate(parts):
            scaled[place, :, part] = (u_ref[place, :, part].astype(F32) * ratio).astype(BF16)
            copy(place, index).start()
        return _

    lax.fori_loop(0, QUAD, block, 0)
    for place in range(QUAD):
        for index in range(len(parts)):
            copy(place, index).wait()


def scale(order, sums, unscaled):
    columns = unscaled.shape[2]
    parts = len(list(chunks(columns, 1792)))
    update, _ = pl.pallas_call(
        scale_kernel,
        out_shape=[
            jax.ShapeDtypeStruct((QUAD * BLK, columns), BF16),
            pltpu.VMEM(unscaled.shape, BF16),
        ],
        in_specs=[SMEM, VMEM, VMEM],
        out_specs=[ANY, VMEM],
        input_output_aliases={2: 1},
        scratch_shapes=[pltpu.SemaphoreType.DMA((QUAD, parts))],
        compiler_params=params(16),
        name="scale",
    )(order, sums, unscaled)
    return update


def swap(value, flip, axis="dp"):
    count = lax.axis_size(axis)
    return lax.ppermute(value, axis, [(i, i ^ flip) for i in range(count)])


def total(value, *axes):
    for axis in axes:
        flip = 1
        while flip < lax.axis_size(axis):
            value = value + swap(value, flip, axis)
            flip *= 2
    return value


def add(*values):
    return sum(value.astype(F32) for value in values).astype(BF16)


def per_device(activations, gradient, owner_slot):
    peer_count = lax.axis_size("dp")
    my_index = lax.axis_index("dp")
    group_index = lax.axis_index("pool")
    tokens_all = activations.shape[0] * peer_count
    order = (my_index % QUAD) ^ jnp.arange(QUAD, dtype=jnp.int32)
    here = jnp.stack([group_index, my_index * SLOTS])

    a, b, c, d = statistics(order, activations)
    mine = add(a, swap(b, 1), swap(c, 2), swap(d, 3))
    flip = QUAD
    other = swap(mine, flip)
    while 2 * flip < peer_count:
        mine = add(mine, other)
        flip *= 2
        other = swap(mine, flip)

    held, *grams = gram(order, gradient, mine)
    a = newton(tokens_all, grams[-1], mine, other)
    sums = jnp.zeros((ROWS, LANES), F32)
    roots = []
    for place, folded in enumerate((a, swap(a, 1), swap(a, 2), swap(a, 3))):
        root, sums = norm(place, folded, grams, sums)
        roots.append(root)
    for place, root in enumerate(roots):
        held = multiply(place, root, held, sums)
    owned = owned_roots(order, here, owner_slot, roots)
    update = scale(order, total(sums, "pool", "dp"), held)
    return (update, owned[None])


def solution(mesh):
    in_specs = (P("dp", "pool"), P("pool", "dp"), P())
    out_specs = (P("pool", "dp"), P("pool", "dp", None, None))
    return jax.shard_map(
        per_device, mesh=mesh, in_specs=in_specs, out_specs=out_specs, check_vma=False
    )
```

```python
import functools

import jax
import jax.numpy as jnp
from jax import lax
from jax.experimental import pallas as pl
from jax.experimental.pallas import tpu as pltpu
from jax.sharding import PartitionSpec as P

BLK = 512
HALF = BLK // 2
FOLD = BLK + 16
ITERS = 3
SLOTS = 2
QUAD = 4
ROWS = 8
LANES = 128

damping = 0.01
F32 = jnp.float32
BF16 = jnp.bfloat16
SMEM = pl.BlockSpec(memory_space=pltpu.SMEM)
VMEM = pl.BlockSpec(memory_space=pltpu.VMEM)
ANY = pl.BlockSpec(memory_space=pl.ANY)


def params(mib):
    return pltpu.CompilerParams(vmem_limit_bytes=mib * 2**20)


def dot(left, right, dims=((1,), (0,))):
    return lax.dot_general(left, right, (dims, ((), ())), preferred_element_type=F32)


def places():
    row = lax.broadcasted_iota(jnp.int32, (HALF, HALF), 0)
    col = lax.broadcasted_iota(jnp.int32, (HALF, HALF), 1)
    return row, col


def fold(first, last):
    row, col = places()
    body = jnp.where(row <= col, first, last)
    diagonal = jnp.sum(jnp.where(row == col, last, 0.0), axis=0, keepdims=True)
    return body, jnp.broadcast_to(diagonal, (FOLD - BLK, HALF))


def unfold(body, diagonal):
    row, col = places()
    turned = body.T
    first = jnp.where(row <= col, body, turned)
    last = jnp.where(row > col, body, jnp.where(row < col, turned, diagonal))
    return first, last


def stat_kernel(order, x_ref, *out):
    for place in (1, 2, 3, 0):
        start = pl.multiple_of(order[place] * BLK, BLK)
        left = x_ref[:, pl.ds(start, HALF)]
        right = x_ref[:, pl.ds(pl.multiple_of(start + HALF, HALF), HALF)]
        along = ((0,), (0,))
        out[place][:HALF] = dot(left, right, along).astype(BF16)
        body, diagonal = fold(dot(left, left, along), dot(right, right, along))
        out[place][HALF:BLK] = body.astype(BF16)
        out[place][BLK:] = diagonal.astype(BF16)


def statistics(order, activations):
    return pl.pallas_call(
        stat_kernel,
        out_shape=[jax.ShapeDtypeStruct((FOLD, HALF), BF16)] * QUAD,
        in_specs=[SMEM, VMEM],
        out_specs=[VMEM] * QUAD,
        compiler_params=params(16),
        name="statistics",
    )(order, activations)


def chunks(width, size):
    start = 0
    while width - start >= 2 * size:
        yield pl.ds(start, size)
        start += size
    yield pl.ds(start, width - start)


def gram_kernel(order, after, g_ref, top_ref, last_ref, norm_ref, held, arrived):
    parts = list(chunks(g_ref.shape[1], 1792))

    slots = held.shape[0]

    def copy(place, index):
        rows = pl.ds(pl.multiple_of(order[place] * BLK, BLK), BLK)
        return pltpu.make_async_copy(
            g_ref.at[rows, parts[index]],
            held.at[place % slots, :, parts[index]],
            arrived.at[place, index],
        )

    for place in range(slots):
        for index in range(len(parts)):
            copy(place, index).start()

    for place in range(QUAD):
        for index, part in enumerate(parts):
            copy(place, index).wait()
            upper = held[place % slots, :HALF, part]
            lower = held[place % slots, HALF:, part]
            across = ((1,), (1,))
            terms = dot(upper, upper, across), dot(upper, lower, across), dot(lower, lower, across)
            if index == 0:
                top_ref[place, :, :HALF] = terms[0]
                top_ref[place, :, HALF:] = terms[1]
                last_ref[place] = terms[2]
            else:
                top_ref[place, :, :HALF] += terms[0]
                top_ref[place, :, HALF:] += terms[1]
                last_ref[place] += terms[2]
            if place + slots < QUAD:
                copy(place + slots, index).start()
        row, col = places()
        squares = jnp.where(row == col, top_ref[place, :, :HALF] + last_ref[place], 0.0)
        norm_ref[place] = jnp.sum(squares, axis=0, keepdims=True)


def gram(order, gradient, after):
    rows, columns = gradient.shape
    parts = len(list(chunks(columns, 1792)))
    return pl.pallas_call(
        gram_kernel,
        out_shape=[
            jax.ShapeDtypeStruct((QUAD, HALF, BLK), F32),
            jax.ShapeDtypeStruct((QUAD, HALF, HALF), F32),
            jax.ShapeDtypeStruct((QUAD, 1, HALF), F32),
        ],
        in_specs=[SMEM, ANY, ANY],
        out_specs=[VMEM] * 3,
        scratch_shapes=[
            pltpu.VMEM((2, BLK, columns), BF16),
            pltpu.SemaphoreType.DMA((QUAD, parts)),
        ],
        compiler_params=params(16),
        cost_estimate=pl.CostEstimate(
            flops=2 * rows * columns * BLK, bytes_accessed=4 * rows * columns, transcendentals=0
        ),
        name="gram",
    )(order, after, gradient)


def product(left, right):
    return dot(left.astype(BF16), right.astype(BF16))


def newton_kernel(tokens, after, mine, other, root, held):
    total = (mine[...].astype(F32) + other[...].astype(F32)) / tokens
    cross = total[:HALF]
    first, last = unfold(total[HALF:BLK], total[BLK : BLK + 1])
    held[:HALF, :HALF] = first
    held[:HALF, HALF:] = cross
    held[HALF:, :HALF] = cross.T
    held[HALF:, HALF:] = last
    row = lax.broadcasted_iota(jnp.int32, (BLK, BLK), 0)
    col = lax.broadcasted_iota(jnp.int32, (BLK, BLK), 1)
    identity = jnp.where(row == col, 1.0, 0.0).astype(F32)
    matrix = held[...] + damping * identity
    bound = jnp.max(jnp.sum(jnp.abs(matrix), axis=0, keepdims=True), axis=1, keepdims=True)
    scale = 2.0 / bound
    iterate = matrix * scale
    estimate = None
    for step in range(ITERS):
        error = (identity - iterate) * 0.25
        if estimate is None:
            estimate = error
        else:
            estimate = estimate + error + product(estimate, error)
        if step + 1 < ITERS:
            square = 2.0 * error + product(error, error)
            fourth = 2.0 * square + product(square, square)
            iterate = iterate + product(fourth, iterate)
    held[...] = (estimate + identity) * jnp.sqrt(jnp.sqrt(scale))
    root[:HALF] = held[:HALF, HALF:].astype(BF16)
    body, diagonal = fold(held[:HALF, :HALF], held[HALF:, HALF:])
    root[HALF:BLK] = body.astype(BF16)
    root[BLK:] = diagonal.astype(BF16)


def newton(tokens, after, mine, other):
    return pl.pallas_call(
        functools.partial(newton_kernel, tokens),
        out_shape=jax.ShapeDtypeStruct((FOLD, HALF), BF16),
        in_specs=[ANY, VMEM, VMEM],
        out_specs=VMEM,
        scratch_shapes=[pltpu.VMEM((BLK, BLK), F32)],
        compiler_params=params(16),
        cost_estimate=pl.CostEstimate(
            flops=16 * BLK**3, bytes_accessed=8 * BLK * BLK, transcendentals=0
        ),
        name="newton",
    )(after, mine, other)


def norm_kernel(place, folded, top_ref, last_ref, square_ref, sums_ref, root_ref, total_ref):
    cross = folded[:HALF]
    rest = folded[HALF:].astype(F32)
    first, last = unfold(rest[:HALF], rest[HALF : HALF + 1])
    root_ref[:HALF, :HALF] = first.astype(BF16)
    root_ref[:HALF, HALF:] = cross
    root_ref[HALF:, :HALF] = cross.astype(F32).T.astype(BF16)
    root_ref[HALF:, HALF:] = last.astype(BF16)
    upper = dot(root_ref[:HALF], root_ref[...]) * top_ref[place]
    lower = dot(root_ref[HALF:], root_ref[:, HALF:]) * last_ref[place]
    new = jnp.sum(upper[:, :HALF] + 2.0 * upper[:, HALF:] + lower, axis=0, keepdims=True)
    old = square_ref[place]
    lanes = lambda value: sum(value[:, i : i + LANES] for i in range(0, HALF, LANES))
    row = lax.broadcasted_iota(jnp.int32, sums_ref.shape, 0)
    total_ref[...] = sums_ref[...] + jnp.where(row == 0, lanes(old), jnp.where(row == 1, lanes(new), 0.0))


def norm(place, folded, grams, sums):
    return pl.pallas_call(
        functools.partial(norm_kernel, place),
        out_shape=[
            jax.ShapeDtypeStruct((BLK, BLK), BF16),
            jax.ShapeDtypeStruct((ROWS, LANES), F32),
        ],
        in_specs=[VMEM] * 5,
        out_specs=[VMEM] * 2,
        compiler_params=params(16),
        name="norm",
    )(folded, *grams, sums)


def multiply_kernel(place, order, after, root_ref, g_ref, u_ref, arrived):
    parts = list(chunks(g_ref.shape[1], BLK))
    rows = pl.ds(pl.multiple_of(order[place] * BLK, BLK), BLK)
    copies = [
        pltpu.make_async_copy(g_ref.at[rows, part], u_ref.at[:, part], arrived.at[index])
        for index, part in enumerate(parts)
    ]
    for copy in copies:
        copy.start()
    for copy, part in zip(copies, parts):
        copy.wait()
        u_ref[:, part] = dot(root_ref[...], u_ref[:, part]).astype(BF16)


def multiply(place, order, root, gradient, after):
    columns = gradient.shape[1]
    return pl.pallas_call(
        functools.partial(multiply_kernel, place),
        out_shape=pltpu.VMEM((BLK, columns), BF16),
        in_specs=[SMEM, ANY, VMEM, ANY],
        out_specs=VMEM,
        scratch_shapes=[pltpu.SemaphoreType.DMA((len(list(chunks(columns, BLK))),))],
        compiler_params=params(16),
        name="multiply",
    )(order, after, root, gradient)


def owned_kernel(order, here, owner_slot, r0, r1, r2, r3, owned_ref):
    owned_ref[...] = jnp.zeros_like(owned_ref)
    for place, root in enumerate((r0, r1, r2, r3)):
        for slot in range(SLOTS):

            @pl.when(owner_slot[here[0], order[place]] == here[1] + slot)
            def _():
                owned_ref[slot] = root[...]


def owned_roots(order, here, owner_slot, roots):
    return pl.pallas_call(
        owned_kernel,
        out_shape=jax.ShapeDtypeStruct((SLOTS, BLK, BLK), BF16),
        grid_spec=pltpu.PrefetchScalarGridSpec(
            num_scalar_prefetch=3,
            grid=(1,),
            in_specs=[pl.BlockSpec((BLK, BLK), lambda i, *_: (0, 0))] * QUAD,
            out_specs=pl.BlockSpec((SLOTS, BLK, BLK), lambda i, *_: (0, 0, 0)),
        ),
        compiler_params=params(16),
        name="owned",
    )(order, here, owner_slot, *roots)


def scale_kernel(order, sums, u0, u1, u2, u3, update_ref, s0, s1, s2, s3, sent):
    both = jnp.sum(sums[...], axis=1, keepdims=True)
    ratio = jnp.sqrt(both[:1] / (both[1:2] + 1e-06))
    parts = list(chunks(u0.shape[1], 1792))
    scaled = (s0, s1, s2, s3)

    def copy(place, index):
        rows = pl.ds(pl.multiple_of(order[place] * BLK, BLK), BLK)
        return pltpu.make_async_copy(
            scaled[place].at[:, parts[index]],
            update_ref.at[rows, parts[index]],
            sent.at[place, index],
        )

    for place, unscaled in enumerate((u0, u1, u2, u3)):
        for index, part in enumerate(parts):
            scaled[place][:, part] = (unscaled[:, part].astype(F32) * ratio).astype(BF16)
            copy(place, index).start()
    for place in range(QUAD):
        for index in range(len(parts)):
            copy(place, index).wait()


def scale(order, sums, unscaled):
    columns = unscaled[0].shape[1]
    parts = len(list(chunks(columns, 1792)))
    return pl.pallas_call(
        scale_kernel,
        out_shape=[jax.ShapeDtypeStruct((QUAD * BLK, columns), BF16)]
        + [pltpu.VMEM((BLK, columns), BF16)] * QUAD,
        in_specs=[SMEM] + [VMEM] * (1 + QUAD),
        out_specs=[ANY] + [VMEM] * QUAD,
        input_output_aliases={2 + place: 1 + place for place in range(QUAD)},
        scratch_shapes=[pltpu.SemaphoreType.DMA((QUAD, parts))],
        compiler_params=params(16),
        name="scale",
    )(order, sums, *unscaled)[0]


def swap(value, flip, axis="dp"):
    count = lax.axis_size(axis)
    return lax.ppermute(value, axis, [(i, i ^ flip) for i in range(count)])


def total(value, *axes):
    for axis in axes:
        flip = 1
        while flip < lax.axis_size(axis):
            value = value + swap(value, flip, axis)
            flip *= 2
    return value


def add(*values):
    return sum(value.astype(F32) for value in values).astype(BF16)


def per_device(activations, gradient, owner_slot):
    peer_count = lax.axis_size("dp")
    my_index = lax.axis_index("dp")
    group_index = lax.axis_index("pool")
    tokens_all = activations.shape[0] * peer_count
    order = (my_index % QUAD) ^ jnp.arange(QUAD, dtype=jnp.int32)
    here = jnp.stack([group_index, my_index * SLOTS])

    a, b, c, d = statistics(order, activations)
    mine = add(a, swap(b, 1), swap(c, 2), swap(d, 3))
    flip = QUAD
    other = swap(mine, flip)
    while 2 * flip < peer_count:
        mine = add(mine, other)
        flip *= 2
        other = swap(mine, flip)

    gradient = pltpu.with_memory_space_constraint(gradient, pltpu.HBM)
    grams = gram(order, gradient, mine)
    a = newton(tokens_all, grams[-1], mine, other)
    sums = jnp.zeros((ROWS, LANES), F32)
    roots = []
    for place, folded in enumerate((a, swap(a, 1), swap(a, 2), swap(a, 3))):
        root, sums = norm(place, folded, grams, sums)
        roots.append(root)
    held = [multiply(place, order, root, gradient, sums) for place, root in enumerate(roots)]
    owned = owned_roots(order, here, owner_slot, roots)
    update = scale(order, total(sums, "pool", "dp"), held)
    return (update, owned[None])


def solution(mesh):
    in_specs = (P("dp", "pool"), P("pool", "dp"), P())
    out_specs = (P("pool", "dp"), P("pool", "dp", None, None))
    return jax.shard_map(
        per_device, mesh=mesh, in_specs=in_specs, out_specs=out_specs, check_vma=False
    )
```

```python
import functools
import math

import jax
import jax.numpy as jnp
from jax import lax
from jax.experimental import pallas as pl
from jax.experimental.pallas import tpu as pltpu
from jax.sharding import PartitionSpec as P

BLK = 512
HALF = BLK // 2
FOLD = BLK + 16
ITERS = 3
SLOTS = 2
QUAD = 4
ROWS = 8
LANES = 128

damping = 0.01
F32 = jnp.float32
BF16 = jnp.bfloat16
SMEM = pl.BlockSpec(memory_space=pltpu.SMEM)
VMEM = pl.BlockSpec(memory_space=pltpu.VMEM)
ANY = pl.BlockSpec(memory_space=pl.ANY)


def params(mib):
    return pltpu.CompilerParams(vmem_limit_bytes=mib * 2**20)


def dot(left, right, dims=((1,), (0,))):
    return lax.dot_general(left, right, (dims, ((), ())), preferred_element_type=F32)


def places():
    row = lax.broadcasted_iota(jnp.int32, (HALF, HALF), 0)
    col = lax.broadcasted_iota(jnp.int32, (HALF, HALF), 1)
    return row, col


def fold(first, last):
    row, col = places()
    body = jnp.where(row <= col, first, last)
    diagonal = jnp.sum(jnp.where(row == col, last, 0.0), axis=0, keepdims=True)
    return body, jnp.broadcast_to(diagonal, (FOLD - BLK, HALF))


def unfold(body, diagonal):
    row, col = places()
    turned = body.T
    first = jnp.where(row <= col, body, turned)
    last = jnp.where(row > col, body, jnp.where(row < col, turned, diagonal))
    return first, last


def stat_kernel(x_ref, out):
    for block in range(QUAD):
        left = x_ref[:, block * BLK : block * BLK + HALF]
        right = x_ref[:, block * BLK + HALF : (block + 1) * BLK]
        along = ((0,), (0,))
        out[block, :HALF] = dot(left, right, along).astype(BF16)
        body, diagonal = fold(dot(left, left, along), dot(right, right, along))
        out[block, HALF:BLK] = body.astype(BF16)
        out[block, BLK:] = diagonal.astype(BF16)


def statistics(activations):
    return pl.pallas_call(
        stat_kernel,
        out_shape=jax.ShapeDtypeStruct((QUAD, FOLD, HALF), BF16),
        in_specs=[VMEM],
        out_specs=VMEM,
        compiler_params=params(16),
        name="statistics",
    )(activations)


def chunks(width, size):
    start = 0
    while width - start >= 2 * size:
        yield pl.ds(start, size)
        start += size
    yield pl.ds(start, width - start)


def gram_kernel(order, after, g_ref, top_ref, last_ref, norm_ref, held, arrived):
    parts = list(chunks(g_ref.shape[1], 1792))

    slots = held.shape[0]

    def copy(place, index):
        rows = pl.ds(pl.multiple_of(order[place] * BLK, BLK), BLK)
        return pltpu.make_async_copy(
            g_ref.at[rows, parts[index]],
            held.at[place % slots, :, parts[index]],
            arrived.at[place, index],
        )

    for place in range(slots):
        for index in range(len(parts)):
            copy(place, index).start()

    for place in range(QUAD):
        for index, part in enumerate(parts):
            copy(place, index).wait()
            upper = held[place % slots, :HALF, part]
            lower = held[place % slots, HALF:, part]
            across = ((1,), (1,))
            terms = dot(upper, upper, across), dot(upper, lower, across), dot(lower, lower, across)
            if index == 0:
                top_ref[place, :, :HALF] = terms[0]
                top_ref[place, :, HALF:] = terms[1]
                last_ref[place] = terms[2]
            else:
                top_ref[place, :, :HALF] += terms[0]
                top_ref[place, :, HALF:] += terms[1]
                last_ref[place] += terms[2]
            if place + slots < QUAD:
                copy(place + slots, index).start()
        row, col = places()
        squares = jnp.where(row == col, top_ref[place, :, :HALF] + last_ref[place], 0.0)
        norm_ref[place] = jnp.sum(squares, axis=0, keepdims=True)


def gram(order, gradient, after):
    rows, columns = gradient.shape
    parts = len(list(chunks(columns, 1792)))
    return pl.pallas_call(
        gram_kernel,
        out_shape=[
            jax.ShapeDtypeStruct((QUAD, HALF, BLK), F32),
            jax.ShapeDtypeStruct((QUAD, HALF, HALF), F32),
            jax.ShapeDtypeStruct((QUAD, 1, HALF), F32),
        ],
        in_specs=[SMEM, ANY, ANY],
        out_specs=[VMEM] * 3,
        scratch_shapes=[
            pltpu.VMEM((2, BLK, columns), BF16),
            pltpu.SemaphoreType.DMA((QUAD, parts)),
        ],
        compiler_params=params(16),
        cost_estimate=pl.CostEstimate(
            flops=2 * rows * columns * BLK, bytes_accessed=4 * rows * columns, transcendentals=0
        ),
        name="gram",
    )(order, after, gradient)


def product(left, right):
    return dot(left.astype(BF16), right.astype(BF16))


def newton_kernel(tokens, after, mine, other, root, held):
    total = (mine[...].astype(F32) + other[...].astype(F32)) / tokens
    cross = total[:HALF]
    first, last = unfold(total[HALF:BLK], total[BLK : BLK + 1])
    held[:HALF, :HALF] = first
    held[:HALF, HALF:] = cross
    held[HALF:, :HALF] = cross.T
    held[HALF:, HALF:] = last
    row = lax.broadcasted_iota(jnp.int32, (BLK, BLK), 0)
    col = lax.broadcasted_iota(jnp.int32, (BLK, BLK), 1)
    identity = jnp.where(row == col, 1.0, 0.0).astype(F32)
    matrix = held[...] + damping * identity
    bound = jnp.max(jnp.sum(jnp.abs(matrix), axis=0, keepdims=True), axis=1, keepdims=True)
    scale = 2.0 / bound
    iterate = matrix * scale
    estimate = None
    for step in range(ITERS):
        error = (identity - iterate) * 0.25
        if estimate is None:
            estimate = error
        else:
            estimate = estimate + error + product(estimate, error)
        if step + 1 < ITERS:
            square = 2.0 * error + product(error, error)
            fourth = 2.0 * square + product(square, square)
            iterate = iterate + product(fourth, iterate)
    held[...] = (estimate + identity) * jnp.sqrt(jnp.sqrt(scale))
    root[:HALF] = held[:HALF, HALF:].astype(BF16)
    body, diagonal = fold(held[:HALF, :HALF], held[HALF:, HALF:])
    root[HALF:BLK] = body.astype(BF16)
    root[BLK:] = diagonal.astype(BF16)


def newton(tokens, after, mine, other):
    return pl.pallas_call(
        functools.partial(newton_kernel, tokens),
        out_shape=jax.ShapeDtypeStruct((FOLD, HALF), BF16),
        in_specs=[ANY, VMEM, VMEM],
        out_specs=VMEM,
        scratch_shapes=[pltpu.VMEM((BLK, BLK), F32)],
        compiler_params=params(16),
        cost_estimate=pl.CostEstimate(
            flops=16 * BLK**3, bytes_accessed=8 * BLK * BLK, transcendentals=0
        ),
        name="newton",
    )(after, mine, other)


def norm_kernel(place, folded, top_ref, last_ref, square_ref, sums_ref, root_ref, total_ref):
    cross = folded[:HALF]
    rest = folded[HALF:].astype(F32)
    first, last = unfold(rest[:HALF], rest[HALF : HALF + 1])
    root_ref[:HALF, :HALF] = first.astype(BF16)
    root_ref[:HALF, HALF:] = cross
    root_ref[HALF:, :HALF] = cross.astype(F32).T.astype(BF16)
    root_ref[HALF:, HALF:] = last.astype(BF16)
    upper = dot(root_ref[:HALF], root_ref[...]) * top_ref[place]
    lower = dot(root_ref[HALF:], root_ref[:, HALF:]) * last_ref[place]
    new = jnp.sum(upper[:, :HALF] + 2.0 * upper[:, HALF:] + lower, axis=0, keepdims=True)
    old = square_ref[place]
    lanes = lambda value: sum(value[:, i : i + LANES] for i in range(0, HALF, LANES))
    row = lax.broadcasted_iota(jnp.int32, sums_ref.shape, 0)
    total_ref[...] = sums_ref[...] + jnp.where(row == 0, lanes(old), jnp.where(row == 1, lanes(new), 0.0))


def norm(place, folded, grams, sums):
    return pl.pallas_call(
        functools.partial(norm_kernel, place),
        out_shape=[
            jax.ShapeDtypeStruct((BLK, BLK), BF16),
            jax.ShapeDtypeStruct((ROWS, LANES), F32),
        ],
        in_specs=[VMEM] * 5,
        out_specs=[VMEM] * 2,
        compiler_params=params(16),
        name="norm",
    )(folded, *grams, sums)


def finish_kernel(order, here, owner_slot, sums, *refs):
    roots, g_ref = refs[:QUAD], refs[QUAD]
    update_ref, owned_ref, held, owned, arrived, sent, stored = refs[QUAD + 1 :]
    pieces = list(chunks(held.shape[2], 1792))

    def copy(place, index, fetch):
        rows = pl.ds(pl.multiple_of(order[place] * BLK, BLK), BLK)
        here = held.at[place, :, pieces[index]]
        if fetch:
            return pltpu.make_async_copy(g_ref.at[rows, pieces[index]], here, arrived.at[place, index])
        return pltpu.make_async_copy(here, update_ref.at[rows, pieces[index]], sent.at[place, index])

    every = [(place, index) for place in range(QUAD) for index in range(len(pieces))]
    for place, index in every:
        copy(place, index, True).start()
    whole = jnp.sum(sums[...], axis=0)
    both = jnp.sum(whole, axis=1, keepdims=True)
    ratio = jnp.sqrt(both[:1] / (both[1:2] + 1e-06))
    owned[...] = jnp.zeros_like(owned)
    for place, root in enumerate(roots):
        for slot in range(SLOTS):

            @pl.when(owner_slot[here[0], order[place]] == here[1] + slot)
            def _():
                owned[slot] = root[...]

    store = pltpu.make_async_copy(owned, owned_ref, stored)
    store.start()
    for place, index in every:
        copy(place, index, True).wait()
        for part in chunks(pieces[index].size, BLK):
            part = pl.ds(pieces[index].start + part.start, part.size)
            product = dot(roots[place][...], held[place, :, part])
            held[place, :, part] = (product * ratio).astype(BF16)
        copy(place, index, False).start()
    for place, index in every:
        copy(place, index, False).wait()
    store.wait()


def finish(order, here, owner_slot, sums, roots, gradient):
    rows, columns = gradient.shape
    pieces = len(list(chunks(columns, 1792)))
    return pl.pallas_call(
        finish_kernel,
        out_shape=[
            jax.ShapeDtypeStruct((rows, columns), BF16),
            jax.ShapeDtypeStruct((SLOTS, BLK, BLK), BF16),
        ],
        in_specs=[SMEM] * 3 + [VMEM] * (1 + QUAD) + [ANY],
        out_specs=[ANY] * 2,
        scratch_shapes=[
            pltpu.VMEM((QUAD, BLK, columns), BF16),
            pltpu.VMEM((SLOTS, BLK, BLK), BF16),
            pltpu.SemaphoreType.DMA((QUAD, pieces)),
            pltpu.SemaphoreType.DMA((QUAD, pieces)),
            pltpu.SemaphoreType.DMA,
        ],
        compiler_params=params(32),
        name="finish",
    )(order, here, owner_slot, sums, *roots, gradient)


def swap(value, flip, axis="dp"):
    count = lax.axis_size(axis)
    return lax.ppermute(value, axis, [(i, i ^ flip) for i in range(count)])


def everywhere(value, axes):
    count = math.prod(lax.axis_size(axis) for axis in axes)
    copies = jnp.broadcast_to(value[None], (count, *value.shape))
    return lax.all_to_all(copies, axes, 0, 0, tiled=True)


def add(*values):
    return sum(value.astype(F32) for value in values).astype(BF16)


def per_device(activations, gradient, owner_slot):
    peer_count = lax.axis_size("dp")
    my_index = lax.axis_index("dp")
    group_index = lax.axis_index("pool")
    tokens_all = activations.shape[0] * peer_count
    order = (my_index % QUAD) ^ jnp.arange(QUAD, dtype=jnp.int32)
    here = jnp.stack([group_index, my_index * SLOTS])

    groups = [list(range(i, i + QUAD)) for i in range(0, peer_count, QUAD)]
    parts = lax.all_to_all(statistics(activations), "dp", 0, 0, axis_index_groups=groups, tiled=True)
    mine = add(*parts)
    flip = QUAD
    other = swap(mine, flip)
    while 2 * flip < peer_count:
        mine = add(mine, other)
        flip *= 2
        other = swap(mine, flip)

    gradient = pltpu.with_memory_space_constraint(gradient, pltpu.HBM)
    grams = gram(order, gradient, mine)
    root = newton(tokens_all, grams[-1], mine, other)
    folded = (root, swap(root, 1), swap(root, 2), swap(root, 3))
    sums = jnp.zeros((ROWS, LANES), F32)
    roots = []
    for place in range(QUAD):
        root, sums = norm(place, folded[place], grams, sums)
        roots.append(root)
    sums = everywhere(sums, ("pool", "dp"))
    update, owned = finish(order, here, owner_slot, sums, roots, gradient)
    return (update, owned[None])


def solution(mesh):
    in_specs = (P("dp", "pool"), P("pool", "dp"), P())
    out_specs = (P("pool", "dp"), P("pool", "dp", None, None))
    return jax.shard_map(
        per_device, mesh=mesh, in_specs=in_specs, out_specs=out_specs, check_vma=False
    )
```

```python
import functools
import math

import jax
import jax.numpy as jnp
from jax import lax
from jax.experimental import pallas as pl
from jax.experimental.pallas import tpu as pltpu
from jax.sharding import PartitionSpec as P

BLK = 512
HALF = BLK // 2
FOLD = BLK + 16
ITERS = 3
SLOTS = 2
QUAD = 4
ROWS = 8
LANES = 128

damping = 0.01
F32 = jnp.float32
BF16 = jnp.bfloat16
SMEM = pl.BlockSpec(memory_space=pltpu.SMEM)
VMEM = pl.BlockSpec(memory_space=pltpu.VMEM)
ANY = pl.BlockSpec(memory_space=pl.ANY)


def params(mib):
    return pltpu.CompilerParams(vmem_limit_bytes=mib * 2**20)


def dot(left, right, dims=((1,), (0,))):
    return lax.dot_general(left, right, (dims, ((), ())), preferred_element_type=F32)


def places():
    row = lax.broadcasted_iota(jnp.int32, (HALF, HALF), 0)
    col = lax.broadcasted_iota(jnp.int32, (HALF, HALF), 1)
    return row, col


def fold(first, last):
    row, col = places()
    body = jnp.where(row <= col, first, last)
    diagonal = jnp.sum(jnp.where(row == col, last, 0.0), axis=0, keepdims=True)
    return body, jnp.broadcast_to(diagonal, (FOLD - BLK, HALF))


def unfold(body, diagonal):
    row, col = places()
    turned = body.T
    first = jnp.where(row <= col, body, turned)
    last = jnp.where(row > col, body, jnp.where(row < col, turned, diagonal))
    return first, last


def stat_kernel(order, x_ref, *out):
    for place in (1, 2, 3, 0):
        start = pl.multiple_of(order[place] * BLK, BLK)
        left = x_ref[:, pl.ds(start, HALF)]
        right = x_ref[:, pl.ds(pl.multiple_of(start + HALF, HALF), HALF)]
        along = ((0,), (0,))
        out[place][:HALF] = dot(left, right, along).astype(BF16)
        body, diagonal = fold(dot(left, left, along), dot(right, right, along))
        out[place][HALF:BLK] = body.astype(BF16)
        out[place][BLK:] = diagonal.astype(BF16)


def statistics(order, activations):
    return pl.pallas_call(
        stat_kernel,
        out_shape=[jax.ShapeDtypeStruct((FOLD, HALF), BF16)] * QUAD,
        in_specs=[SMEM, VMEM],
        out_specs=[VMEM] * QUAD,
        compiler_params=params(12),
        name="statistics",
    )(order, activations)


def chunks(width, size):
    start = 0
    while width - start >= 2 * size:
        yield pl.ds(start, size)
        start += size
    yield pl.ds(start, width - start)


def gram_kernel(order, after, g_ref, *refs):
    held, folded = refs[:QUAD], refs[QUAD : 2 * QUAD]
    norm_ref, top, last, arrived = refs[2 * QUAD :]
    parts = list(chunks(g_ref.shape[1], 1792))

    def copy(place, index):
        rows = pl.ds(pl.multiple_of(order[place] * BLK, BLK), BLK)
        return pltpu.make_async_copy(
            g_ref.at[rows, parts[index]], held[place].at[:, parts[index]], arrived.at[place, index]
        )

    for place in range(QUAD):
        for index in range(len(parts)):
            copy(place, index).start()
    norm_ref[...] = jnp.zeros_like(norm_ref)
    row, col = places()
    for place in range(QUAD):
        for index, part in enumerate(parts):
            copy(place, index).wait()
            upper = held[place][:HALF, part]
            lower = held[place][HALF:, part]
            across = ((1,), (1,))
            terms = dot(upper, upper, across), dot(upper, lower, across), dot(lower, lower, across)
            if index == 0:
                top[:, :HALF] = terms[0]
                top[:, HALF:] = terms[1]
                last[...] = terms[2]
            else:
                top[:, :HALF] += terms[0]
                top[:, HALF:] += terms[1]
                last[...] += terms[2]
        squares = jnp.where(row == col, top[:, :HALF] + last[...], 0.0)
        norm_ref[...] += jnp.sum(squares, axis=0, keepdims=True)
        body, diagonal = fold(top[:, :HALF], last[...])
        folded[place][:HALF] = top[:, HALF:].astype(BF16)
        folded[place][HALF:BLK] = body.astype(BF16)
        folded[place][BLK:] = diagonal.astype(BF16)


def gram(order, gradient, after):
    rows, columns = gradient.shape
    parts = len(list(chunks(columns, 1792)))
    results = pl.pallas_call(
        gram_kernel,
        out_shape=[pltpu.VMEM((BLK, columns), BF16)] * QUAD
        + [jax.ShapeDtypeStruct((FOLD, HALF), BF16)] * QUAD
        + [jax.ShapeDtypeStruct((1, HALF), F32)],
        in_specs=[SMEM, ANY, ANY],
        out_specs=[VMEM] * (2 * QUAD + 1),
        scratch_shapes=[
            pltpu.VMEM((HALF, BLK), F32),
            pltpu.VMEM((HALF, HALF), F32),
            pltpu.SemaphoreType.DMA((QUAD, parts)),
        ],
        compiler_params=params(12),
        cost_estimate=pl.CostEstimate(
            flops=2 * rows * columns * BLK, bytes_accessed=2 * rows * columns, transcendentals=0
        ),
        name="gram",
    )(order, after, pltpu.with_memory_space_constraint(gradient, pltpu.HBM))
    return results[:QUAD], results[QUAD : 2 * QUAD], results[-1]


def product(left, right):
    return dot(left.astype(BF16), right.astype(BF16))


def newton_kernel(tokens, after, mine, other, root, held):
    total = (mine[...].astype(F32) + other[...].astype(F32)) / tokens
    cross = total[:HALF]
    first, last = unfold(total[HALF:BLK], total[BLK : BLK + 1])
    held[:HALF, :HALF] = first
    held[:HALF, HALF:] = cross
    held[HALF:, :HALF] = cross.T
    held[HALF:, HALF:] = last
    row = lax.broadcasted_iota(jnp.int32, (BLK, BLK), 0)
    col = lax.broadcasted_iota(jnp.int32, (BLK, BLK), 1)
    identity = jnp.where(row == col, 1.0, 0.0).astype(F32)
    matrix = held[...] + damping * identity
    bound = jnp.max(jnp.sum(jnp.abs(matrix), axis=0, keepdims=True), axis=1, keepdims=True)
    scale = 2.0 / bound
    iterate = matrix * scale
    estimate = None
    for step in range(ITERS):
        error = (identity - iterate) * 0.25
        if estimate is None:
            estimate = error
        else:
            estimate = estimate + error + product(estimate, error)
        if step + 1 < ITERS:
            square = 2.0 * error + product(error, error)
            fourth = 2.0 * square + product(square, square)
            iterate = iterate + product(fourth, iterate)
    held[...] = (estimate + identity) * jnp.sqrt(jnp.sqrt(scale))
    root[:HALF] = held[:HALF, HALF:].astype(BF16)
    body, diagonal = fold(held[:HALF, :HALF], held[HALF:, HALF:])
    root[HALF:BLK] = body.astype(BF16)
    root[BLK:] = diagonal.astype(BF16)


def newton(tokens, after, mine, other):
    return pl.pallas_call(
        functools.partial(newton_kernel, tokens),
        out_shape=jax.ShapeDtypeStruct((FOLD, HALF), BF16),
        in_specs=[ANY, VMEM, VMEM],
        out_specs=VMEM,
        scratch_shapes=[pltpu.VMEM((BLK, BLK), F32)],
        compiler_params=params(12),
        cost_estimate=pl.CostEstimate(
            flops=16 * BLK**3, bytes_accessed=8 * BLK * BLK, transcendentals=0
        ),
        name="newton",
    )(after, mine, other)


def unfold_root(folded, root_ref):
    cross = folded[:HALF]
    rest = folded[HALF:].astype(F32)
    first, last = unfold(rest[:HALF], rest[HALF : HALF + 1])
    root_ref[:HALF, :HALF] = first.astype(BF16)
    root_ref[:HALF, HALF:] = cross
    root_ref[HALF:, :HALF] = cross.astype(F32).T.astype(BF16)
    root_ref[HALF:, HALF:] = last.astype(BF16)


def norm_kernel(folded, mine, from_y, from_z, squares, total_ref, root):
    unfold_root(folded, root)
    grams = mine[...].astype(F32) + from_y[...].astype(F32) + from_z[...].astype(F32)
    upper = dot(root[:HALF], root[...])
    last = dot(root[HALF:], root[:, HALF:])
    first, cross = upper[:, :HALF], upper[:, HALF:]
    row, col = places()
    weights = jnp.where(row < col, 2.0 * first, jnp.where(row > col, 2.0 * last, first))
    terms = weights * grams[HALF:BLK] + 2.0 * cross * grams[:HALF]
    terms += jnp.where(row == col, last, 0.0) * grams[BLK : BLK + 1]
    lanes = lambda value: sum(value[:, i : i + LANES] for i in range(0, HALF, LANES))
    new = lanes(jnp.sum(terms, axis=0, keepdims=True))
    row = lax.broadcasted_iota(jnp.int32, total_ref.shape, 0)
    total_ref[...] = jnp.where(row == 0, lanes(squares[...]), jnp.where(row == 1, new, 0.0))


def norm(*operands):
    return pl.pallas_call(
        norm_kernel,
        out_shape=jax.ShapeDtypeStruct((ROWS, LANES), F32),
        in_specs=[VMEM] * 5,
        out_specs=VMEM,
        scratch_shapes=[pltpu.VMEM((BLK, BLK), BF16)],
        compiler_params=params(12),
        name="norm",
    )(*operands)


def multiply_kernel(after, folded, held_ref, u_ref, root_ref):
    unfold_root(folded, root_ref)
    for part in chunks(u_ref.shape[1], BLK):
        u_ref[:, part] = dot(root_ref[...], held_ref[:, part]).astype(BF16)


def multiply(folded, held, after):
    return pl.pallas_call(
        multiply_kernel,
        out_shape=[pltpu.VMEM(held.shape, BF16), jax.ShapeDtypeStruct((BLK, BLK), BF16)],
        in_specs=[ANY, VMEM, VMEM],
        out_specs=[VMEM] * 2,
        input_output_aliases={2: 0},
        compiler_params=params(12),
        cost_estimate=pl.CostEstimate(
            flops=2 * BLK * BLK * held.shape[1], bytes_accessed=1, transcendentals=0
        ),
        name="multiply",
    )(after, folded, held)


def finish_kernel(order, owner_slot, sums, folded, *refs):
    roots, blocks = refs[: QUAD - 1], refs[QUAD - 1 : 2 * QUAD - 1]
    update_ref, owned_ref = refs[2 * QUAD - 1 : 2 * QUAD + 1]
    scaled = refs[2 * QUAD + 1 : 3 * QUAD + 1]
    final, owned, sent, stored = refs[3 * QUAD + 1 :]
    both = jnp.sum(sums[...], axis=1, keepdims=True)
    ratio = jnp.sqrt(both[:1] / (both[1:2] + 1e-06))
    parts = list(chunks(blocks[0].shape[1], BLK))

    def copy(place, index):
        rows = pl.ds(pl.multiple_of(order[place] * BLK, BLK), BLK)
        return pltpu.make_async_copy(
            scaled[place].at[:, parts[index]],
            update_ref.at[rows, parts[index]],
            sent.at[place, index],
        )

    def rescale(place):
        for index, part in enumerate(parts):
            scaled[place][:, part] = (blocks[place][:, part].astype(F32) * ratio).astype(BF16)
            copy(place, index).start()

    rescale(0)
    unfold_root(folded, final)
    for index, part in enumerate(parts):
        product = dot(final[...], blocks[-1][:, part])
        scaled[-1][:, part] = (product * ratio).astype(BF16)
        copy(QUAD - 1, index).start()
    rescale(1)
    owned[...] = jnp.zeros_like(owned)
    for place, root in enumerate((*roots, final)):
        for slot in range(SLOTS):

            @pl.when(owner_slot[order[QUAD], order[place]] == order[QUAD + 1] + slot)
            def _():
                owned[slot] = root[...]

    store = pltpu.make_async_copy(owned, owned_ref, stored)
    store.start()
    rescale(2)
    for place in range(QUAD):
        for index in range(len(parts)):
            copy(place, index).wait()
    store.wait()


def finish(order, owner_slot, sums, folded, roots, blocks):
    columns = blocks[0].shape[1]
    parts = len(list(chunks(columns, BLK)))
    return pl.pallas_call(
        finish_kernel,
        out_shape=[
            jax.ShapeDtypeStruct((QUAD * BLK, columns), BF16),
            jax.ShapeDtypeStruct((SLOTS, BLK, BLK), BF16),
        ]
        + [pltpu.VMEM((BLK, columns), BF16)] * QUAD,
        in_specs=[SMEM] * 2 + [VMEM] * (1 + 2 * QUAD),
        out_specs=[ANY] * 2 + [VMEM] * QUAD,
        input_output_aliases={3 + QUAD + place: 2 + place for place in range(QUAD)},
        scratch_shapes=[
            pltpu.VMEM((BLK, BLK), BF16),
            pltpu.VMEM((SLOTS, BLK, BLK), BF16),
            pltpu.SemaphoreType.DMA((QUAD, parts)),
            pltpu.SemaphoreType.DMA,
        ],
        compiler_params=params(12),
        name="finish",
    )(order, owner_slot, sums, folded, *roots, *blocks)[:2]


def swap(value, flip):
    axes = ("pool", "dp")
    count = math.prod(lax.axis_size(axis) for axis in axes)
    return lax.ppermute(value, axes, [(i, i ^ flip) for i in range(count)])


def rounds():
    peer_bits = lax.axis_size("dp").bit_length() - 1
    bits = [1 << i for i in range(peer_bits + lax.axis_size("pool").bit_length() - 1)]
    bits = bits[:peer_bits] + bits[peer_bits:][::-1]
    pairs = [bits[i : i + 2] for i in range(0, len(bits), 2)]
    return [pair if len(pair) == 1 else [*pair, sum(pair)] for pair in pairs]


def add(*values):
    return sum(value.astype(F32) for value in values).astype(BF16)


def per_device(activations, gradient, owner_slot):
    peer_count = lax.axis_size("dp")
    my_index = lax.axis_index("dp")
    group_index = lax.axis_index("pool")
    tokens_all = activations.shape[0] * peer_count
    order = (my_index % QUAD) ^ jnp.arange(QUAD, dtype=jnp.int32)
    order = jnp.concatenate([order, jnp.stack([group_index, my_index * SLOTS])])

    a, b, c, d = statistics(order, activations)
    b, c, d = swap(b, 1), swap(c, 2), swap(d, 3)
    blocks, grams, squares = gram(order, gradient, a)
    mine = add(a, b, c, d)
    flip = QUAD
    other = swap(mine, flip)
    while 2 * flip < peer_count:
        mine = add(mine, other)
        flip *= 2
        other = swap(mine, flip)

    across = swap(grams[3], 1)
    from_y = swap(grams[1], 1)
    from_z = swap(add(grams[2], across), 2)
    root = newton(tokens_all, squares, mine, other)
    folded = (root, swap(root, 1), swap(root, 2), swap(root, 3))
    blocks, folded, roots = list(blocks), list(folded), []

    def precondition(place):
        blocks[place], root = multiply(folded[place], blocks[place], folded[place])
        roots.append(root)

    precondition(0)
    blocks[0], from_y = lax.optimization_barrier((blocks[0], from_y))
    sums = norm(root, grams[0], from_y, from_z, squares)
    for step, flips in enumerate(rounds()):
        if step == 1:
            sums, folded[2] = lax.optimization_barrier((sums, folded[2]))
        if step == 2:
            sums, folded[3] = lax.optimization_barrier((sums, folded[3]))
        received = [swap(sums, flip) for flip in flips]
        if step < QUAD - 2:
            precondition(step + 1)
            blocks[step + 1], *received = lax.optimization_barrier((blocks[step + 1], *received))
        sums = sums + sum(received)
    update, owned = finish(order, owner_slot, sums, folded[-1], roots, blocks)
    return (update, owned[None])


def solution(mesh):
    in_specs = (P("dp", "pool"), P("pool", "dp"), P())
    out_specs = (P("pool", "dp"), P("pool", "dp", None, None))
    return jax.shard_map(
        per_device, mesh=mesh, in_specs=in_specs, out_specs=out_specs, check_vma=False
    )
```

```python
import functools
import math

import jax
import jax.numpy as jnp
from jax import lax
from jax.experimental import pallas as pl
from jax.experimental.pallas import tpu as pltpu
from jax.sharding import PartitionSpec as P

BLK = 512
HALF = BLK // 2
FOLD = BLK + 16
ITERS = 3
SLOTS = 2
QUAD = 4
EARLY = 2
BAND = 128
ROWS = 8
LANES = 128

damping = 0.01
F32 = jnp.float32
BF16 = jnp.bfloat16
SMEM = pl.BlockSpec(memory_space=pltpu.SMEM)
VMEM = pl.BlockSpec(memory_space=pltpu.VMEM)
ANY = pl.BlockSpec(memory_space=pl.ANY)


def params(mib):
    return pltpu.CompilerParams(vmem_limit_bytes=mib * 2**20)


def dot(left, right, dims=((1,), (0,))):
    return lax.dot_general(left, right, (dims, ((), ())), preferred_element_type=F32)


def places():
    row = lax.broadcasted_iota(jnp.int32, (HALF, HALF), 0)
    col = lax.broadcasted_iota(jnp.int32, (HALF, HALF), 1)
    return row, col


def fold(first, last):
    row, col = places()
    body = jnp.where(row <= col, first, last)
    diagonal = jnp.sum(jnp.where(row == col, last, 0.0), axis=0, keepdims=True)
    return body, jnp.broadcast_to(diagonal, (FOLD - BLK, HALF))


def unfold(body, diagonal):
    row, col = places()
    turned = body.T
    first = jnp.where(row <= col, body, turned)
    last = jnp.where(row > col, body, jnp.where(row < col, turned, diagonal))
    return first, last


def stat_kernel(order, x_ref, *out):
    for place in (1, 2, 3, 0):
        start = pl.multiple_of(order[place] * BLK, BLK)
        left = x_ref[:, pl.ds(start, HALF)]
        right = x_ref[:, pl.ds(pl.multiple_of(start + HALF, HALF), HALF)]
        along = ((0,), (0,))
        out[place][:HALF] = dot(left, right, along).astype(BF16)
        body, diagonal = fold(dot(left, left, along), dot(right, right, along))
        out[place][HALF:BLK] = body.astype(BF16)
        out[place][BLK:] = diagonal.astype(BF16)


def statistics(order, activations):
    return pl.pallas_call(
        stat_kernel,
        out_shape=[jax.ShapeDtypeStruct((FOLD, HALF), BF16)] * QUAD,
        in_specs=[SMEM, VMEM],
        out_specs=[VMEM] * QUAD,
        compiler_params=params(12),
        name="statistics",
    )(order, activations)


def chunks(width, size):
    start = 0
    while width - start >= 2 * size:
        yield pl.ds(start, size)
        start += size
    yield pl.ds(start, width - start)


def gram_kernel(order, after, g_ref, *refs):
    held, folded = refs[:QUAD], refs[QUAD : 2 * QUAD]
    norm_ref, top, last, arrived = refs[2 * QUAD :]
    parts = list(chunks(g_ref.shape[1], 1792))

    def copy(place, index):
        rows = pl.ds(pl.multiple_of(order[place] * BLK, BLK), BLK)
        return pltpu.make_async_copy(
            g_ref.at[rows, parts[index]], held[place].at[:, parts[index]], arrived.at[place, index]
        )

    for place in range(QUAD):
        for index in range(len(parts)):
            copy(place, index).start()
    norm_ref[...] = jnp.zeros_like(norm_ref)
    row, col = places()
    for place in range(QUAD):
        for index, part in enumerate(parts):
            copy(place, index).wait()
            upper = held[place][:HALF, part]
            lower = held[place][HALF:, part]
            across = ((1,), (1,))
            terms = dot(upper, upper, across), dot(upper, lower, across), dot(lower, lower, across)
            if index == 0:
                top[:, :HALF] = terms[0]
                top[:, HALF:] = terms[1]
                last[...] = terms[2]
            else:
                top[:, :HALF] += terms[0]
                top[:, HALF:] += terms[1]
                last[...] += terms[2]
        squares = jnp.where(row == col, top[:, :HALF] + last[...], 0.0)
        norm_ref[...] += jnp.sum(squares, axis=0, keepdims=True)
        body, diagonal = fold(top[:, :HALF], last[...])
        folded[place][:HALF] = top[:, HALF:].astype(BF16)
        folded[place][HALF:BLK] = body.astype(BF16)
        folded[place][BLK:] = diagonal.astype(BF16)


def gram(order, gradient, after):
    rows, columns = gradient.shape
    parts = len(list(chunks(columns, 1792)))
    results = pl.pallas_call(
        gram_kernel,
        out_shape=[pltpu.VMEM((BLK, columns), BF16)] * QUAD
        + [jax.ShapeDtypeStruct((FOLD, HALF), BF16)] * QUAD
        + [jax.ShapeDtypeStruct((1, HALF), F32)],
        in_specs=[SMEM, ANY, ANY],
        out_specs=[VMEM] * (2 * QUAD + 1),
        scratch_shapes=[
            pltpu.VMEM((HALF, BLK), F32),
            pltpu.VMEM((HALF, HALF), F32),
            pltpu.SemaphoreType.DMA((QUAD, parts)),
        ],
        compiler_params=params(12),
        cost_estimate=pl.CostEstimate(
            flops=2 * rows * columns * BLK, bytes_accessed=2 * rows * columns, transcendentals=0
        ),
        name="gram",
    )(order, after, pltpu.with_memory_space_constraint(gradient, pltpu.HBM))
    return results[:QUAD], results[QUAD : 2 * QUAD], results[-1]


def product(left, right):
    return dot(left.astype(BF16), right.astype(BF16))


def newton_kernel(tokens, after, mine, other, root, held):
    total = (mine[...].astype(F32) + other[...].astype(F32)) / tokens
    cross = total[:HALF]
    first, last = unfold(total[HALF:BLK], total[BLK : BLK + 1])
    held[:HALF, :HALF] = first
    held[:HALF, HALF:] = cross
    held[HALF:, :HALF] = cross.T
    held[HALF:, HALF:] = last
    row = lax.broadcasted_iota(jnp.int32, (BLK, BLK), 0)
    col = lax.broadcasted_iota(jnp.int32, (BLK, BLK), 1)
    identity = jnp.where(row == col, 1.0, 0.0).astype(F32)
    matrix = held[...] + damping * identity
    bound = jnp.max(jnp.sum(jnp.abs(matrix), axis=0, keepdims=True), axis=1, keepdims=True)
    scale = 2.0 / bound
    iterate = matrix * scale
    estimate = None
    for step in range(ITERS):
        error = (identity - iterate) * 0.25
        if estimate is None:
            estimate = error
        else:
            estimate = estimate + error + product(estimate, error)
        if step + 1 < ITERS:
            square = 2.0 * error + product(error, error)
            fourth = 2.0 * square + product(square, square)
            iterate = iterate + product(fourth, iterate)
    held[...] = (estimate + identity) * jnp.sqrt(jnp.sqrt(scale))
    root[:HALF] = held[:HALF, HALF:].astype(BF16)
    body, diagonal = fold(held[:HALF, :HALF], held[HALF:, HALF:])
    root[HALF:BLK] = body.astype(BF16)
    root[BLK:] = diagonal.astype(BF16)


def newton(tokens, after, mine, other):
    return pl.pallas_call(
        functools.partial(newton_kernel, tokens),
        out_shape=jax.ShapeDtypeStruct((FOLD, HALF), BF16),
        in_specs=[ANY, VMEM, VMEM],
        out_specs=VMEM,
        scratch_shapes=[pltpu.VMEM((BLK, BLK), F32)],
        compiler_params=params(12),
        cost_estimate=pl.CostEstimate(
            flops=16 * BLK**3, bytes_accessed=8 * BLK * BLK, transcendentals=0
        ),
        name="newton",
    )(after, mine, other)


def unfold_root(folded, root_ref):
    cross = folded[:HALF]
    rest = folded[HALF:].astype(F32)
    first, last = unfold(rest[:HALF], rest[HALF : HALF + 1])
    root_ref[:HALF, :HALF] = first.astype(BF16)
    root_ref[:HALF, HALF:] = cross
    root_ref[HALF:, :HALF] = cross.astype(F32).T.astype(BF16)
    root_ref[HALF:, HALF:] = last.astype(BF16)


def norm_kernel(folded, mine, from_y, from_z, squares, total_ref, root):
    unfold_root(folded, root)
    grams = mine[...].astype(F32) + from_y[...].astype(F32) + from_z[...].astype(F32)
    upper = dot(root[:HALF], root[...])
    last = dot(root[HALF:], root[:, HALF:])
    first, cross = upper[:, :HALF], upper[:, HALF:]
    row, col = places()
    weights = jnp.where(row < col, 2.0 * first, jnp.where(row > col, 2.0 * last, first))
    terms = weights * grams[HALF:BLK] + 2.0 * cross * grams[:HALF]
    terms += jnp.where(row == col, last, 0.0) * grams[BLK : BLK + 1]
    lanes = lambda value: sum(value[:, i : i + LANES] for i in range(0, HALF, LANES))
    new = lanes(jnp.sum(terms, axis=0, keepdims=True))
    row = lax.broadcasted_iota(jnp.int32, total_ref.shape, 0)
    total_ref[...] = jnp.where(row == 0, lanes(squares[...]), jnp.where(row == 1, new, 0.0))


def norm(*operands):
    return pl.pallas_call(
        norm_kernel,
        out_shape=jax.ShapeDtypeStruct((ROWS, LANES), F32),
        in_specs=[VMEM] * 5,
        out_specs=VMEM,
        scratch_shapes=[pltpu.VMEM((BLK, BLK), BF16)],
        compiler_params=params(12),
        name="norm",
    )(*operands)


def multiply_kernel(after, folded, held_ref, u_ref, root_ref):
    unfold_root(folded, root_ref)
    for part in chunks(u_ref.shape[1], BLK):
        u_ref[:, part] = dot(root_ref[...], held_ref[:, part]).astype(BF16)


def multiply(folded, held, after):
    return pl.pallas_call(
        multiply_kernel,
        out_shape=[pltpu.VMEM(held.shape, BF16), jax.ShapeDtypeStruct((BLK, BLK), BF16)],
        in_specs=[ANY, VMEM, VMEM],
        out_specs=[VMEM] * 2,
        input_output_aliases={2: 0},
        compiler_params=params(12),
        cost_estimate=pl.CostEstimate(flops=1880000000, bytes_accessed=1, transcendentals=0),
        name="multiply",
    )(after, folded, held)


def finish_kernel(order, owner_slot, sums, *refs):
    roots, folded, blocks = refs[:EARLY], refs[EARLY:QUAD], refs[QUAD : 2 * QUAD]
    update_ref, owned_ref = refs[2 * QUAD : 2 * QUAD + 2]
    scaled = refs[2 * QUAD + 2 : 3 * QUAD + 2]
    late, owned, sent, stored = refs[3 * QUAD + 2 :]
    both = jnp.sum(sums[...], axis=1, keepdims=True)
    ratio = jnp.sqrt(both[:1] / (both[1:2] + 1e-06))
    parts = list(chunks(blocks[0].shape[1], BLK))
    waits = []

    def send(place, rows, columns):
        at = pl.multiple_of(order[place] * BLK + rows.start, rows.size)
        copy = pltpu.make_async_copy(
            scaled[place].at[rows, columns],
            update_ref.at[pl.ds(at, rows.size), columns],
            sent.at[len(waits)],
        )
        copy.start()
        waits.append(copy)

    def rescale(place):
        for start in range(0, BLK, BAND):
            rows = pl.ds(start, BAND)
            scaled[place][rows] = (blocks[place][rows].astype(F32) * ratio).astype(BF16)
            send(place, rows, pl.ds(0, blocks[0].shape[1]))

    for place in range(EARLY):
        rescale(place)
    for place in range(EARLY, QUAD):
        final = late.at[place - EARLY]
        unfold_root(folded[place - EARLY], final)
        for part in parts:
            product = dot(final[...], blocks[place][:, part])
            scaled[place][:, part] = (product * ratio).astype(BF16)
            send(place, pl.ds(0, BLK), part)
    owned[...] = jnp.zeros_like(owned)
    for place in range(QUAD):
        for slot in range(SLOTS):

            @pl.when(owner_slot[order[QUAD], order[place]] == order[QUAD + 1] + slot)
            def _():
                owned[slot] = roots[place][...] if place < EARLY else late[place - EARLY]

    store = pltpu.make_async_copy(owned, owned_ref, stored)
    store.start()
    for copy in waits:
        copy.wait()
    store.wait()


def finish(order, owner_slot, sums, roots, folded, blocks):
    columns = blocks[0].shape[1]
    pieces = EARLY * (BLK // BAND) + (QUAD - EARLY) * len(list(chunks(columns, BLK)))
    return pl.pallas_call(
        finish_kernel,
        out_shape=[
            jax.ShapeDtypeStruct((QUAD * BLK, columns), BF16),
            jax.ShapeDtypeStruct((SLOTS, BLK, BLK), BF16),
        ]
        + [pltpu.VMEM((BLK, columns), BF16)] * QUAD,
        in_specs=[SMEM] * 2 + [VMEM] * (1 + 2 * QUAD),
        out_specs=[ANY] * 2 + [VMEM] * QUAD,
        input_output_aliases={3 + QUAD + place: 2 + place for place in range(QUAD)},
        scratch_shapes=[
            pltpu.VMEM((QUAD - EARLY, BLK, BLK), BF16),
            pltpu.VMEM((SLOTS, BLK, BLK), BF16),
            pltpu.SemaphoreType.DMA((pieces,)),
            pltpu.SemaphoreType.DMA,
        ],
        compiler_params=params(12),
        name="finish",
    )(order, owner_slot, sums, *roots, *folded, *blocks)[:2]


def swap(value, flip):
    axes = ("pool", "dp")
    count = math.prod(lax.axis_size(axis) for axis in axes)
    return lax.ppermute(value, axes, [(i, i ^ flip) for i in range(count)])


def rounds():
    peer_bits = lax.axis_size("dp").bit_length() - 1
    bits = [1 << i for i in range(peer_bits + lax.axis_size("pool").bit_length() - 1)]
    bits = bits[:peer_bits] + bits[peer_bits:][::-1]
    pairs = [bits[i : i + 2] for i in range(0, len(bits), 2)]
    return [pair if len(pair) == 1 else [*pair, sum(pair)] for pair in pairs]


def add(*values):
    return sum(value.astype(F32) for value in values).astype(BF16)


def per_device(activations, gradient, owner_slot):
    peer_count = lax.axis_size("dp")
    my_index = lax.axis_index("dp")
    group_index = lax.axis_index("pool")
    tokens_all = activations.shape[0] * peer_count
    order = (my_index % QUAD) ^ jnp.arange(QUAD, dtype=jnp.int32)
    order = jnp.concatenate([order, jnp.stack([group_index, my_index * SLOTS])])

    a, b, c, d = statistics(order, activations)
    b, c, d = swap(b, 1), swap(c, 2), swap(d, 3)
    blocks, grams, squares = gram(order, gradient, a)
    mine = add(a, b, c, d)
    flip = QUAD
    other = swap(mine, flip)
    grams = list(grams)
    while 2 * flip < peer_count:
        mine = add(mine, other)
        flip *= 2
        other = swap(mine, flip)

    mine, grams[1] = lax.optimization_barrier((mine, grams[1]))
    across = swap(grams[3], 1)
    from_y = swap(grams[1], 1)
    from_z = swap(add(grams[2], across), 2)
    root = newton(tokens_all, squares, mine, other)
    folded = (root, swap(root, 1), swap(root, 2), swap(root, 3))
    blocks, folded, roots = list(blocks), list(folded), []

    def precondition(place):
        blocks[place], root = multiply(folded[place], blocks[place], folded[place])
        roots.append(root)

    sums = norm(root, grams[0], from_y, from_z, squares)
    arrivals = {0: [1], 1: [2, 3]}
    for step, flips in enumerate(rounds()):
        received = [swap(sums, flip) for flip in flips]
        if step < EARLY:
            precondition(step)
            blocks[step], *received = lax.optimization_barrier((blocks[step], *received))
        for place in arrivals.get(step, ()):
            folded[place], *received = lax.optimization_barrier((folded[place], *received))
        sums = sums + sum(received)
    update, owned = finish(order, owner_slot, sums, roots, folded[EARLY:], blocks)
    return (update, owned[None])


def solution(mesh):
    in_specs = (P("dp", "pool"), P("pool", "dp"), P())
    out_specs = (P("pool", "dp"), P("pool", "dp", None, None))
    return jax.shard_map(
        per_device, mesh=mesh, in_specs=in_specs, out_specs=out_specs, check_vma=False
    )
```

```python
import functools
import math

import jax
import jax.numpy as jnp
from jax import lax
from jax.experimental import pallas as pl
from jax.experimental.pallas import tpu as pltpu
from jax.sharding import PartitionSpec as P

BLK = 512
HALF = BLK // 2
FOLD = BLK + 16
ITERS = 3
SLOTS = 2
QUAD = 4
EARLY = 2
BAND = 128
ROWS = 8
LANES = 128

damping = 0.01
F32 = jnp.float32
BF16 = jnp.bfloat16
SMEM = pl.BlockSpec(memory_space=pltpu.SMEM)
VMEM = pl.BlockSpec(memory_space=pltpu.VMEM)
ANY = pl.BlockSpec(memory_space=pl.ANY)


def params(mib):
    return pltpu.CompilerParams(vmem_limit_bytes=mib * 2**20)


def dot(left, right, dims=((1,), (0,))):
    return lax.dot_general(left, right, (dims, ((), ())), preferred_element_type=F32)


def places():
    row = lax.broadcasted_iota(jnp.int32, (HALF, HALF), 0)
    col = lax.broadcasted_iota(jnp.int32, (HALF, HALF), 1)
    return row, col


def fold(first, last):
    row, col = places()
    body = jnp.where(row <= col, first, last)
    diagonal = jnp.sum(jnp.where(row == col, last, 0.0), axis=0, keepdims=True)
    return body, jnp.broadcast_to(diagonal, (FOLD - BLK, HALF))


def unfold(body, diagonal):
    row, col = places()
    turned = body.T
    first = jnp.where(row <= col, body, turned)
    last = jnp.where(row > col, body, jnp.where(row < col, turned, diagonal))
    return first, last


def stat_kernel(order, x_ref, *refs):
    out, held, arrived = refs[:QUAD], refs[QUAD], refs[QUAD + 1]
    places = (1, 2, 3, 0)

    def copy(place):
        columns = pl.ds(pl.multiple_of(order[place] * BLK, BLK), BLK)
        return pltpu.make_async_copy(x_ref.at[:, columns], held.at[place], arrived.at[place])

    for place in places:
        copy(place).start()
    for place in places:
        copy(place).wait()
        left, right = held[place, :, :HALF], held[place, :, HALF:]
        along = ((0,), (0,))
        out[place][:HALF] = dot(left, right, along).astype(BF16)
        body, diagonal = fold(dot(left, left, along), dot(right, right, along))
        out[place][HALF:BLK] = body.astype(BF16)
        out[place][BLK:] = diagonal.astype(BF16)


def statistics(order, activations):
    return pl.pallas_call(
        stat_kernel,
        out_shape=[jax.ShapeDtypeStruct((FOLD, HALF), BF16)] * QUAD,
        in_specs=[SMEM, ANY],
        out_specs=[VMEM] * QUAD,
        scratch_shapes=[
            pltpu.VMEM((QUAD, activations.shape[0], BLK), BF16),
            pltpu.SemaphoreType.DMA((QUAD,)),
        ],
        compiler_params=params(12),
        name="statistics",
    )(order, pltpu.with_memory_space_constraint(activations, pltpu.HBM))


def chunks(width, size):
    start = 0
    while width - start >= 2 * size:
        yield pl.ds(start, size)
        start += size
    yield pl.ds(start, width - start)


def gram_kernel(order, after, g_ref, *refs):
    held, folded = refs[:QUAD], refs[QUAD : 2 * QUAD]
    norm_ref, top, last, arrived = refs[2 * QUAD :]
    parts = list(chunks(g_ref.shape[1], 1792))

    def copy(place, index):
        rows = pl.ds(pl.multiple_of(order[place] * BLK, BLK), BLK)
        return pltpu.make_async_copy(
            g_ref.at[rows, parts[index]], held[place].at[:, parts[index]], arrived.at[place, index]
        )

    for place in range(QUAD):
        for index in range(len(parts)):
            copy(place, index).start()
    norm_ref[...] = jnp.zeros_like(norm_ref)
    row, col = places()
    for place in range(QUAD):
        for index, part in enumerate(parts):
            copy(place, index).wait()
            upper = held[place][:HALF, part]
            lower = held[place][HALF:, part]
            across = ((1,), (1,))
            terms = dot(upper, upper, across), dot(upper, lower, across), dot(lower, lower, across)
            if index == 0:
                top[:, :HALF] = terms[0]
                top[:, HALF:] = terms[1]
                last[...] = terms[2]
            else:
                top[:, :HALF] += terms[0]
                top[:, HALF:] += terms[1]
                last[...] += terms[2]
        squares = jnp.where(row == col, top[:, :HALF] + last[...], 0.0)
        norm_ref[...] += jnp.sum(squares, axis=0, keepdims=True)
        body, diagonal = fold(top[:, :HALF], last[...])
        folded[place][:HALF] = top[:, HALF:].astype(BF16)
        folded[place][HALF:BLK] = body.astype(BF16)
        folded[place][BLK:] = diagonal.astype(BF16)


def gram(order, gradient, after):
    rows, columns = gradient.shape
    parts = len(list(chunks(columns, 1792)))
    results = pl.pallas_call(
        gram_kernel,
        out_shape=[pltpu.VMEM((BLK, columns), BF16)] * QUAD
        + [jax.ShapeDtypeStruct((FOLD, HALF), BF16)] * QUAD
        + [jax.ShapeDtypeStruct((1, HALF), F32)],
        in_specs=[SMEM, ANY, ANY],
        out_specs=[VMEM] * (2 * QUAD + 1),
        scratch_shapes=[
            pltpu.VMEM((HALF, BLK), F32),
            pltpu.VMEM((HALF, HALF), F32),
            pltpu.SemaphoreType.DMA((QUAD, parts)),
        ],
        compiler_params=params(12),
        cost_estimate=pl.CostEstimate(
            flops=2 * rows * columns * BLK, bytes_accessed=2 * rows * columns, transcendentals=0
        ),
        name="gram",
    )(order, after, pltpu.with_memory_space_constraint(gradient, pltpu.HBM))
    return results[:QUAD], results[QUAD : 2 * QUAD], results[-1]


def product(left, right):
    return dot(left.astype(BF16), right.astype(BF16))


def newton_kernel(tokens, after, mine, other, root, held):
    total = (mine[...].astype(F32) + other[...].astype(F32)) / tokens
    cross = total[:HALF]
    first, last = unfold(total[HALF:BLK], total[BLK : BLK + 1])
    held[:HALF, :HALF] = first
    held[:HALF, HALF:] = cross
    held[HALF:, :HALF] = cross.T
    held[HALF:, HALF:] = last
    row = lax.broadcasted_iota(jnp.int32, (BLK, BLK), 0)
    col = lax.broadcasted_iota(jnp.int32, (BLK, BLK), 1)
    identity = jnp.where(row == col, 1.0, 0.0).astype(F32)
    matrix = held[...] + damping * identity
    bound = jnp.max(jnp.sum(jnp.abs(matrix), axis=0, keepdims=True), axis=1, keepdims=True)
    scale = 2.0 / bound
    iterate = matrix * scale
    estimate = None
    for step in range(ITERS):
        error = (identity - iterate) * 0.25
        if estimate is None:
            estimate = error
        else:
            estimate = estimate + error + product(estimate, error)
        if step + 1 < ITERS:
            square = 2.0 * error + product(error, error)
            fourth = 2.0 * square + product(square, square)
            iterate = iterate + product(fourth, iterate)
    held[...] = (estimate + identity) * jnp.sqrt(jnp.sqrt(scale))
    root[:HALF] = held[:HALF, HALF:].astype(BF16)
    body, diagonal = fold(held[:HALF, :HALF], held[HALF:, HALF:])
    root[HALF:BLK] = body.astype(BF16)
    root[BLK:] = diagonal.astype(BF16)


def newton(tokens, after, mine, other):
    return pl.pallas_call(
        functools.partial(newton_kernel, tokens),
        out_shape=jax.ShapeDtypeStruct((FOLD, HALF), BF16),
        in_specs=[ANY, VMEM, VMEM],
        out_specs=VMEM,
        scratch_shapes=[pltpu.VMEM((BLK, BLK), F32)],
        compiler_params=params(12),
        cost_estimate=pl.CostEstimate(
            flops=16 * BLK**3, bytes_accessed=8 * BLK * BLK, transcendentals=0
        ),
        name="newton",
    )(after, mine, other)


def unfold_root(folded, root_ref):
    cross = folded[:HALF]
    rest = folded[HALF:].astype(F32)
    first, last = unfold(rest[:HALF], rest[HALF : HALF + 1])
    root_ref[:HALF, :HALF] = first.astype(BF16)
    root_ref[:HALF, HALF:] = cross
    root_ref[HALF:, :HALF] = cross.astype(F32).T.astype(BF16)
    root_ref[HALF:, HALF:] = last.astype(BF16)


def norm_kernel(folded, mine, from_y, from_z, squares, total_ref, root):
    unfold_root(folded, root)
    grams = mine[...].astype(F32) + from_y[...].astype(F32) + from_z[...].astype(F32)
    upper = dot(root[:HALF], root[...])
    last = dot(root[HALF:], root[:, HALF:])
    first, cross = upper[:, :HALF], upper[:, HALF:]
    row, col = places()
    weights = jnp.where(row < col, 2.0 * first, jnp.where(row > col, 2.0 * last, first))
    terms = weights * grams[HALF:BLK] + 2.0 * cross * grams[:HALF]
    terms += jnp.where(row == col, last, 0.0) * grams[BLK : BLK + 1]
    lanes = lambda value: sum(value[:, i : i + LANES] for i in range(0, HALF, LANES))
    new = lanes(jnp.sum(terms, axis=0, keepdims=True))
    row = lax.broadcasted_iota(jnp.int32, total_ref.shape, 0)
    total_ref[...] = jnp.where(row == 0, lanes(squares[...]), jnp.where(row == 1, new, 0.0))


def norm(*operands):
    return pl.pallas_call(
        norm_kernel,
        out_shape=jax.ShapeDtypeStruct((ROWS, LANES), F32),
        in_specs=[VMEM] * 5,
        out_specs=VMEM,
        scratch_shapes=[pltpu.VMEM((BLK, BLK), BF16)],
        compiler_params=params(12),
        name="norm",
    )(*operands)


def multiply_kernel(after, folded, held_ref, u_ref, root_ref):
    unfold_root(folded, root_ref)
    for part in chunks(u_ref.shape[1], BLK):
        u_ref[:, part] = dot(root_ref[...], held_ref[:, part]).astype(BF16)


def multiply(folded, held, after):
    return pl.pallas_call(
        multiply_kernel,
        out_shape=[pltpu.VMEM(held.shape, BF16), jax.ShapeDtypeStruct((BLK, BLK), BF16)],
        in_specs=[ANY, VMEM, VMEM],
        out_specs=[VMEM] * 2,
        input_output_aliases={2: 0},
        compiler_params=params(12),
        cost_estimate=pl.CostEstimate(flops=1880000000, bytes_accessed=1, transcendentals=0),
        name="multiply",
    )(after, folded, held)


def finish_kernel(order, owner_slot, sums, *refs):
    roots, folded, blocks = refs[:EARLY], refs[EARLY:QUAD], refs[QUAD : 2 * QUAD]
    update_ref, owned_ref = refs[2 * QUAD : 2 * QUAD + 2]
    scaled = refs[2 * QUAD + 2 : 3 * QUAD + 2]
    late, empty, sent, stored = refs[3 * QUAD + 2 :]
    both = jnp.sum(sums[...], axis=1, keepdims=True)
    ratio = jnp.sqrt(both[:1] / (both[1:2] + 1e-06))
    columns = blocks[0].shape[1]
    waits = []

    def send(place, rows, columns):
        at = pl.multiple_of(order[place] * BLK + rows.start, rows.size)
        copy = pltpu.make_async_copy(
            scaled[place].at[rows, columns],
            update_ref.at[pl.ds(at, rows.size), columns],
            sent.at[len(waits)],
        )
        copy.start()
        waits.append(copy)

    def store(source, slot):
        return pltpu.make_async_copy(source, owned_ref.at[slot], stored.at[slot])

    def rescale(place, rows):
        scaled[place][rows] = (blocks[place][rows].astype(F32) * ratio).astype(BF16)

    bands = [(place, pl.ds(i, BAND)) for place in range(EARLY) for i in range(0, BLK, BAND)]
    products = [(place, part) for place in range(EARLY, QUAD) for part in chunks(columns, BLK)]
    rescale(*bands[0])
    send(*bands[0], pl.ds(0, columns))
    bands = bands[1:]
    empty[...] = jnp.zeros_like(empty)
    for place in range(EARLY, QUAD):
        unfold_root(folded[place - EARLY], late.at[place - EARLY])
    for slot in range(SLOTS):
        mine = [owner_slot[order[QUAD], order[place]] == order[QUAD + 1] + slot for place in range(QUAD)]
        for place in range(QUAD):
            source = roots[place] if place < EARLY else late.at[place - EARLY]
            pl.when(mine[place])(store(source, slot).start)
        pl.when(jnp.logical_not(functools.reduce(jnp.logical_or, mine)))(store(empty, slot).start)
    for place, part in products:
        product = dot(late[place - EARLY], blocks[place][:, part])
        scaled[place][:, part] = (product * ratio).astype(BF16)
        band, bands = bands[:1], bands[1:]
        for one in band:
            rescale(*one)
            send(*one, pl.ds(0, columns))
        send(place, pl.ds(0, BLK), part)
    for one in bands:
        rescale(*one)
        send(*one, pl.ds(0, columns))
    for copy in waits:
        copy.wait()
    for slot in range(SLOTS):
        store(empty, slot).wait()


def finish(order, owner_slot, sums, roots, folded, blocks):
    columns = blocks[0].shape[1]
    pieces = EARLY * (BLK // BAND) + (QUAD - EARLY) * len(list(chunks(columns, BLK)))
    return pl.pallas_call(
        finish_kernel,
        out_shape=[
            jax.ShapeDtypeStruct((QUAD * BLK, columns), BF16),
            jax.ShapeDtypeStruct((SLOTS, BLK, BLK), BF16),
        ]
        + [pltpu.VMEM((BLK, columns), BF16)] * QUAD,
        in_specs=[SMEM] * 2 + [VMEM] * (1 + 2 * QUAD),
        out_specs=[ANY] * 2 + [VMEM] * QUAD,
        input_output_aliases={3 + QUAD + place: 2 + place for place in range(QUAD)},
        scratch_shapes=[
            pltpu.VMEM((QUAD - EARLY, BLK, BLK), BF16),
            pltpu.VMEM((BLK, BLK), BF16),
            pltpu.SemaphoreType.DMA((pieces,)),
            pltpu.SemaphoreType.DMA((SLOTS,)),
        ],
        compiler_params=params(12),
        name="finish",
    )(order, owner_slot, sums, *roots, *folded, *blocks)[:2]


def swap(value, flip):
    axes = ("pool", "dp")
    count = math.prod(lax.axis_size(axis) for axis in axes)
    return lax.ppermute(value, axes, [(i, i ^ flip) for i in range(count)])


def rounds():
    peer_bits = lax.axis_size("dp").bit_length() - 1
    bits = [1 << i for i in range(peer_bits + lax.axis_size("pool").bit_length() - 1)]
    bits = bits[:peer_bits] + bits[peer_bits:][::-1]
    pairs = [bits[i : i + 2] for i in range(0, len(bits), 2)]
    return [pair if len(pair) == 1 else [*pair, sum(pair)] for pair in pairs]


def add(*values):
    return sum(value.astype(F32) for value in values).astype(BF16)


def per_device(activations, gradient, owner_slot):
    peer_count = lax.axis_size("dp")
    my_index = lax.axis_index("dp")
    group_index = lax.axis_index("pool")
    tokens_all = activations.shape[0] * peer_count
    order = (my_index % QUAD) ^ jnp.arange(QUAD, dtype=jnp.int32)
    order = jnp.concatenate([order, jnp.stack([group_index, my_index * SLOTS])])

    a, b, c, d = statistics(order, activations)
    b, c, d = swap(b, 1), swap(c, 2), swap(d, 3)
    blocks, grams, squares = gram(order, gradient, a)
    mine = add(a, b, c, d)
    flip = QUAD
    other = swap(mine, flip)
    grams = list(grams)
    while 2 * flip < peer_count:
        mine = add(mine, other)
        flip *= 2
        other = swap(mine, flip)

    across = swap(grams[3], 1)
    across, grams[1] = lax.optimization_barrier((across, grams[1]))
    from_y = swap(grams[1], 1)
    from_z = swap(add(grams[2], across), 2)
    root = newton(tokens_all, squares, mine, other)
    folded = (root, swap(root, 1), swap(root, 2), swap(root, 3))
    blocks, folded, roots = list(blocks), list(folded), []

    def precondition(place):
        blocks[place], root = multiply(folded[place], blocks[place], folded[place])
        roots.append(root)

    sums = norm(root, grams[0], from_y, from_z, squares)
    arrivals = {0: [1, 2], 1: [3]}
    for step, flips in enumerate(rounds()):
        received = [swap(sums, flip) for flip in flips]
        if step < EARLY:
            precondition(step)
            blocks[step], *received = lax.optimization_barrier((blocks[step], *received))
        for place in arrivals.get(step, ()):
            folded[place], *received = lax.optimization_barrier((folded[place], *received))
        sums = sums + sum(received)
    update, owned = finish(order, owner_slot, sums, roots, folded[EARLY:], blocks)
    return (update, owned[None])


def solution(mesh):
    in_specs = (P("dp", "pool"), P("pool", "dp"), P())
    out_specs = (P("pool", "dp"), P("pool", "dp", None, None))
    return jax.shard_map(
        per_device, mesh=mesh, in_specs=in_specs, out_specs=out_specs, check_vma=False
    )
```

```python
import functools
import math

import jax
import jax.numpy as jnp
from jax import lax
from jax.experimental import pallas as pl
from jax.experimental.pallas import tpu as pltpu
from jax.sharding import PartitionSpec as P

BLK = 512
HALF = BLK // 2
FOLD = BLK + 16
ITERS = 3
SLOTS = 2
QUAD = 4
EARLY = 3
BAND = 128
ROWS = 8
LANES = 128

damping = 0.01
F32 = jnp.float32
BF16 = jnp.bfloat16
SMEM = pl.BlockSpec(memory_space=pltpu.SMEM)
VMEM = pl.BlockSpec(memory_space=pltpu.VMEM)
ANY = pl.BlockSpec(memory_space=pl.ANY)


def params(mib):
    return pltpu.CompilerParams(vmem_limit_bytes=mib * 2**20)


def dot(left, right, dims=((1,), (0,))):
    return lax.dot_general(left, right, (dims, ((), ())), preferred_element_type=F32)


def places():
    row = lax.broadcasted_iota(jnp.int32, (HALF, HALF), 0)
    col = lax.broadcasted_iota(jnp.int32, (HALF, HALF), 1)
    return row, col


def fold(first, last):
    row, col = places()
    body = jnp.where(row <= col, first, last)
    diagonal = jnp.sum(jnp.where(row == col, last, 0.0), axis=0, keepdims=True)
    return body, jnp.broadcast_to(diagonal, (FOLD - BLK, HALF))


def unfold(body, diagonal):
    row, col = places()
    turned = body.T
    first = jnp.where(row <= col, body, turned)
    last = jnp.where(row > col, body, jnp.where(row < col, turned, diagonal))
    return first, last


def stat_kernel(order, x_ref, *out):
    for place in (1, 2, 3, 0):
        start = pl.multiple_of(order[place] * BLK, BLK)
        left = x_ref[:, pl.ds(start, HALF)]
        right = x_ref[:, pl.ds(pl.multiple_of(start + HALF, HALF), HALF)]
        along = ((0,), (0,))
        out[place][:HALF] = dot(left, right, along).astype(BF16)
        body, diagonal = fold(dot(left, left, along), dot(right, right, along))
        out[place][HALF:BLK] = body.astype(BF16)
        out[place][BLK:] = diagonal.astype(BF16)


def statistics(order, activations):
    return pl.pallas_call(
        stat_kernel,
        out_shape=[jax.ShapeDtypeStruct((FOLD, HALF), BF16)] * QUAD,
        in_specs=[SMEM, VMEM],
        out_specs=[VMEM] * QUAD,
        compiler_params=params(12),
        name="statistics",
    )(order, activations)


def chunks(width, size):
    start = 0
    while width - start >= 2 * size:
        yield pl.ds(start, size)
        start += size
    yield pl.ds(start, width - start)


def gram_kernel(order, after, g_ref, *refs):
    held, folded = refs[:QUAD], refs[QUAD : 2 * QUAD]
    norm_ref, left, last, arrived = refs[2 * QUAD :]
    parts = list(chunks(g_ref.shape[1], 1792))

    def copy(place, index):
        rows = pl.ds(pl.multiple_of(order[place] * BLK, BLK), BLK)
        return pltpu.make_async_copy(
            g_ref.at[rows, parts[index]], held[place].at[:, parts[index]], arrived.at[place, index]
        )

    for place in range(QUAD):
        for index in range(len(parts)):
            copy(place, index).start()
    norm_ref[...] = jnp.zeros_like(norm_ref)
    row, col = places()
    for place in range(QUAD):
        for index, part in enumerate(parts):
            copy(place, index).wait()
            whole = held[place][:, part]
            across = ((1,), (1,))
            terms = dot(whole, whole[:HALF], across), dot(whole[HALF:], whole[HALF:], across)
            if index == 0:
                left[...] = terms[0]
                last[...] = terms[1]
            else:
                left[...] += terms[0]
                last[...] += terms[1]
        squares = jnp.where(row == col, left[:HALF] + last[...], 0.0)
        norm_ref[...] += jnp.sum(squares, axis=0, keepdims=True)
        body, diagonal = fold(left[:HALF], last[...])
        folded[place][:HALF] = left[HALF:].astype(BF16)
        folded[place][HALF:BLK] = body.astype(BF16)
        folded[place][BLK:] = diagonal.astype(BF16)


def gram(order, gradient, after):
    rows, columns = gradient.shape
    parts = len(list(chunks(columns, 1792)))
    results = pl.pallas_call(
        gram_kernel,
        out_shape=[pltpu.VMEM((BLK, columns), BF16)] * QUAD
        + [jax.ShapeDtypeStruct((FOLD, HALF), BF16)] * QUAD
        + [jax.ShapeDtypeStruct((1, HALF), F32)],
        in_specs=[SMEM, ANY, ANY],
        out_specs=[VMEM] * (2 * QUAD + 1),
        scratch_shapes=[
            pltpu.VMEM((BLK, HALF), F32),
            pltpu.VMEM((HALF, HALF), F32),
            pltpu.SemaphoreType.DMA((QUAD, parts)),
        ],
        compiler_params=params(12),
        cost_estimate=pl.CostEstimate(
            flops=2 * rows * columns * BLK, bytes_accessed=2 * rows * columns, transcendentals=0
        ),
        name="gram",
    )(order, after, pltpu.with_memory_space_constraint(gradient, pltpu.HBM))
    return results[:QUAD], results[QUAD : 2 * QUAD], results[-1]


def product(left, right):
    return dot(left.astype(BF16), right.astype(BF16))


def newton_kernel(tokens, after, mine, other, root, held):
    total = (mine[...].astype(F32) + other[...].astype(F32)) / tokens
    cross = total[:HALF]
    first, last = unfold(total[HALF:BLK], total[BLK : BLK + 1])
    held[:HALF, :HALF] = first
    held[:HALF, HALF:] = cross
    held[HALF:, :HALF] = cross.T
    held[HALF:, HALF:] = last
    row = lax.broadcasted_iota(jnp.int32, (BLK, BLK), 0)
    col = lax.broadcasted_iota(jnp.int32, (BLK, BLK), 1)
    identity = jnp.where(row == col, 1.0, 0.0).astype(F32)
    matrix = held[...] + damping * identity
    bound = jnp.max(jnp.sum(jnp.abs(matrix), axis=0, keepdims=True), axis=1, keepdims=True)
    scale = 2.0 / bound
    iterate = matrix * scale
    estimate = None
    for step in range(ITERS):
        error = (identity - iterate) * 0.25
        if estimate is None:
            estimate = error
        else:
            estimate = estimate + error + product(estimate, error)
        if step + 1 < ITERS:
            square = 2.0 * error + product(error, error)
            fourth = 2.0 * square + product(square, square)
            iterate = iterate + product(fourth, iterate)
    held[...] = (estimate + identity) * jnp.sqrt(jnp.sqrt(scale))
    root[:HALF] = held[:HALF, HALF:].astype(BF16)
    body, diagonal = fold(held[:HALF, :HALF], held[HALF:, HALF:])
    root[HALF:BLK] = body.astype(BF16)
    root[BLK:] = diagonal.astype(BF16)


def newton(tokens, after, mine, other):
    return pl.pallas_call(
        functools.partial(newton_kernel, tokens),
        out_shape=jax.ShapeDtypeStruct((FOLD, HALF), BF16),
        in_specs=[ANY, VMEM, VMEM],
        out_specs=VMEM,
        scratch_shapes=[pltpu.VMEM((BLK, BLK), F32)],
        compiler_params=params(12),
        cost_estimate=pl.CostEstimate(
            flops=16 * BLK**3, bytes_accessed=8 * BLK * BLK, transcendentals=0
        ),
        name="newton",
    )(after, mine, other)


def unfold_root(folded, root_ref):
    cross = folded[:HALF]
    rest = folded[HALF:].astype(F32)
    first, last = unfold(rest[:HALF], rest[HALF : HALF + 1])
    root_ref[:HALF, :HALF] = first.astype(BF16)
    root_ref[:HALF, HALF:] = cross
    root_ref[HALF:, :HALF] = cross.astype(F32).T.astype(BF16)
    root_ref[HALF:, HALF:] = last.astype(BF16)


def norm_kernel(folded, mine, from_y, from_z, squares, total_ref, root):
    unfold_root(folded, root)
    grams = mine[...].astype(F32) + from_y[...].astype(F32) + from_z[...].astype(F32)
    first = dot(root[:HALF], root[:, :HALF])
    lower = dot(root[HALF:], root[...])
    cross, last = lower[:, :HALF], lower[:, HALF:]
    row, col = places()
    weights = jnp.where(row < col, 2.0 * first, jnp.where(row > col, 2.0 * last, first))
    terms = weights * grams[HALF:BLK] + 2.0 * cross * grams[:HALF]
    terms += jnp.where(row == col, last, 0.0) * grams[BLK : BLK + 1]
    lanes = lambda value: sum(value[:, i : i + LANES] for i in range(0, HALF, LANES))
    new = lanes(jnp.sum(terms, axis=0, keepdims=True))
    row = lax.broadcasted_iota(jnp.int32, total_ref.shape, 0)
    total_ref[...] = jnp.where(row == 0, lanes(squares[...]), jnp.where(row == 1, new, 0.0))


def norm(*operands):
    return pl.pallas_call(
        norm_kernel,
        out_shape=jax.ShapeDtypeStruct((ROWS, LANES), F32),
        in_specs=[VMEM] * 5,
        out_specs=VMEM,
        scratch_shapes=[pltpu.VMEM((BLK, BLK), BF16)],
        compiler_params=params(12),
        name="norm",
    )(*operands)


def multiply_kernel(after, folded, held_ref, u_ref, root_ref):
    unfold_root(folded, root_ref)
    for part in chunks(u_ref.shape[1], BLK):
        u_ref[:, part] = dot(root_ref[...], held_ref[:, part]).astype(BF16)


def multiply(folded, held, after):
    return pl.pallas_call(
        multiply_kernel,
        out_shape=[pltpu.VMEM(held.shape, BF16), jax.ShapeDtypeStruct((BLK, BLK), BF16)],
        in_specs=[ANY, VMEM, VMEM],
        out_specs=[VMEM] * 2,
        input_output_aliases={2: 0},
        compiler_params=params(12),
        cost_estimate=pl.CostEstimate(flops=1880000000, bytes_accessed=1, transcendentals=0),
        name="multiply",
    )(after, folded, held)


def finish_kernel(order, owner_slot, sums, *refs):
    roots, folded, blocks = refs[:EARLY], refs[EARLY:QUAD], refs[QUAD : 2 * QUAD]
    update_ref, owned_ref = refs[2 * QUAD : 2 * QUAD + 2]
    scaled = refs[2 * QUAD + 2 : 3 * QUAD + 2]
    late, empty, sent, stored = refs[3 * QUAD + 2 :]
    both = jnp.sum(sums[...], axis=1, keepdims=True)
    ratio = jnp.sqrt(both[:1] / (both[1:2] + 1e-06))
    columns = blocks[0].shape[1]
    waits = []

    def send(place, rows, columns):
        at = pl.multiple_of(order[place] * BLK + rows.start, rows.size)
        copy = pltpu.make_async_copy(
            scaled[place].at[rows, columns],
            update_ref.at[pl.ds(at, rows.size), columns],
            sent.at[len(waits)],
        )
        copy.start()
        waits.append(copy)

    def store(source, slot):
        return pltpu.make_async_copy(source, owned_ref.at[slot], stored.at[slot])

    def rescale(place, rows):
        scaled[place][rows] = (blocks[place][rows].astype(F32) * ratio).astype(BF16)

    bands = [(place, pl.ds(i, BAND)) for place in range(EARLY) for i in range(0, BLK, BAND)]
    products = [(place, part) for place in range(EARLY, QUAD) for part in chunks(columns, BLK)]
    rescale(*bands[0])
    send(*bands[0], pl.ds(0, columns))
    bands = bands[1:]
    empty[...] = jnp.zeros_like(empty)
    for place in range(EARLY, QUAD):
        unfold_root(folded[place - EARLY], late.at[place - EARLY])
    for slot in range(SLOTS):
        mine = [owner_slot[order[QUAD], order[place]] == order[QUAD + 1] + slot for place in range(QUAD)]
        for place in range(QUAD):
            source = roots[place] if place < EARLY else late.at[place - EARLY]
            pl.when(mine[place])(store(source, slot).start)
        pl.when(jnp.logical_not(functools.reduce(jnp.logical_or, mine)))(store(empty, slot).start)
    for place, part in products:
        product = dot(late[place - EARLY], blocks[place][:, part])
        scaled[place][:, part] = (product * ratio).astype(BF16)
        band, bands = bands[:1], bands[1:]
        for one in band:
            rescale(*one)
            send(*one, pl.ds(0, columns))
        send(place, pl.ds(0, BLK), part)
    for one in bands:
        rescale(*one)
        send(*one, pl.ds(0, columns))
    for copy in waits:
        copy.wait()
    for slot in range(SLOTS):
        store(empty, slot).wait()


def finish(order, owner_slot, sums, roots, folded, blocks):
    columns = blocks[0].shape[1]
    pieces = EARLY * (BLK // BAND) + (QUAD - EARLY) * len(list(chunks(columns, BLK)))
    return pl.pallas_call(
        finish_kernel,
        out_shape=[
            jax.ShapeDtypeStruct((QUAD * BLK, columns), BF16),
            jax.ShapeDtypeStruct((SLOTS, BLK, BLK), BF16),
        ]
        + [pltpu.VMEM((BLK, columns), BF16)] * QUAD,
        in_specs=[SMEM] * 2 + [VMEM] * (1 + 2 * QUAD),
        out_specs=[ANY] * 2 + [VMEM] * QUAD,
        input_output_aliases={3 + QUAD + place: 2 + place for place in range(QUAD)},
        scratch_shapes=[
            pltpu.VMEM((QUAD - EARLY, BLK, BLK), BF16),
            pltpu.VMEM((BLK, BLK), BF16),
            pltpu.SemaphoreType.DMA((pieces,)),
            pltpu.SemaphoreType.DMA((SLOTS,)),
        ],
        compiler_params=params(12),
        name="finish",
    )(order, owner_slot, sums, *roots, *folded, *blocks)[:2]


def swap(value, flip):
    axes = ("pool", "dp")
    count = math.prod(lax.axis_size(axis) for axis in axes)
    return lax.ppermute(value, axes, [(i, i ^ flip) for i in range(count)])


def rounds():
    peer_bits = lax.axis_size("dp").bit_length() - 1
    bits = [1 << i for i in range(peer_bits + lax.axis_size("pool").bit_length() - 1)]
    bits = bits[peer_bits:] + bits[:peer_bits]
    pairs = [bits[i : i + 2] for i in range(0, len(bits), 2)]
    return [pair if len(pair) == 1 else [*pair, sum(pair)] for pair in pairs]


def add(*values):
    return sum(value.astype(F32) for value in values).astype(BF16)


def per_device(activations, gradient, owner_slot):
    peer_count = lax.axis_size("dp")
    my_index = lax.axis_index("dp")
    group_index = lax.axis_index("pool")
    tokens_all = activations.shape[0] * peer_count
    order = (my_index % QUAD) ^ jnp.arange(QUAD, dtype=jnp.int32)
    order = jnp.concatenate([order, jnp.stack([group_index, my_index * SLOTS])])

    a, b, c, d = statistics(order, activations)
    b, c, d = swap(b, 1), swap(c, 2), swap(d, 3)
    blocks, grams, squares = gram(order, gradient, a)
    mine = add(a, b, c, d)
    flip = QUAD
    other = swap(mine, flip)
    grams = list(grams)
    while 2 * flip < peer_count:
        mine = add(mine, other)
        flip *= 2
        other = swap(mine, flip)

    across = swap(grams[3], 1)
    across, grams[1] = lax.optimization_barrier((across, grams[1]))
    from_y = swap(grams[1], 1)
    from_z = swap(add(grams[2], across), 2)
    root = newton(tokens_all, squares, mine, other)
    folded = (root, swap(root, 1), swap(root, 2), swap(root, 3))
    blocks, folded, roots = list(blocks), list(folded), []

    def precondition(place):
        blocks[place], root = multiply(folded[place], blocks[place], folded[place])
        roots.append(root)

    sums = norm(root, grams[0], from_y, from_z, squares)
    arrivals = {0:[1,2],1:[3]}
    for step, flips in enumerate(rounds()):
        received = [swap(sums, flip) for flip in flips]
        if step < EARLY:
            precondition(step)
            blocks[step], *received = lax.optimization_barrier((blocks[step], *received))
        for place in arrivals.get(step, ()):
            folded[place], *received = lax.optimization_barrier((folded[place], *received))
        sums = sums + sum(received)
    update, owned = finish(order, owner_slot, sums, roots, folded[EARLY:], blocks)
    return (update, owned[None])


def solution(mesh):
    in_specs = (P("dp", "pool"), P("pool", "dp"), P())
    out_specs = (P("pool", "dp"), P("pool", "dp", None, None))
    return jax.shard_map(
        per_device, mesh=mesh, in_specs=in_specs, out_specs=out_specs, check_vma=False
    )
```

```python
import functools
import math

import jax
import jax.numpy as jnp
from jax import lax
from jax.experimental import pallas as pl
from jax.experimental.pallas import tpu as pltpu
from jax.sharding import PartitionSpec as P

BLK = 512
HALF = BLK // 2
FOLD = BLK + 16
ITERS = 3
SLOTS = 2
QUAD = 4
EARLY = 3
BAND = 128
ROWS = 8
LANES = 128

damping = 0.01
F32 = jnp.float32
BF16 = jnp.bfloat16
SMEM = pl.BlockSpec(memory_space=pltpu.SMEM)
VMEM = pl.BlockSpec(memory_space=pltpu.VMEM)
ANY = pl.BlockSpec(memory_space=pl.ANY)


def params(mib):
    return pltpu.CompilerParams(vmem_limit_bytes=mib * 2**20)


def dot(left, right, dims=((1,), (0,))):
    return lax.dot_general(left, right, (dims, ((), ())), preferred_element_type=F32)


def places():
    row = lax.broadcasted_iota(jnp.int32, (HALF, HALF), 0)
    col = lax.broadcasted_iota(jnp.int32, (HALF, HALF), 1)
    return row, col


def fold(first, last):
    row, col = places()
    body = jnp.where(row <= col, first, last)
    diagonal = jnp.sum(jnp.where(row == col, last, 0.0), axis=0, keepdims=True)
    return body, jnp.broadcast_to(diagonal, (FOLD - BLK, HALF))


def unfold(body, diagonal):
    row, col = places()
    turned = body.T
    first = jnp.where(row <= col, body, turned)
    last = jnp.where(row > col, body, jnp.where(row < col, turned, diagonal))
    return first, last


def stat_kernel(order, x_ref, *out):
    for place in (1, 2, 3, 0):
        start = pl.multiple_of(order[place] * BLK, BLK)
        left = x_ref[:, pl.ds(start, HALF)]
        right = x_ref[:, pl.ds(pl.multiple_of(start + HALF, HALF), HALF)]
        along = ((0,), (0,))
        out[place][:HALF] = dot(left, right, along).astype(BF16)
        body, diagonal = fold(dot(left, left, along), dot(right, right, along))
        out[place][HALF:BLK] = body.astype(BF16)
        out[place][BLK:] = diagonal.astype(BF16)


def statistics(order, activations):
    return pl.pallas_call(
        stat_kernel,
        out_shape=[jax.ShapeDtypeStruct((FOLD, HALF), BF16)] * QUAD,
        in_specs=[SMEM, VMEM],
        out_specs=[VMEM] * QUAD,
        compiler_params=params(12),
        name="statistics",
    )(order, activations)


def chunks(width, size):
    start = 0
    while width - start >= 2 * size:
        yield pl.ds(start, size)
        start += size
    yield pl.ds(start, width - start)


def gram_kernel(order, after, g_ref, *refs):
    held, folded = refs[:QUAD], refs[QUAD : 2 * QUAD]
    norm_ref, left, last, arrived = refs[2 * QUAD :]
    parts = list(chunks(g_ref.shape[1], 1792))

    def copy(place, index):
        rows = pl.ds(pl.multiple_of(order[place] * BLK, BLK), BLK)
        return pltpu.make_async_copy(
            g_ref.at[rows, parts[index]], held[place].at[:, parts[index]], arrived.at[place, index]
        )

    for place in range(QUAD):
        for index in range(len(parts)):
            copy(place, index).start()
    norm_ref[...] = jnp.zeros_like(norm_ref)
    row, col = places()
    for place in range(QUAD):
        for index in range(len(parts)):
            copy(place, index).wait()
        whole = held[place][...]
        across = ((1,), (1,))
        left[...] = dot(whole, whole[:HALF], across)
        last[...] = dot(whole[HALF:], whole[HALF:], across)
        squares = jnp.where(row == col, left[:HALF] + last[...], 0.0)
        norm_ref[...] += jnp.sum(squares, axis=0, keepdims=True)
        body, diagonal = fold(left[:HALF], last[...])
        folded[place][:HALF] = left[HALF:].astype(BF16)
        folded[place][HALF:BLK] = body.astype(BF16)
        folded[place][BLK:] = diagonal.astype(BF16)


def gram(order, gradient, after):
    rows, columns = gradient.shape
    parts = len(list(chunks(columns, 1792)))
    results = pl.pallas_call(
        gram_kernel,
        out_shape=[pltpu.VMEM((BLK, columns), BF16)] * QUAD
        + [jax.ShapeDtypeStruct((FOLD, HALF), BF16)] * QUAD
        + [jax.ShapeDtypeStruct((1, HALF), F32)],
        in_specs=[SMEM, ANY, ANY],
        out_specs=[VMEM] * (2 * QUAD + 1),
        scratch_shapes=[
            pltpu.VMEM((BLK, HALF), F32),
            pltpu.VMEM((HALF, HALF), F32),
            pltpu.SemaphoreType.DMA((QUAD, parts)),
        ],
        compiler_params=params(12),
        cost_estimate=pl.CostEstimate(
            flops=2 * rows * columns * BLK, bytes_accessed=2 * rows * columns, transcendentals=0
        ),
        name="gram",
    )(order, after, pltpu.with_memory_space_constraint(gradient, pltpu.HBM))
    return results[:QUAD], results[QUAD : 2 * QUAD], results[-1]


def product(left, right):
    return dot(left.astype(BF16), right.astype(BF16))


def newton_kernel(tokens, after, mine, other, root, held):
    total = (mine[...].astype(F32) + other[...].astype(F32)) / tokens
    cross = total[:HALF]
    first, last = unfold(total[HALF:BLK], total[BLK : BLK + 1])
    held[:HALF, :HALF] = first
    held[:HALF, HALF:] = cross
    held[HALF:, :HALF] = cross.T
    held[HALF:, HALF:] = last
    row = lax.broadcasted_iota(jnp.int32, (BLK, BLK), 0)
    col = lax.broadcasted_iota(jnp.int32, (BLK, BLK), 1)
    identity = jnp.where(row == col, 1.0, 0.0).astype(F32)
    matrix = held[...] + damping * identity
    bound = jnp.max(jnp.sum(jnp.abs(matrix), axis=0, keepdims=True), axis=1, keepdims=True)
    scale = 2.0 / bound
    iterate = matrix * scale
    estimate = None
    for step in range(ITERS):
        error = (identity - iterate) * 0.25
        if estimate is None:
            estimate = error
        else:
            estimate = estimate + error + product(estimate, error)
        if step + 1 < ITERS:
            square = 2.0 * error + product(error, error)
            fourth = 2.0 * square + product(square, square)
            iterate = iterate + product(fourth, iterate)
    held[...] = (estimate + identity) * jnp.sqrt(jnp.sqrt(scale))
    root[:HALF] = held[:HALF, HALF:].astype(BF16)
    body, diagonal = fold(held[:HALF, :HALF], held[HALF:, HALF:])
    root[HALF:BLK] = body.astype(BF16)
    root[BLK:] = diagonal.astype(BF16)


def newton(tokens, after, mine, other):
    return pl.pallas_call(
        functools.partial(newton_kernel, tokens),
        out_shape=jax.ShapeDtypeStruct((FOLD, HALF), BF16),
        in_specs=[ANY, VMEM, VMEM],
        out_specs=VMEM,
        scratch_shapes=[pltpu.VMEM((BLK, BLK), F32)],
        compiler_params=params(12),
        cost_estimate=pl.CostEstimate(
            flops=16 * BLK**3, bytes_accessed=8 * BLK * BLK, transcendentals=0
        ),
        name="newton",
    )(after, mine, other)


def unfold_root(folded, root_ref):
    cross = folded[:HALF]
    rest = folded[HALF:].astype(F32)
    first, last = unfold(rest[:HALF], rest[HALF : HALF + 1])
    root_ref[:HALF, :HALF] = first.astype(BF16)
    root_ref[:HALF, HALF:] = cross
    root_ref[HALF:, :HALF] = cross.astype(F32).T.astype(BF16)
    root_ref[HALF:, HALF:] = last.astype(BF16)


def norm_kernel(folded, mine, from_y, from_z, squares, total_ref, root):
    unfold_root(folded, root)
    grams = mine[...].astype(F32) + from_y[...].astype(F32) + from_z[...].astype(F32)
    first = dot(root[:HALF], root[:, :HALF])
    lower = dot(root[HALF:], root[...])
    cross, last = lower[:, :HALF], lower[:, HALF:]
    row, col = places()
    weights = jnp.where(row < col, 2.0 * first, jnp.where(row > col, 2.0 * last, first))
    terms = weights * grams[HALF:BLK] + 2.0 * cross * grams[:HALF]
    terms += jnp.where(row == col, last, 0.0) * grams[BLK : BLK + 1]
    lanes = lambda value: sum(value[:, i : i + LANES] for i in range(0, HALF, LANES))
    new = lanes(jnp.sum(terms, axis=0, keepdims=True))
    row = lax.broadcasted_iota(jnp.int32, total_ref.shape, 0)
    total_ref[...] = jnp.where(row == 0, lanes(squares[...]), jnp.where(row == 1, new, 0.0))


def norm(*operands):
    return pl.pallas_call(
        norm_kernel,
        out_shape=jax.ShapeDtypeStruct((ROWS, LANES), F32),
        in_specs=[VMEM] * 5,
        out_specs=VMEM,
        scratch_shapes=[pltpu.VMEM((BLK, BLK), BF16)],
        compiler_params=params(12),
        name="norm",
    )(*operands)


def multiply_kernel(after, folded, held_ref, u_ref, root_ref):
    unfold_root(folded, root_ref)
    for part in chunks(u_ref.shape[1], BLK):
        u_ref[:, part] = dot(root_ref[...], held_ref[:, part]).astype(BF16)


def multiply(folded, held, after):
    return pl.pallas_call(
        multiply_kernel,
        out_shape=[pltpu.VMEM(held.shape, BF16), jax.ShapeDtypeStruct((BLK, BLK), BF16)],
        in_specs=[ANY, VMEM, VMEM],
        out_specs=[VMEM] * 2,
        input_output_aliases={2: 0},
        compiler_params=params(12),
        cost_estimate=pl.CostEstimate(flops=1880000000, bytes_accessed=1, transcendentals=0),
        name="multiply",
    )(after, folded, held)


def finish_kernel(order, owner_slot, sums, *refs):
    roots, folded, blocks = refs[:EARLY], refs[EARLY:QUAD], refs[QUAD : 2 * QUAD]
    update_ref, owned_ref = refs[2 * QUAD : 2 * QUAD + 2]
    scaled = refs[2 * QUAD + 2 : 3 * QUAD + 2]
    late, empty, sent, stored = refs[3 * QUAD + 2 :]
    both = jnp.sum(sums[...], axis=1, keepdims=True)
    ratio = jnp.sqrt(both[:1] / (both[1:2] + 1e-06))
    columns = blocks[0].shape[1]
    waits = []

    def send(place, rows, columns):
        at = pl.multiple_of(order[place] * BLK + rows.start, rows.size)
        copy = pltpu.make_async_copy(
            scaled[place].at[rows, columns],
            update_ref.at[pl.ds(at, rows.size), columns],
            sent.at[len(waits)],
        )
        copy.start()
        waits.append(copy)

    def store(source, slot):
        return pltpu.make_async_copy(source, owned_ref.at[slot], stored.at[slot])

    def rescale(place, rows):
        scaled[place][rows] = (blocks[place][rows].astype(F32) * ratio).astype(BF16)

    bands = [(place, pl.ds(i, BAND)) for place in range(EARLY) for i in range(0, BLK, BAND)]
    products = [(place, part) for place in range(EARLY, QUAD) for part in chunks(columns, BLK)]
    rescale(*bands[0])
    send(*bands[0], pl.ds(0, columns))
    bands = bands[1:]
    empty[...] = jnp.zeros_like(empty)
    for place in range(EARLY, QUAD):
        unfold_root(folded[place - EARLY], late.at[place - EARLY])
    for slot in range(SLOTS):
        mine = [owner_slot[order[QUAD], order[place]] == order[QUAD + 1] + slot for place in range(QUAD)]
        for place in range(QUAD):
            source = roots[place] if place < EARLY else late.at[place - EARLY]
            pl.when(mine[place])(store(source, slot).start)
        pl.when(jnp.logical_not(functools.reduce(jnp.logical_or, mine)))(store(empty, slot).start)
    for place, part in products:
        product = dot(late[place - EARLY], blocks[place][:, part])
        scaled[place][:, part] = (product * ratio).astype(BF16)
        band, bands = bands[:1], bands[1:]
        for one in band:
            rescale(*one)
            send(*one, pl.ds(0, columns))
        send(place, pl.ds(0, BLK), part)
    for one in bands:
        rescale(*one)
        send(*one, pl.ds(0, columns))
    for copy in waits:
        copy.wait()
    for slot in range(SLOTS):
        store(empty, slot).wait()


def finish(order, owner_slot, sums, roots, folded, blocks):
    columns = blocks[0].shape[1]
    pieces = EARLY * (BLK // BAND) + (QUAD - EARLY) * len(list(chunks(columns, BLK)))
    return pl.pallas_call(
        finish_kernel,
        out_shape=[
            jax.ShapeDtypeStruct((QUAD * BLK, columns), BF16),
            jax.ShapeDtypeStruct((SLOTS, BLK, BLK), BF16),
        ]
        + [pltpu.VMEM((BLK, columns), BF16)] * QUAD,
        in_specs=[SMEM] * 2 + [VMEM] * (1 + 2 * QUAD),
        out_specs=[ANY] * 2 + [VMEM] * QUAD,
        input_output_aliases={3 + QUAD + place: 2 + place for place in range(QUAD)},
        scratch_shapes=[
            pltpu.VMEM((QUAD - EARLY, BLK, BLK), BF16),
            pltpu.VMEM((BLK, BLK), BF16),
            pltpu.SemaphoreType.DMA((pieces,)),
            pltpu.SemaphoreType.DMA((SLOTS,)),
        ],
        compiler_params=params(12),
        name="finish",
    )(order, owner_slot, sums, *roots, *folded, *blocks)[:2]


def swap(value, flip):
    axes = ("pool", "dp")
    count = math.prod(lax.axis_size(axis) for axis in axes)
    return lax.ppermute(value, axes, [(i, i ^ flip) for i in range(count)])


def rounds():
    peer_bits = lax.axis_size("dp").bit_length() - 1
    bits = [1 << i for i in range(peer_bits + lax.axis_size("pool").bit_length() - 1)]
    bits = bits[peer_bits:] + bits[:peer_bits]
    pairs = [bits[i : i + 2] for i in range(0, len(bits), 2)]
    return [pair if len(pair) == 1 else [*pair, sum(pair)] for pair in pairs]


def add(*values):
    return sum(value.astype(F32) for value in values).astype(BF16)


def per_device(activations, gradient, owner_slot):
    peer_count = lax.axis_size("dp")
    my_index = lax.axis_index("dp")
    group_index = lax.axis_index("pool")
    tokens_all = activations.shape[0] * peer_count
    order = (my_index % QUAD) ^ jnp.arange(QUAD, dtype=jnp.int32)
    order = jnp.concatenate([order, jnp.stack([group_index, my_index * SLOTS])])

    a, b, c, d = statistics(order, activations)
    b, c, d = swap(b, 1), swap(c, 2), swap(d, 3)
    blocks, grams, squares = gram(order, gradient, a)
    mine = add(a, b, c, d)
    flip = QUAD
    other = swap(mine, flip)
    grams = list(grams)
    while 2 * flip < peer_count:
        mine = add(mine, other)
        flip *= 2
        other = swap(mine, flip)

    across = swap(grams[3], 1)
    across, grams[1] = lax.optimization_barrier((across, grams[1]))
    from_y = swap(grams[1], 1)
    from_z = swap(add(grams[2], across), 2)
    root = newton(tokens_all, squares, mine, other)
    folded = [root, swap(root, 1), swap(root, 2)]
    folded.append(swap(folded[2], 1))
    blocks, roots = list(blocks), []

    def precondition(place):
        blocks[place], root = multiply(folded[place], blocks[place], folded[place])
        roots.append(root)

    sums = norm(root, grams[0], from_y, from_z, squares)
    early, arrivals = {0:[0],1:[1],2:[2]}, {0:[1,2],1:[3]}
    for step, flips in enumerate(rounds()):
        received = [swap(sums, flip) for flip in flips]
        for place in early.get(step, ()):
            precondition(place)
            blocks[place], *received = lax.optimization_barrier((blocks[place], *received))
        for place in arrivals.get(step, ()):
            folded[place], *received = lax.optimization_barrier((folded[place], *received))
        sums = sums + sum(received)
    update, owned = finish(order, owner_slot, sums, roots, folded[EARLY:], blocks)
    return (update, owned[None])


def solution(mesh):
    in_specs = (P("dp", "pool"), P("pool", "dp"), P())
    out_specs = (P("pool", "dp"), P("pool", "dp", None, None))
    return jax.shard_map(
        per_device, mesh=mesh, in_specs=in_specs, out_specs=out_specs, check_vma=False
    )
```

```python
import functools
import math

import jax
import jax.numpy as jnp
from jax import lax
from jax.experimental import pallas as pl
from jax.experimental.pallas import tpu as pltpu
from jax.sharding import PartitionSpec as P

BLK = 512
HALF = BLK // 2
FOLD = BLK + 16
ITERS = 3
SLOTS = 2
QUAD = 4
EARLY = 3
BAND = 128
ROWS = 8
LANES = 128

damping = 0.01
F32 = jnp.float32
BF16 = jnp.bfloat16
SMEM = pl.BlockSpec(memory_space=pltpu.SMEM)
VMEM = pl.BlockSpec(memory_space=pltpu.VMEM)
ANY = pl.BlockSpec(memory_space=pl.ANY)


def params(mib):
    return pltpu.CompilerParams(vmem_limit_bytes=mib * 2**20)


def dot(left, right, dims=((1,), (0,))):
    return lax.dot_general(left, right, (dims, ((), ())), preferred_element_type=F32)


def places():
    row = lax.broadcasted_iota(jnp.int32, (HALF, HALF), 0)
    col = lax.broadcasted_iota(jnp.int32, (HALF, HALF), 1)
    return row, col


def fold(first, last):
    row, col = places()
    body = jnp.where(row <= col, first, last)
    diagonal = jnp.sum(jnp.where(row == col, last, 0.0), axis=0, keepdims=True)
    return body, jnp.broadcast_to(diagonal, (FOLD - BLK, HALF))


def unfold(body, diagonal):
    row, col = places()
    turned = body.T
    first = jnp.where(row <= col, body, turned)
    last = jnp.where(row > col, body, jnp.where(row < col, turned, diagonal))
    return first, last


def stat_kernel(order, x_ref, *out):
    for place in (1, 2, 3, 0):
        start = pl.multiple_of(order[place] * BLK, BLK)
        left = x_ref[:, pl.ds(start, HALF)]
        right = x_ref[:, pl.ds(pl.multiple_of(start + HALF, HALF), HALF)]
        along = ((0,), (0,))
        out[place][:HALF] = dot(left, right, along).astype(BF16)
        body, diagonal = fold(dot(left, left, along), dot(right, right, along))
        out[place][HALF:BLK] = body.astype(BF16)
        out[place][BLK:] = diagonal.astype(BF16)


def statistics(order, activations):
    return pl.pallas_call(
        stat_kernel,
        out_shape=[jax.ShapeDtypeStruct((FOLD, HALF), BF16)] * QUAD,
        in_specs=[SMEM, VMEM],
        out_specs=[VMEM] * QUAD,
        compiler_params=params(12),
        name="statistics",
    )(order, activations)


def chunks(width, size):
    start = 0
    while width - start >= 2 * size:
        yield pl.ds(start, size)
        start += size
    yield pl.ds(start, width - start)


def gram_kernel(order, after, g_ref, *refs):
    held, folded = refs[:QUAD], refs[QUAD : 2 * QUAD]
    norm_ref, left, last, arrived = refs[2 * QUAD :]
    parts = list(chunks(g_ref.shape[1], 1792))

    def copy(place, index):
        rows = pl.ds(pl.multiple_of(order[place] * BLK, BLK), BLK)
        return pltpu.make_async_copy(
            g_ref.at[rows, parts[index]], held[place].at[:, parts[index]], arrived.at[place, index]
        )

    for place in range(QUAD):
        for index in range(len(parts)):
            copy(place, index).start()
    norm_ref[...] = jnp.zeros_like(norm_ref)
    row, col = places()
    for place in range(QUAD):
        for index in range(len(parts)):
            copy(place, index).wait()
        whole = held[place][...]
        across = ((1,), (1,))
        left[...] = dot(whole, whole[:HALF], across)
        last[...] = dot(whole[HALF:], whole[HALF:], across)
        squares = jnp.where(row == col, left[:HALF] + last[...], 0.0)
        norm_ref[...] += jnp.sum(squares, axis=0, keepdims=True)
        body, diagonal = fold(left[:HALF], last[...])
        folded[place][:HALF] = left[HALF:].astype(BF16)
        folded[place][HALF:BLK] = body.astype(BF16)
        folded[place][BLK:] = diagonal.astype(BF16)


def gram(order, gradient, after):
    rows, columns = gradient.shape
    parts = len(list(chunks(columns, 1792)))
    results = pl.pallas_call(
        gram_kernel,
        out_shape=[pltpu.VMEM((BLK, columns), BF16)] * QUAD
        + [jax.ShapeDtypeStruct((FOLD, HALF), BF16)] * QUAD
        + [jax.ShapeDtypeStruct((1, HALF), F32)],
        in_specs=[SMEM, ANY, ANY],
        out_specs=[VMEM] * (2 * QUAD + 1),
        scratch_shapes=[
            pltpu.VMEM((BLK, HALF), F32),
            pltpu.VMEM((HALF, HALF), F32),
            pltpu.SemaphoreType.DMA((QUAD, parts)),
        ],
        compiler_params=params(12),
        cost_estimate=pl.CostEstimate(
            flops=2 * rows * columns * BLK, bytes_accessed=2 * rows * columns, transcendentals=0
        ),
        name="gram",
    )(order, after, pltpu.with_memory_space_constraint(gradient, pltpu.HBM))
    return results[:QUAD], results[QUAD : 2 * QUAD], results[-1]


def product(left, right):
    return dot(left.astype(BF16), right.astype(BF16))


def newton_kernel(tokens, after, mine, other, root, held):
    total = (mine[...].astype(F32) + other[...].astype(F32)) / tokens
    cross = total[:HALF]
    first, last = unfold(total[HALF:BLK], total[BLK : BLK + 1])
    held[:HALF, :HALF] = first
    held[:HALF, HALF:] = cross
    held[HALF:, :HALF] = cross.T
    held[HALF:, HALF:] = last
    row = lax.broadcasted_iota(jnp.int32, (BLK, BLK), 0)
    col = lax.broadcasted_iota(jnp.int32, (BLK, BLK), 1)
    identity = jnp.where(row == col, 1.0, 0.0).astype(F32)
    matrix = held[...] + damping * identity
    bound = jnp.max(jnp.sum(jnp.abs(matrix), axis=0, keepdims=True), axis=1, keepdims=True)
    scale = 2.0 / bound
    iterate = matrix * scale
    estimate = None
    for step in range(ITERS):
        error = (identity - iterate) * 0.25
        if estimate is None:
            estimate = error
        else:
            estimate = estimate + error + product(estimate, error)
        if step + 1 < ITERS:
            square = 2.0 * error + product(error, error)
            fourth = 2.0 * square + product(square, square)
            iterate = iterate + product(fourth, iterate)
    held[...] = (estimate + identity) * jnp.sqrt(jnp.sqrt(scale))
    root[:HALF] = held[:HALF, HALF:].astype(BF16)
    body, diagonal = fold(held[:HALF, :HALF], held[HALF:, HALF:])
    root[HALF:BLK] = body.astype(BF16)
    root[BLK:] = diagonal.astype(BF16)


def newton(tokens, after, mine, other):
    return pl.pallas_call(
        functools.partial(newton_kernel, tokens),
        out_shape=jax.ShapeDtypeStruct((FOLD, HALF), BF16),
        in_specs=[ANY, VMEM, VMEM],
        out_specs=VMEM,
        scratch_shapes=[pltpu.VMEM((BLK, BLK), F32)],
        compiler_params=params(12),
        cost_estimate=pl.CostEstimate(
            flops=16 * BLK**3, bytes_accessed=8 * BLK * BLK, transcendentals=0
        ),
        name="newton",
    )(after, mine, other)


def unfold_root(folded, root_ref):
    cross = folded[:HALF]
    rest = folded[HALF:].astype(F32)
    first, last = unfold(rest[:HALF], rest[HALF : HALF + 1])
    root_ref[:HALF, :HALF] = first.astype(BF16)
    root_ref[:HALF, HALF:] = cross
    root_ref[HALF:, :HALF] = cross.astype(F32).T.astype(BF16)
    root_ref[HALF:, HALF:] = last.astype(BF16)


def norm_kernel(folded, mine, from_y, from_z, squares, total_ref, root):
    unfold_root(folded, root)
    grams = mine[...].astype(F32) + from_y[...].astype(F32) + from_z[...].astype(F32)
    first = dot(root[:HALF], root[:, :HALF])
    lower = dot(root[HALF:], root[...])
    cross, last = lower[:, :HALF], lower[:, HALF:]
    row, col = places()
    weights = jnp.where(row < col, 2.0 * first, jnp.where(row > col, 2.0 * last, first))
    terms = weights * grams[HALF:BLK] + 2.0 * cross * grams[:HALF]
    terms += jnp.where(row == col, last, 0.0) * grams[BLK : BLK + 1]
    lanes = lambda value: sum(value[:, i : i + LANES] for i in range(0, HALF, LANES))
    new = lanes(jnp.sum(terms, axis=0, keepdims=True))
    row = lax.broadcasted_iota(jnp.int32, total_ref.shape, 0)
    total_ref[...] = jnp.where(row == 0, lanes(squares[...]), jnp.where(row == 1, new, 0.0))


def norm(*operands):
    return pl.pallas_call(
        norm_kernel,
        out_shape=jax.ShapeDtypeStruct((ROWS, LANES), F32),
        in_specs=[VMEM] * 5,
        out_specs=VMEM,
        scratch_shapes=[pltpu.VMEM((BLK, BLK), BF16)],
        compiler_params=params(12),
        name="norm",
    )(*operands)


def multiply_kernel(after, folded, held_ref, u_ref, root_ref):
    unfold_root(folded, root_ref)
    for part in chunks(u_ref.shape[1], BLK):
        u_ref[:, part] = dot(root_ref[...], held_ref[:, part]).astype(BF16)


def multiply(folded, held, after):
    return pl.pallas_call(
        multiply_kernel,
        out_shape=[pltpu.VMEM(held.shape, BF16), jax.ShapeDtypeStruct((BLK, BLK), BF16)],
        in_specs=[ANY, VMEM, VMEM],
        out_specs=[VMEM] * 2,
        input_output_aliases={2: 0},
        compiler_params=params(12),
        cost_estimate=pl.CostEstimate(flops=1, bytes_accessed=1, transcendentals=0),
        name="multiply",
    )(after, folded, held)


def finish_kernel(order, owner_slot, sums, *refs):
    roots, folded, blocks = refs[:EARLY], refs[EARLY:QUAD], refs[QUAD : 2 * QUAD]
    update_ref, owned_ref = refs[2 * QUAD : 2 * QUAD + 2]
    scaled = refs[2 * QUAD + 2 : 3 * QUAD + 2]
    late, empty, sent, stored = refs[3 * QUAD + 2 :]
    both = jnp.sum(sums[...], axis=1, keepdims=True)
    ratio = jnp.sqrt(both[:1] / (both[1:2] + 1e-06))
    columns = blocks[0].shape[1]
    waits = []

    def send(place, rows, columns):
        at = pl.multiple_of(order[place] * BLK + rows.start, rows.size)
        copy = pltpu.make_async_copy(
            scaled[place].at[rows, columns],
            update_ref.at[pl.ds(at, rows.size), columns],
            sent.at[len(waits)],
        )
        copy.start()
        waits.append(copy)

    def store(source, slot):
        return pltpu.make_async_copy(source, owned_ref.at[slot], stored.at[slot])

    def rescale(place, rows):
        scaled[place][rows] = (blocks[place][rows].astype(F32) * ratio).astype(BF16)

    bands = [(place, pl.ds(i, BAND)) for place in range(EARLY) for i in range(0, BLK, BAND)]
    products = [(place, part) for place in range(EARLY, QUAD) for part in chunks(columns, BLK)]
    rescale(*bands[0])
    send(*bands[0], pl.ds(0, columns))
    bands = bands[1:]
    empty[...] = jnp.zeros_like(empty)
    for place in range(EARLY, QUAD):
        unfold_root(folded[place - EARLY], late.at[place - EARLY])
    for slot in range(SLOTS):
        mine = [owner_slot[order[QUAD], order[place]] == order[QUAD + 1] + slot for place in range(QUAD)]
        for place in range(QUAD):
            source = roots[place] if place < EARLY else late.at[place - EARLY]
            pl.when(mine[place])(store(source, slot).start)
        pl.when(jnp.logical_not(functools.reduce(jnp.logical_or, mine)))(store(empty, slot).start)
    for place, part in products:
        product = dot(late[place - EARLY], blocks[place][:, part])
        scaled[place][:, part] = (product * ratio).astype(BF16)
        band, bands = bands[:1], bands[1:]
        for one in band:
            rescale(*one)
            send(*one, pl.ds(0, columns))
        send(place, pl.ds(0, BLK), part)
    for one in bands:
        rescale(*one)
        send(*one, pl.ds(0, columns))
    for copy in waits:
        copy.wait()
    for slot in range(SLOTS):
        store(empty, slot).wait()


def finish(order, owner_slot, sums, roots, folded, blocks):
    columns = blocks[0].shape[1]
    pieces = EARLY * (BLK // BAND) + (QUAD - EARLY) * len(list(chunks(columns, BLK)))
    return pl.pallas_call(
        finish_kernel,
        out_shape=[
            jax.ShapeDtypeStruct((QUAD * BLK, columns), BF16),
            jax.ShapeDtypeStruct((SLOTS, BLK, BLK), BF16),
        ]
        + [pltpu.VMEM((BLK, columns), BF16)] * QUAD,
        in_specs=[SMEM] * 2 + [VMEM] * (1 + 2 * QUAD),
        out_specs=[ANY] * 2 + [VMEM] * QUAD,
        input_output_aliases={3 + QUAD + place: 2 + place for place in range(QUAD)},
        scratch_shapes=[
            pltpu.VMEM((QUAD - EARLY, BLK, BLK), BF16),
            pltpu.VMEM((BLK, BLK), BF16),
            pltpu.SemaphoreType.DMA((pieces,)),
            pltpu.SemaphoreType.DMA((SLOTS,)),
        ],
        compiler_params=params(12),
        name="finish",
    )(order, owner_slot, sums, *roots, *folded, *blocks)[:2]


def swap(value, flip):
    axes = ("pool", "dp")
    count = math.prod(lax.axis_size(axis) for axis in axes)
    return lax.ppermute(value, axes, [(i, i ^ flip) for i in range(count)])


def rounds():
    peer_bits = lax.axis_size("dp").bit_length() - 1
    bits = [1 << i for i in range(peer_bits + lax.axis_size("pool").bit_length() - 1)]
    bits = bits[peer_bits:] + bits[:peer_bits]
    pairs = [bits[i : i + 2] for i in range(0, len(bits), 2)]
    return [pair if len(pair) == 1 else [*pair, sum(pair)] for pair in pairs]


def add(*values):
    return sum(value.astype(F32) for value in values).astype(BF16)


def per_device(activations, gradient, owner_slot):
    peer_count = lax.axis_size("dp")
    my_index = lax.axis_index("dp")
    group_index = lax.axis_index("pool")
    tokens_all = activations.shape[0] * peer_count
    order = (my_index % QUAD) ^ jnp.arange(QUAD, dtype=jnp.int32)
    order = jnp.concatenate([order, jnp.stack([group_index, my_index * SLOTS])])

    a, b, c, d = statistics(order, activations)
    b, c, d = swap(b, 1), swap(c, 2), swap(d, 3)
    blocks, grams, squares = gram(order, gradient, a)
    mine = add(a, b, c, d)
    flip = QUAD
    other = swap(mine, flip)
    grams = list(grams)
    while 2 * flip < peer_count:
        mine = add(mine, other)
        flip *= 2
        other = swap(mine, flip)

    across = swap(grams[3], 1)
    across, grams[1] = lax.optimization_barrier((across, grams[1]))
    from_y = swap(grams[1], 1)
    from_z = swap(add(grams[2], across), 2)
    root = newton(tokens_all, squares, mine, other)
    folded = [root, swap(root, 1), swap(root, 2)]
    folded.append(swap(folded[2], 1))
    blocks, roots = list(blocks), []

    def precondition(place):
        blocks[place], root = multiply(folded[place], blocks[place], folded[place])
        roots.append(root)

    sums = norm(root, grams[0], from_y, from_z, squares)
    early, arrivals = {0:[0],1:[1],2:[2]}, {1:[1,2],2:[3]}
    for step, flips in enumerate(rounds()):
        received = [swap(sums, flip) for flip in flips]
        for place in early.get(step, ()):
            precondition(place)
            blocks[place], *received = lax.optimization_barrier((blocks[place], *received))
        for place in arrivals.get(step, ()):
            folded[place], *received = lax.optimization_barrier((folded[place], *received))
        sums = sums + sum(received)
    update, owned = finish(order, owner_slot, sums, roots, folded[EARLY:], blocks)
    return (update, owned[None])


def solution(mesh):
    in_specs = (P("dp", "pool"), P("pool", "dp"), P())
    out_specs = (P("pool", "dp"), P("pool", "dp", None, None))
    return jax.shard_map(
        per_device, mesh=mesh, in_specs=in_specs, out_specs=out_specs, check_vma=False
    )
```

```python
import functools
import math

import jax
import jax.numpy as jnp
from jax import lax
from jax.experimental import pallas as pl
from jax.experimental.pallas import tpu as pltpu
from jax.sharding import PartitionSpec as P

BLK = 512
HALF = BLK // 2
TAIL = HALF + 16
FOLD = HALF + TAIL
ITERS = 3
SLOTS = 2
QUAD = 4
EARLY = 3
BAND = 128
ROWS = 8
LANES = 128

damping = 0.01
F32 = jnp.float32
BF16 = jnp.bfloat16
SMEM = pl.BlockSpec(memory_space=pltpu.SMEM)
VMEM = pl.BlockSpec(memory_space=pltpu.VMEM)
ANY = pl.BlockSpec(memory_space=pl.ANY)


def params(mib):
    return pltpu.CompilerParams(vmem_limit_bytes=mib * 2**20)


def dot(left, right, dims=((1,), (0,))):
    return lax.dot_general(left, right, (dims, ((), ())), preferred_element_type=F32)


def places():
    row = lax.broadcasted_iota(jnp.int32, (HALF, HALF), 0)
    col = lax.broadcasted_iota(jnp.int32, (HALF, HALF), 1)
    return row, col


def fold(first, last):
    row, col = places()
    body = jnp.where(row <= col, first, last)
    diagonal = jnp.sum(jnp.where(row == col, last, 0.0), axis=0, keepdims=True)
    return body, jnp.broadcast_to(diagonal, (FOLD - BLK, HALF))


def unfold(body, diagonal):
    row, col = places()
    turned = body.T
    first = jnp.where(row <= col, body, turned)
    last = jnp.where(row > col, body, jnp.where(row < col, turned, diagonal))
    return first, last


def folded_shapes(*splits):
    rows = [part for split in splits for part in ((HALF, TAIL) if split else (FOLD,))]
    return [jax.ShapeDtypeStruct((part, HALF), BF16) for part in rows]


def store_folded(refs, cross, first, last):
    body, diagonal = fold(first, last)
    refs = list(refs) if len(refs) > 1 else [refs[0].at[:HALF], refs[0].at[HALF:]]
    refs[0][...] = cross.astype(BF16)
    refs[1][:HALF] = body.astype(BF16)
    refs[1][HALF:] = diagonal.astype(BF16)


def load_folded(refs):
    return (refs[0][:HALF], refs[0][HALF:]) if len(refs) == 1 else (refs[0][...], refs[1][...])


def stat_kernel(order, x_ref, *out):
    for place, refs in enumerate((out[:1], out[1:2], out[2:3], out[3:])):
        start = pl.multiple_of(order[place] * BLK, BLK)
        left = x_ref[:, pl.ds(start, HALF)]
        right = x_ref[:, pl.ds(pl.multiple_of(start + HALF, HALF), HALF)]
        along = ((0,), (0,))
        store_folded(refs, dot(left, right, along), dot(left, left, along), dot(right, right, along))


def statistics(order, activations):
    shapes = folded_shapes(False, False, False, True)
    a, b, c, *d = pl.pallas_call(
        stat_kernel,
        out_shape=shapes,
        in_specs=[SMEM, VMEM],
        out_specs=[VMEM] * len(shapes),
        compiler_params=params(12),
        name="statistics",
    )(order, activations)
    return a, b, c, d


def chunks(width, size):
    start = 0
    while width - start >= 2 * size:
        yield pl.ds(start, size)
        start += size
    yield pl.ds(start, width - start)


def gram_kernel(order, after, g_ref, *refs):
    held, folded = refs[:QUAD], refs[QUAD : 2 * QUAD]
    norm_ref, left, last, arrived = refs[2 * QUAD :]
    parts = list(chunks(g_ref.shape[1], 1792))

    def copy(place, index):
        rows = pl.ds(pl.multiple_of(order[place] * BLK, BLK), BLK)
        return pltpu.make_async_copy(
            g_ref.at[rows, parts[index]], held[place].at[:, parts[index]], arrived.at[place, index]
        )

    for place in range(QUAD):
        for index in range(len(parts)):
            copy(place, index).start()
    norm_ref[...] = jnp.zeros_like(norm_ref)
    row, col = places()
    for place in range(QUAD):
        for index in range(len(parts)):
            copy(place, index).wait()
        whole = held[place][...]
        across = ((1,), (1,))
        left[...] = dot(whole, whole[:HALF], across)
        last[...] = dot(whole[HALF:], whole[HALF:], across)
        squares = jnp.where(row == col, left[:HALF] + last[...], 0.0)
        norm_ref[...] += jnp.sum(squares, axis=0, keepdims=True)
        store_folded(folded[place : place + 1], left[HALF:], left[:HALF], last[...])


def gram(order, gradient, after):
    rows, columns = gradient.shape
    parts = len(list(chunks(columns, 1792)))
    results = pl.pallas_call(
        gram_kernel,
        out_shape=[pltpu.VMEM((BLK, columns), BF16)] * QUAD
        + [jax.ShapeDtypeStruct((FOLD, HALF), BF16)] * QUAD
        + [jax.ShapeDtypeStruct((1, HALF), F32)],
        in_specs=[SMEM, ANY, ANY],
        out_specs=[VMEM] * (2 * QUAD + 1),
        scratch_shapes=[
            pltpu.VMEM((BLK, HALF), F32),
            pltpu.VMEM((HALF, HALF), F32),
            pltpu.SemaphoreType.DMA((QUAD, parts)),
        ],
        compiler_params=params(12),
        cost_estimate=pl.CostEstimate(
            flops=2 * rows * columns * BLK, bytes_accessed=2 * rows * columns, transcendentals=0
        ),
        name="gram",
    )(order, after, pltpu.with_memory_space_constraint(gradient, pltpu.HBM))
    return results[:QUAD], results[QUAD : 2 * QUAD], results[-1]


def product(left, right):
    return dot(left.astype(BF16), right.astype(BF16))


def newton_kernel(tokens, after, mine0, mine1, other0, other1, root, root0, root1, held):
    cross = (mine0[...].astype(F32) + other0[...].astype(F32)) / tokens
    rest = (mine1[...].astype(F32) + other1[...].astype(F32)) / tokens
    first, last = unfold(rest[:HALF], rest[HALF : HALF + 1])
    held[:HALF, :HALF] = first
    held[:HALF, HALF:] = cross
    held[HALF:, :HALF] = cross.T
    held[HALF:, HALF:] = last
    row = lax.broadcasted_iota(jnp.int32, (BLK, BLK), 0)
    col = lax.broadcasted_iota(jnp.int32, (BLK, BLK), 1)
    identity = jnp.where(row == col, 1.0, 0.0).astype(F32)
    matrix = held[...] + damping * identity
    bound = jnp.max(jnp.sum(jnp.abs(matrix), axis=0, keepdims=True), axis=1, keepdims=True)
    scale = 2.0 / bound
    iterate = matrix * scale
    estimate = None
    for step in range(ITERS):
        error = (identity - iterate) * 0.25
        if estimate is None:
            estimate = error
        else:
            estimate = estimate + error + product(estimate, error)
        if step + 1 < ITERS:
            square = 2.0 * error + product(error, error)
            fourth = 2.0 * square + product(square, square)
            iterate = iterate + product(fourth, iterate)
    held[...] = (estimate + identity) * jnp.sqrt(jnp.sqrt(scale))
    store_folded((root0, root1), held[:HALF, HALF:], held[:HALF, :HALF], held[HALF:, HALF:])
    root[:HALF] = root0[...]
    root[HALF:] = root1[...]


def newton(tokens, after, mine, other):
    return pl.pallas_call(
        functools.partial(newton_kernel, tokens),
        out_shape=folded_shapes(False, True),
        in_specs=[ANY] + [VMEM] * 4,
        out_specs=[VMEM] * 3,
        scratch_shapes=[pltpu.VMEM((BLK, BLK), F32)],
        compiler_params=params(12),
        cost_estimate=pl.CostEstimate(
            flops=16 * BLK**3, bytes_accessed=8 * BLK * BLK, transcendentals=0
        ),
        name="newton",
    )(after, *mine, *other)


def unfold_root(refs, root_ref):
    cross, rest = load_folded(refs)
    rest = rest.astype(F32)
    first, last = unfold(rest[:HALF], rest[HALF : HALF + 1])
    root_ref[:HALF, :HALF] = first.astype(BF16)
    root_ref[:HALF, HALF:] = cross
    root_ref[HALF:, :HALF] = cross.astype(F32).T.astype(BF16)
    root_ref[HALF:, HALF:] = last.astype(BF16)


def norm_kernel(folded, mine, from_y, from_z, squares, total_ref, root):
    unfold_root((folded,), root)
    grams = mine[...].astype(F32) + from_y[...].astype(F32) + from_z[...].astype(F32)
    first = dot(root[:HALF], root[:, :HALF])
    lower = dot(root[HALF:], root[...])
    cross, last = lower[:, :HALF], lower[:, HALF:]
    row, col = places()
    weights = jnp.where(row < col, 2.0 * first, jnp.where(row > col, 2.0 * last, first))
    terms = weights * grams[HALF:BLK] + 2.0 * cross * grams[:HALF]
    terms += jnp.where(row == col, last, 0.0) * grams[BLK : BLK + 1]
    lanes = lambda value: sum(value[:, i : i + LANES] for i in range(0, HALF, LANES))
    new = lanes(jnp.sum(terms, axis=0, keepdims=True))
    row = lax.broadcasted_iota(jnp.int32, total_ref.shape, 0)
    total_ref[...] = jnp.where(row == 0, lanes(squares[...]), jnp.where(row == 1, new, 0.0))


def norm(*operands):
    return pl.pallas_call(
        norm_kernel,
        out_shape=jax.ShapeDtypeStruct((ROWS, LANES), F32),
        in_specs=[VMEM] * 5,
        out_specs=VMEM,
        scratch_shapes=[pltpu.VMEM((BLK, BLK), BF16)],
        compiler_params=params(12),
        name="norm",
    )(*operands)


def multiply_kernel(*refs):
    *folded, held_ref, u_ref, root_ref = refs
    unfold_root(folded, root_ref)
    for part in chunks(u_ref.shape[1], BLK):
        u_ref[:, part] = dot(root_ref[...], held_ref[:, part]).astype(BF16)


def multiply(folded, held):
    return pl.pallas_call(
        multiply_kernel,
        out_shape=[pltpu.VMEM(held.shape, BF16), jax.ShapeDtypeStruct((BLK, BLK), BF16)],
        in_specs=[VMEM] * (len(folded) + 1),
        out_specs=[VMEM] * 2,
        input_output_aliases={len(folded): 0},
        compiler_params=params(12),
        cost_estimate=pl.CostEstimate(flops=1, bytes_accessed=1, transcendentals=0),
        name="multiply",
    )(*folded, held)


def finish_kernel(order, owner_slot, sums, *refs):
    refs = list(refs)
    take = lambda count: [refs.pop(0) for _ in range(count)]
    roots, folded, blocks = take(EARLY), take(2), take(QUAD)
    (update_ref, owned_ref), scaled, (late, empty, sent, stored) = take(2), take(QUAD), refs
    both = jnp.sum(sums[...], axis=1, keepdims=True)
    ratio = jnp.sqrt(both[:1] / (both[1:2] + 1e-06))
    columns = blocks[0].shape[1]
    waits = []

    def send(place, rows, columns):
        at = pl.multiple_of(order[place] * BLK + rows.start, rows.size)
        copy = pltpu.make_async_copy(
            scaled[place].at[rows, columns],
            update_ref.at[pl.ds(at, rows.size), columns],
            sent.at[len(waits)],
        )
        copy.start()
        waits.append(copy)

    def store(source, slot):
        return pltpu.make_async_copy(source, owned_ref.at[slot], stored.at[slot])

    def rescale(place, rows):
        scaled[place][rows] = (blocks[place][rows].astype(F32) * ratio).astype(BF16)

    bands = [(place, pl.ds(i, BAND)) for place in range(EARLY) for i in range(0, BLK, BAND)]
    products = [(place, part) for place in range(EARLY, QUAD) for part in chunks(columns, BLK)]
    rescale(*bands[0])
    send(*bands[0], pl.ds(0, columns))
    bands = bands[1:]
    empty[...] = jnp.zeros_like(empty)
    for place in range(EARLY, QUAD):
        unfold_root(folded, late.at[place - EARLY])
    for slot in range(SLOTS):
        mine = [owner_slot[order[QUAD], order[place]] == order[QUAD + 1] + slot for place in range(QUAD)]
        for place in range(QUAD):
            source = roots[place] if place < EARLY else late.at[place - EARLY]
            pl.when(mine[place])(store(source, slot).start)
        pl.when(jnp.logical_not(functools.reduce(jnp.logical_or, mine)))(store(empty, slot).start)
    for place, part in products:
        product = dot(late[place - EARLY], blocks[place][:, part])
        scaled[place][:, part] = (product * ratio).astype(BF16)
        band, bands = bands[:1], bands[1:]
        for one in band:
            rescale(*one)
            send(*one, pl.ds(0, columns))
        send(place, pl.ds(0, BLK), part)
    for one in bands:
        rescale(*one)
        send(*one, pl.ds(0, columns))
    for copy in waits:
        copy.wait()
    for slot in range(SLOTS):
        store(empty, slot).wait()


def finish(order, owner_slot, sums, roots, folded, blocks):
    columns = blocks[0].shape[1]
    pieces = EARLY * (BLK // BAND) + (QUAD - EARLY) * len(list(chunks(columns, BLK)))
    return pl.pallas_call(
        finish_kernel,
        out_shape=[
            jax.ShapeDtypeStruct((QUAD * BLK, columns), BF16),
            jax.ShapeDtypeStruct((SLOTS, BLK, BLK), BF16),
        ]
        + [pltpu.VMEM((BLK, columns), BF16)] * QUAD,
        in_specs=[SMEM] * 2 + [VMEM] * (3 + EARLY + QUAD),
        out_specs=[ANY] * 2 + [VMEM] * QUAD,
        input_output_aliases={5 + EARLY + place: 2 + place for place in range(QUAD)},
        scratch_shapes=[
            pltpu.VMEM((QUAD - EARLY, BLK, BLK), BF16),
            pltpu.VMEM((BLK, BLK), BF16),
            pltpu.SemaphoreType.DMA((pieces,)),
            pltpu.SemaphoreType.DMA((SLOTS,)),
        ],
        compiler_params=params(12),
        name="finish",
    )(order, owner_slot, sums, *roots, *folded, *blocks)[:2]


def swap(value, flip):
    axes = ("pool", "dp")
    count = math.prod(lax.axis_size(axis) for axis in axes)
    pairs = [(i, i ^ flip) for i in range(count)]
    return jax.tree.map(lambda part: lax.ppermute(part, axes, pairs), value)


def rounds():
    peer_bits = lax.axis_size("dp").bit_length() - 1
    bits = [1 << i for i in range(peer_bits + lax.axis_size("pool").bit_length() - 1)]
    pairs = [bits[i : min(i + 2, peer_bits)] for i in range(0, peer_bits, 2)]
    return [[bit] for bit in bits[peer_bits:][::-1]] + [pair + [sum(pair)] * (len(pair) - 1) for pair in pairs]


def add(*values):
    return sum(value.astype(F32) for value in values).astype(BF16)


def per_device(activations, gradient, owner_slot):
    peer_count = lax.axis_size("dp")
    my_index = lax.axis_index("dp")
    group_index = lax.axis_index("pool")
    tokens_all = activations.shape[0] * peer_count
    order = (my_index % QUAD) ^ jnp.arange(QUAD, dtype=jnp.int32)
    order = jnp.concatenate([order, jnp.stack([group_index, my_index * SLOTS])])

    a, b, c, d = statistics(order, activations)
    b, c, d = swap(b, 1), swap(c, 2), swap(d, 3)
    blocks, grams, squares = gram(order, gradient, a)
    grams = list(grams)
    mine = [add(a[rows], b[rows], c[rows], part) for rows, part in zip((slice(HALF), slice(HALF, None)), d)]
    flip = QUAD
    other = swap(mine, flip)
    while 2 * flip < peer_count:
        mine = [add(*parts) for parts in zip(mine, other)]
        flip *= 2
        other = swap(mine, flip)

    across = swap(grams[3], 1)
    across, grams[1] = lax.optimization_barrier((across, grams[1]))
    from_y = swap(grams[1], 1)
    from_z = swap(add(grams[2], across), 2)
    root, *halves = newton(tokens_all, squares, mine, other)
    from_c = swap(halves, 2)
    folded = [[root], [swap(root, 1)], from_c, swap(from_c, 1)]
    blocks, roots = list(blocks), []

    def precondition(place):
        blocks[place], root = multiply(folded[place], blocks[place])
        roots.append(root)

    sums = norm(root, grams[0], from_y, from_z, squares)
    early, arrivals = {0:[0],2:[1],3:[2]}, {2:[1,2],3:[3]}
    for step, flips in enumerate(rounds()):
        received = [swap(sums, flip) for flip in flips]
        for place in early.get(step, ()):
            precondition(place)
            blocks[place], *received = lax.optimization_barrier((blocks[place], *received))
        for place in arrivals.get(step, ()):
            folded[place], *received = lax.optimization_barrier((folded[place], *received))
        sums = sums + sum(received)
    update, owned = finish(order, owner_slot, sums, roots, folded[-1], blocks)
    return (update, owned[None])


def solution(mesh):
    in_specs = (P("dp", "pool"), P("pool", "dp"), P())
    out_specs = (P("pool", "dp"), P("pool", "dp", None, None))
    return jax.shard_map(
        per_device, mesh=mesh, in_specs=in_specs, out_specs=out_specs, check_vma=False
    )
```

```python
import functools
import math

import jax
import jax.numpy as jnp
from jax import lax
from jax.experimental import pallas as pl
from jax.experimental.pallas import tpu as pltpu
from jax.sharding import PartitionSpec as P

BLK = 512
HALF = BLK // 2
FOLD = BLK + 16
ITERS = 3
SLOTS = 2
QUAD = 4
EARLY = 3
BAND = 128
ROWS = 8
LANES = 128

damping = 0.01
F32 = jnp.float32
BF16 = jnp.bfloat16
SMEM = pl.BlockSpec(memory_space=pltpu.SMEM)
VMEM = pl.BlockSpec(memory_space=pltpu.VMEM)
ANY = pl.BlockSpec(memory_space=pl.ANY)


def params(mib):
    return pltpu.CompilerParams(vmem_limit_bytes=mib * 2**20)


def dot(left, right, dims=((1,), (0,))):
    return lax.dot_general(left, right, (dims, ((), ())), preferred_element_type=F32)


def places():
    row = lax.broadcasted_iota(jnp.int32, (HALF, HALF), 0)
    col = lax.broadcasted_iota(jnp.int32, (HALF, HALF), 1)
    return row, col


def fold(first, last):
    row, col = places()
    body = jnp.where(row <= col, first, last)
    diagonal = jnp.sum(jnp.where(row == col, last, 0.0), axis=0, keepdims=True)
    return body, jnp.broadcast_to(diagonal, (FOLD - BLK, HALF))


def unfold(body, diagonal):
    row, col = places()
    turned = body.T
    first = jnp.where(row <= col, body, turned)
    last = jnp.where(row > col, body, jnp.where(row < col, turned, diagonal))
    return first, last


def stat_kernel(order, x_ref, *out):
    for place in (1, 2, 3, 0):
        start = pl.multiple_of(order[place] * BLK, BLK)
        left = x_ref[:, pl.ds(start, HALF)]
        right = x_ref[:, pl.ds(pl.multiple_of(start + HALF, HALF), HALF)]
        along = ((0,), (0,))
        out[place][:HALF] = dot(left, right, along).astype(BF16)
        body, diagonal = fold(dot(left, left, along), dot(right, right, along))
        out[place][HALF:BLK] = body.astype(BF16)
        out[place][BLK:] = diagonal.astype(BF16)


def statistics(order, activations):
    return pl.pallas_call(
        stat_kernel,
        out_shape=[jax.ShapeDtypeStruct((FOLD, HALF), BF16)] * QUAD,
        in_specs=[SMEM, VMEM],
        out_specs=[VMEM] * QUAD,
        compiler_params=params(12),
        name="statistics",
    )(order, activations)


def chunks(width, size):
    start = 0
    while width - start >= 2 * size:
        yield pl.ds(start, size)
        start += size
    yield pl.ds(start, width - start)


def gram_kernel(order, after, g_ref, *refs):
    held, folded = refs[:QUAD], refs[QUAD : 2 * QUAD]
    norm_ref, left, last, arrived = refs[2 * QUAD :]
    parts = list(chunks(g_ref.shape[1], 1792))

    def copy(place, index):
        rows = pl.ds(pl.multiple_of(order[place] * BLK, BLK), BLK)
        return pltpu.make_async_copy(
            g_ref.at[rows, parts[index]], held[place].at[:, parts[index]], arrived.at[place, index]
        )

    for place in range(QUAD):
        for index in range(len(parts)):
            copy(place, index).start()
    norm_ref[...] = jnp.zeros_like(norm_ref)
    row, col = places()
    for place in range(QUAD):
        for index in range(len(parts)):
            copy(place, index).wait()
        whole = held[place][...]
        across = ((1,), (1,))
        left[...] = dot(whole, whole[:HALF], across)
        last[...] = dot(whole[HALF:], whole[HALF:], across)
        squares = jnp.where(row == col, left[:HALF] + last[...], 0.0)
        norm_ref[...] += jnp.sum(squares, axis=0, keepdims=True)
        body, diagonal = fold(left[:HALF], last[...])
        folded[place][:HALF] = left[HALF:].astype(BF16)
        folded[place][HALF:BLK] = body.astype(BF16)
        folded[place][BLK:] = diagonal.astype(BF16)


def gram(order, gradient, after):
    rows, columns = gradient.shape
    parts = len(list(chunks(columns, 1792)))
    results = pl.pallas_call(
        gram_kernel,
        out_shape=[pltpu.VMEM((BLK, columns), BF16)] * QUAD
        + [jax.ShapeDtypeStruct((FOLD, HALF), BF16)] * QUAD
        + [jax.ShapeDtypeStruct((1, HALF), F32)],
        in_specs=[SMEM, ANY, ANY],
        out_specs=[VMEM] * (2 * QUAD + 1),
        scratch_shapes=[
            pltpu.VMEM((BLK, HALF), F32),
            pltpu.VMEM((HALF, HALF), F32),
            pltpu.SemaphoreType.DMA((QUAD, parts)),
        ],
        compiler_params=params(12),
        cost_estimate=pl.CostEstimate(
            flops=2 * rows * columns * BLK, bytes_accessed=2 * rows * columns, transcendentals=0
        ),
        name="gram",
    )(order, after, pltpu.with_memory_space_constraint(gradient, pltpu.HBM))
    return results[:QUAD], results[QUAD : 2 * QUAD], results[-1]


def product(left, right):
    return dot(left.astype(BF16), right.astype(BF16))


def newton_kernel(tokens, after, mine, other, root, held):
    total = (mine[...].astype(F32) + other[...].astype(F32)) / tokens
    cross = total[:HALF]
    first, last = unfold(total[HALF:BLK], total[BLK : BLK + 1])
    held[:HALF, :HALF] = first
    held[:HALF, HALF:] = cross
    held[HALF:, :HALF] = cross.T
    held[HALF:, HALF:] = last
    row = lax.broadcasted_iota(jnp.int32, (BLK, BLK), 0)
    col = lax.broadcasted_iota(jnp.int32, (BLK, BLK), 1)
    identity = jnp.where(row == col, 1.0, 0.0).astype(F32)
    matrix = held[...] + damping * identity
    bound = jnp.max(jnp.sum(jnp.abs(matrix), axis=0, keepdims=True), axis=1, keepdims=True)
    scale = 2.0 / bound
    iterate = matrix * scale
    estimate = None
    for step in range(ITERS):
        error = (identity - iterate) * 0.25
        if estimate is None:
            estimate = error
        else:
            estimate = estimate + error + product(estimate, error)
        if step + 1 < ITERS:
            square = 2.0 * error + product(error, error)
            fourth = 2.0 * square + product(square, square)
            iterate = iterate + product(fourth, iterate)
    held[...] = (estimate + identity) * jnp.sqrt(jnp.sqrt(scale))
    root[:HALF] = held[:HALF, HALF:].astype(BF16)
    body, diagonal = fold(held[:HALF, :HALF], held[HALF:, HALF:])
    root[HALF:BLK] = body.astype(BF16)
    root[BLK:] = diagonal.astype(BF16)


def newton(tokens, after, mine, other):
    return pl.pallas_call(
        functools.partial(newton_kernel, tokens),
        out_shape=jax.ShapeDtypeStruct((FOLD, HALF), BF16),
        in_specs=[ANY, VMEM, VMEM],
        out_specs=VMEM,
        scratch_shapes=[pltpu.VMEM((BLK, BLK), F32)],
        compiler_params=params(12),
        cost_estimate=pl.CostEstimate(
            flops=16 * BLK**3, bytes_accessed=8 * BLK * BLK, transcendentals=0
        ),
        name="newton",
    )(after, mine, other)


def unfold_root(folded, root_ref):
    cross = folded[:HALF]
    rest = folded[HALF:].astype(F32)
    first, last = unfold(rest[:HALF], rest[HALF : HALF + 1])
    root_ref[:HALF, :HALF] = first.astype(BF16)
    root_ref[:HALF, HALF:] = cross
    root_ref[HALF:, :HALF] = cross.astype(F32).T.astype(BF16)
    root_ref[HALF:, HALF:] = last.astype(BF16)


def norm_kernel(folded, mine, from_y, from_z, squares, total_ref, root):
    unfold_root(folded, root)
    grams = mine[...].astype(F32) + from_y[...].astype(F32) + from_z[...].astype(F32)
    first = dot(root[:HALF], root[:, :HALF])
    lower = dot(root[HALF:], root[...])
    cross, last = lower[:, :HALF], lower[:, HALF:]
    row, col = places()
    weights = jnp.where(row < col, 2.0 * first, jnp.where(row > col, 2.0 * last, first))
    terms = weights * grams[HALF:BLK] + 2.0 * cross * grams[:HALF]
    terms += jnp.where(row == col, last, 0.0) * grams[BLK : BLK + 1]
    lanes = lambda value: sum(value[:, i : i + LANES] for i in range(0, HALF, LANES))
    new = lanes(jnp.sum(terms, axis=0, keepdims=True))
    row = lax.broadcasted_iota(jnp.int32, total_ref.shape, 0)
    total_ref[...] = jnp.where(row == 0, lanes(squares[...]), jnp.where(row == 1, new, 0.0))


def norm(*operands):
    return pl.pallas_call(
        norm_kernel,
        out_shape=jax.ShapeDtypeStruct((ROWS, LANES), F32),
        in_specs=[VMEM] * 5,
        out_specs=VMEM,
        scratch_shapes=[pltpu.VMEM((BLK, BLK), BF16)],
        compiler_params=params(12),
        name="norm",
    )(*operands)


def multiply_kernel(after, folded, held_ref, u_ref, root_ref):
    unfold_root(folded, root_ref)
    for part in chunks(u_ref.shape[1], BLK):
        u_ref[:, part] = dot(root_ref[...], held_ref[:, part]).astype(BF16)


def multiply(folded, held, after):
    return pl.pallas_call(
        multiply_kernel,
        out_shape=[pltpu.VMEM(held.shape, BF16), jax.ShapeDtypeStruct((BLK, BLK), BF16)],
        in_specs=[ANY, VMEM, VMEM],
        out_specs=[VMEM] * 2,
        input_output_aliases={2: 0},
        compiler_params=params(12),
        cost_estimate=pl.CostEstimate(flops=1, bytes_accessed=1, transcendentals=0),
        name="multiply",
    )(after, folded, held)


def finish_kernel(order, owner_slot, sums, *refs):
    roots, folded, blocks = refs[:EARLY], refs[EARLY:QUAD], refs[QUAD : 2 * QUAD]
    update_ref, owned_ref = refs[2 * QUAD : 2 * QUAD + 2]
    scaled = refs[2 * QUAD + 2 : 3 * QUAD + 2]
    late, empty, sent, stored = refs[3 * QUAD + 2 :]
    both = jnp.sum(sums[...], axis=1, keepdims=True)
    ratio = jnp.sqrt(both[:1] / (both[1:2] + 1e-06))
    columns = blocks[0].shape[1]
    waits = []

    def send(place, rows, columns):
        at = pl.multiple_of(order[place] * BLK + rows.start, rows.size)
        copy = pltpu.make_async_copy(
            scaled[place].at[rows, columns],
            update_ref.at[pl.ds(at, rows.size), columns],
            sent.at[len(waits)],
        )
        copy.start()
        waits.append(copy)

    def store(source, slot):
        return pltpu.make_async_copy(source, owned_ref.at[slot], stored.at[slot])

    def rescale(place, rows):
        scaled[place][rows] = (blocks[place][rows].astype(F32) * ratio).astype(BF16)

    bands = [(place, pl.ds(i, BAND)) for place in range(EARLY) for i in range(0, BLK, BAND)]
    products = [(place, part) for place in range(EARLY, QUAD) for part in chunks(columns, BLK)]
    ahead = len(bands) - len(products) // 2
    for one in bands[:ahead]:
        rescale(*one)
        send(*one, pl.ds(0, columns))
    bands = bands[ahead:]
    empty[...] = jnp.zeros_like(empty)
    for place in range(EARLY, QUAD):
        unfold_root(folded[place - EARLY], late.at[place - EARLY])
    for slot in range(SLOTS):
        mine = [owner_slot[order[QUAD], order[place]] == order[QUAD + 1] + slot for place in range(QUAD)]
        for place in range(QUAD):
            source = roots[place] if place < EARLY else late.at[place - EARLY]
            pl.when(mine[place])(store(source, slot).start)
        pl.when(jnp.logical_not(functools.reduce(jnp.logical_or, mine)))(store(empty, slot).start)
    for place, part in products:
        product = dot(late[place - EARLY], blocks[place][:, part])
        scaled[place][:, part] = (product * ratio).astype(BF16)
        band, bands = bands[:1], bands[1:]
        for one in band:
            rescale(*one)
            send(*one, pl.ds(0, columns))
        send(place, pl.ds(0, BLK), part)
    for one in bands:
        rescale(*one)
        send(*one, pl.ds(0, columns))
    for copy in waits:
        copy.wait()
    for slot in range(SLOTS):
        store(empty, slot).wait()


def finish(order, owner_slot, sums, roots, folded, blocks):
    columns = blocks[0].shape[1]
    pieces = EARLY * (BLK // BAND) + (QUAD - EARLY) * len(list(chunks(columns, BLK)))
    return pl.pallas_call(
        finish_kernel,
        out_shape=[
            jax.ShapeDtypeStruct((QUAD * BLK, columns), BF16),
            jax.ShapeDtypeStruct((SLOTS, BLK, BLK), BF16),
        ]
        + [pltpu.VMEM((BLK, columns), BF16)] * QUAD,
        in_specs=[SMEM] * 2 + [VMEM] * (1 + 2 * QUAD),
        out_specs=[ANY] * 2 + [VMEM] * QUAD,
        input_output_aliases={3 + QUAD + place: 2 + place for place in range(QUAD)},
        scratch_shapes=[
            pltpu.VMEM((QUAD - EARLY, BLK, BLK), BF16),
            pltpu.VMEM((BLK, BLK), BF16),
            pltpu.SemaphoreType.DMA((pieces,)),
            pltpu.SemaphoreType.DMA((SLOTS,)),
        ],
        compiler_params=params(12),
        name="finish",
    )(order, owner_slot, sums, *roots, *folded, *blocks)[:2]


def swap(value, flip):
    axes = ("pool", "dp")
    count = math.prod(lax.axis_size(axis) for axis in axes)
    return lax.ppermute(value, axes, [(i, i ^ flip) for i in range(count)])


def rounds():
    peer_bits = lax.axis_size("dp").bit_length() - 1
    bits = [1 << i for i in range(peer_bits + lax.axis_size("pool").bit_length() - 1)]
    return bits[peer_bits:][::-1] + bits[:peer_bits]


def add(*values):
    return sum(value.astype(F32) for value in values).astype(BF16)


def per_device(activations, gradient, owner_slot):
    peer_count = lax.axis_size("dp")
    my_index = lax.axis_index("dp")
    group_index = lax.axis_index("pool")
    tokens_all = activations.shape[0] * peer_count
    order = (my_index % QUAD) ^ jnp.arange(QUAD, dtype=jnp.int32)
    order = jnp.concatenate([order, jnp.stack([group_index, my_index * SLOTS])])

    a, b, c, d = statistics(order, activations)
    b, c, d = swap(b, 1), swap(c, 2), swap(d, 3)
    blocks, grams, squares = gram(order, gradient, a)
    mine = add(a, b, c, d)
    flip = QUAD
    other = swap(mine, flip)
    grams = list(grams)
    while 2 * flip < peer_count:
        mine = add(mine, other)
        flip *= 2
        other = swap(mine, flip)

    across = swap(grams[3], 1)
    across, grams[1] = lax.optimization_barrier((across, grams[1]))
    from_y = swap(grams[1], 1)
    from_z = swap(add(grams[2], across), 2)
    root = newton(tokens_all, squares, mine, other)
    folded = [root, swap(root, 1), swap(root, 2), swap(root, 3)]
    blocks, roots = list(blocks), []

    def precondition(place):
        blocks[place], root = multiply(folded[place], blocks[place], folded[place])
        roots.append(root)

    sums = norm(root, grams[0], from_y, from_z, squares)
    early, arrivals = {0:[0],3:[1],4:[2]}, {3:[1,2],4:[3]}
    for step, flip in enumerate(rounds()):
        received = swap(sums, flip)
        for place in early.get(step, ()):
            precondition(place)
            blocks[place], received = lax.optimization_barrier((blocks[place], received))
        for place in arrivals.get(step, ()):
            folded[place], received = lax.optimization_barrier((folded[place], received))
        sums = sums + received
    update, owned = finish(order, owner_slot, sums, roots, folded[EARLY:], blocks)
    return (update, owned[None])


def solution(mesh):
    in_specs = (P("dp", "pool"), P("pool", "dp"), P())
    out_specs = (P("pool", "dp"), P("pool", "dp", None, None))
    return jax.shard_map(
        per_device, mesh=mesh, in_specs=in_specs, out_specs=out_specs, check_vma=False
    )
```

```python
import functools
import math

import jax
import jax.numpy as jnp
from jax import lax
from jax.experimental import pallas as pl
from jax.experimental.pallas import tpu as pltpu
from jax.sharding import PartitionSpec as P

BLK = 512
HALF = BLK // 2
FOLD = BLK + 16
ITERS = 3
SLOTS = 2
QUAD = 4
EARLY = 3
BAND = 128
ROWS = 8
LANES = 128

damping = 0.01
F32 = jnp.float32
BF16 = jnp.bfloat16
SMEM = pl.BlockSpec(memory_space=pltpu.SMEM)
VMEM = pl.BlockSpec(memory_space=pltpu.VMEM)
ANY = pl.BlockSpec(memory_space=pl.ANY)


def params(mib):
    return pltpu.CompilerParams(vmem_limit_bytes=mib * 2**20)


def dot(left, right, dims=((1,), (0,))):
    return lax.dot_general(left, right, (dims, ((), ())), preferred_element_type=F32)


def places():
    row = lax.broadcasted_iota(jnp.int32, (HALF, HALF), 0)
    col = lax.broadcasted_iota(jnp.int32, (HALF, HALF), 1)
    return row, col


def fold(first, last):
    row, col = places()
    body = jnp.where(row <= col, first, last)
    diagonal = jnp.sum(jnp.where(row == col, last, 0.0), axis=0, keepdims=True)
    return body, jnp.broadcast_to(diagonal, (FOLD - BLK, HALF))


def unfold(body, diagonal):
    row, col = places()
    turned = body.T
    first = jnp.where(row <= col, body, turned)
    last = jnp.where(row > col, body, jnp.where(row < col, turned, diagonal))
    return first, last


def stat_kernel(order, x_ref, *out):
    for place in (1, 2, 3, 0):
        start = pl.multiple_of(order[place] * BLK, BLK)
        left = x_ref[:, pl.ds(start, HALF)]
        right = x_ref[:, pl.ds(pl.multiple_of(start + HALF, HALF), HALF)]
        along = ((0,), (0,))
        out[place][:HALF] = dot(left, right, along).astype(BF16)
        body, diagonal = fold(dot(left, left, along), dot(right, right, along))
        out[place][HALF:BLK] = body.astype(BF16)
        out[place][BLK:] = diagonal.astype(BF16)


def statistics(order, activations):
    return pl.pallas_call(
        stat_kernel,
        out_shape=[jax.ShapeDtypeStruct((FOLD, HALF), BF16)] * QUAD,
        in_specs=[SMEM, VMEM],
        out_specs=[VMEM] * QUAD,
        compiler_params=params(12),
        name="statistics",
    )(order, activations)


def chunks(width, size):
    start = 0
    while width - start >= 2 * size:
        yield pl.ds(start, size)
        start += size
    yield pl.ds(start, width - start)


def gram_kernel(order, after, g_ref, *refs):
    held, folded = refs[:QUAD], refs[QUAD : 2 * QUAD]
    norm_ref, left, last, arrived = refs[2 * QUAD :]
    parts = list(chunks(g_ref.shape[1], 1792))

    def copy(place, index):
        rows = pl.ds(pl.multiple_of(order[place] * BLK, BLK), BLK)
        return pltpu.make_async_copy(
            g_ref.at[rows, parts[index]], held[place].at[:, parts[index]], arrived.at[place, index]
        )

    for place in range(QUAD):
        for index in range(len(parts)):
            copy(place, index).start()
    norm_ref[...] = jnp.zeros_like(norm_ref)
    row, col = places()
    for place in range(QUAD):
        for index in range(len(parts)):
            copy(place, index).wait()
        whole = held[place][...]
        across = ((1,), (1,))
        left[...] = dot(whole, whole[:HALF], across)
        last[...] = dot(whole[HALF:], whole[HALF:], across)
        squares = jnp.where(row == col, left[:HALF] + last[...], 0.0)
        norm_ref[...] += jnp.sum(squares, axis=0, keepdims=True)
        body, diagonal = fold(left[:HALF], last[...])
        folded[place][:HALF] = left[HALF:].astype(BF16)
        folded[place][HALF:BLK] = body.astype(BF16)
        folded[place][BLK:] = diagonal.astype(BF16)


def gram(order, gradient, after):
    rows, columns = gradient.shape
    parts = len(list(chunks(columns, 1792)))
    results = pl.pallas_call(
        gram_kernel,
        out_shape=[pltpu.VMEM((BLK, columns), BF16)] * QUAD
        + [jax.ShapeDtypeStruct((FOLD, HALF), BF16)] * QUAD
        + [jax.ShapeDtypeStruct((1, HALF), F32)],
        in_specs=[SMEM, ANY, ANY],
        out_specs=[VMEM] * (2 * QUAD + 1),
        scratch_shapes=[
            pltpu.VMEM((BLK, HALF), F32),
            pltpu.VMEM((HALF, HALF), F32),
            pltpu.SemaphoreType.DMA((QUAD, parts)),
        ],
        compiler_params=params(12),
        cost_estimate=pl.CostEstimate(
            flops=2 * rows * columns * BLK, bytes_accessed=2 * rows * columns, transcendentals=0
        ),
        name="gram",
    )(order, after, pltpu.with_memory_space_constraint(gradient, pltpu.HBM))
    return results[:QUAD], results[QUAD : 2 * QUAD], results[-1]


def product(left, right):
    return dot(left.astype(BF16), right.astype(BF16))


def newton_kernel(tokens, after, mine, other, root, held):
    total = (mine[...].astype(F32) + other[...].astype(F32)) / tokens
    cross = total[:HALF]
    first, last = unfold(total[HALF:BLK], total[BLK : BLK + 1])
    held[:HALF, :HALF] = first
    held[:HALF, HALF:] = cross
    held[HALF:, :HALF] = cross.T
    held[HALF:, HALF:] = last
    row = lax.broadcasted_iota(jnp.int32, (BLK, BLK), 0)
    col = lax.broadcasted_iota(jnp.int32, (BLK, BLK), 1)
    identity = jnp.where(row == col, 1.0, 0.0).astype(F32)
    matrix = held[...] + damping * identity
    bound = jnp.max(jnp.sum(jnp.abs(matrix), axis=0, keepdims=True), axis=1, keepdims=True)
    scale = 2.0 / bound
    iterate = matrix * scale
    estimate = None
    for step in range(ITERS):
        error = (identity - iterate) * 0.25
        if estimate is None:
            estimate = error
        else:
            estimate = estimate + error + product(estimate, error)
        if step + 1 < ITERS:
            square = 2.0 * error + product(error, error)
            fourth = 2.0 * square + product(square, square)
            iterate = iterate + product(fourth, iterate)
    held[...] = (estimate + identity) * jnp.sqrt(jnp.sqrt(scale))
    root[:HALF] = held[:HALF, HALF:].astype(BF16)
    body, diagonal = fold(held[:HALF, :HALF], held[HALF:, HALF:])
    root[HALF:BLK] = body.astype(BF16)
    root[BLK:] = diagonal.astype(BF16)


def newton(tokens, after, mine, other):
    return pl.pallas_call(
        functools.partial(newton_kernel, tokens),
        out_shape=jax.ShapeDtypeStruct((FOLD, HALF), BF16),
        in_specs=[ANY, VMEM, VMEM],
        out_specs=VMEM,
        scratch_shapes=[pltpu.VMEM((BLK, BLK), F32)],
        compiler_params=params(12),
        cost_estimate=pl.CostEstimate(
            flops=16 * BLK**3, bytes_accessed=8 * BLK * BLK, transcendentals=0
        ),
        name="newton",
    )(after, mine, other)


def unfold_root(folded, root_ref):
    cross = folded[:HALF]
    rest = folded[HALF:].astype(F32)
    first, last = unfold(rest[:HALF], rest[HALF : HALF + 1])
    root_ref[:HALF, :HALF] = first.astype(BF16)
    root_ref[:HALF, HALF:] = cross
    root_ref[HALF:, :HALF] = cross.astype(F32).T.astype(BF16)
    root_ref[HALF:, HALF:] = last.astype(BF16)


def norm_kernel(folded, mine, from_y, from_z, squares, total_ref, root):
    unfold_root(folded, root)
    grams = mine[...].astype(F32) + from_y[...].astype(F32) + from_z[...].astype(F32)
    first = dot(root[:HALF], root[:, :HALF])
    lower = dot(root[HALF:], root[...])
    cross, last = lower[:, :HALF], lower[:, HALF:]
    row, col = places()
    weights = jnp.where(row < col, 2.0 * first, jnp.where(row > col, 2.0 * last, first))
    terms = weights * grams[HALF:BLK] + 2.0 * cross * grams[:HALF]
    terms += jnp.where(row == col, last, 0.0) * grams[BLK : BLK + 1]
    lanes = lambda value: sum(value[:, i : i + LANES] for i in range(0, HALF, LANES))
    new = lanes(jnp.sum(terms, axis=0, keepdims=True))
    row = lax.broadcasted_iota(jnp.int32, total_ref.shape, 0)
    total_ref[...] = jnp.where(row == 0, lanes(squares[...]), jnp.where(row == 1, new, 0.0))


def norm(*operands):
    return pl.pallas_call(
        norm_kernel,
        out_shape=jax.ShapeDtypeStruct((ROWS, LANES), F32),
        in_specs=[VMEM] * 5,
        out_specs=VMEM,
        scratch_shapes=[pltpu.VMEM((BLK, BLK), BF16)],
        compiler_params=params(12),
        name="norm",
    )(*operands)


def multiply_kernel(after, folded, held_ref, u_ref, root_ref):
    unfold_root(folded, root_ref)
    for part in chunks(u_ref.shape[1], BLK):
        u_ref[:, part] = dot(root_ref[...], held_ref[:, part]).astype(BF16)


def multiply(folded, held, after):
    return pl.pallas_call(
        multiply_kernel,
        out_shape=[pltpu.VMEM(held.shape, BF16), jax.ShapeDtypeStruct((BLK, BLK), BF16)],
        in_specs=[ANY, VMEM, VMEM],
        out_specs=[VMEM] * 2,
        input_output_aliases={2: 0},
        compiler_params=params(12),
        cost_estimate=pl.CostEstimate(flops=1, bytes_accessed=1, transcendentals=0),
        name="multiply",
    )(after, folded, held)


def finish_kernel(order, owner_slot, sums, *refs):
    roots, folded, blocks = refs[:EARLY], refs[EARLY:QUAD], refs[QUAD : 2 * QUAD]
    update_ref, owned_ref = refs[2 * QUAD : 2 * QUAD + 2]
    scaled = refs[2 * QUAD + 2 : 3 * QUAD + 2]
    late, empty, sent, stored = refs[3 * QUAD + 2 :]
    both = jnp.sum(sums[...], axis=1, keepdims=True)
    ratio = jnp.sqrt(both[:1] / (both[1:2] + 1e-06))
    columns = blocks[0].shape[1]
    waits = []

    def send(place, rows, columns):
        at = pl.multiple_of(order[place] * BLK + rows.start, rows.size)
        copy = pltpu.make_async_copy(
            scaled[place].at[rows, columns],
            update_ref.at[pl.ds(at, rows.size), columns],
            sent.at[len(waits)],
        )
        copy.start()
        waits.append(copy)

    def store(source, slot):
        return pltpu.make_async_copy(source, owned_ref.at[slot], stored.at[slot])

    def rescale(place, rows):
        scaled[place][rows] = (blocks[place][rows].astype(F32) * ratio).astype(BF16)

    bands = [(place, pl.ds(i, BAND)) for place in range(EARLY) for i in range(0, BLK, BAND)]
    products = [(place, part) for place in range(EARLY, QUAD) for part in chunks(columns, BLK)]
    ahead = 1
    for one in bands[:ahead]:
        rescale(*one)
        send(*one, pl.ds(0, columns))
    bands = bands[ahead:]
    empty[...] = jnp.zeros_like(empty)
    for place in range(EARLY, QUAD):
        unfold_root(folded[place - EARLY], late.at[place - EARLY])
    for slot in range(SLOTS):
        mine = [owner_slot[order[QUAD], order[place]] == order[QUAD + 1] + slot for place in range(QUAD)]
        for place in range(QUAD):
            source = roots[place] if place < EARLY else late.at[place - EARLY]
            pl.when(mine[place])(store(source, slot).start)
        pl.when(jnp.logical_not(functools.reduce(jnp.logical_or, mine)))(store(empty, slot).start)
    for place, part in products:
        product = dot(late[place - EARLY], blocks[place][:, part])
        scaled[place][:, part] = (product * ratio).astype(BF16)
        band, bands = bands[:1], bands[1:]
        for one in band:
            rescale(*one)
            send(*one, pl.ds(0, columns))
        send(place, pl.ds(0, BLK), part)
    for one in bands:
        rescale(*one)
        send(*one, pl.ds(0, columns))
    for copy in waits:
        copy.wait()
    for slot in range(SLOTS):
        store(empty, slot).wait()


def finish(order, owner_slot, sums, roots, folded, blocks):
    columns = blocks[0].shape[1]
    pieces = EARLY * (BLK // BAND) + (QUAD - EARLY) * len(list(chunks(columns, BLK)))
    return pl.pallas_call(
        finish_kernel,
        out_shape=[
            jax.ShapeDtypeStruct((QUAD * BLK, columns), BF16),
            jax.ShapeDtypeStruct((SLOTS, BLK, BLK), BF16),
        ]
        + [pltpu.VMEM((BLK, columns), BF16)] * QUAD,
        in_specs=[SMEM] * 2 + [VMEM] * (1 + 2 * QUAD),
        out_specs=[ANY] * 2 + [VMEM] * QUAD,
        input_output_aliases={3 + QUAD + place: 2 + place for place in range(QUAD)},
        scratch_shapes=[
            pltpu.VMEM((QUAD - EARLY, BLK, BLK), BF16),
            pltpu.VMEM((BLK, BLK), BF16),
            pltpu.SemaphoreType.DMA((pieces,)),
            pltpu.SemaphoreType.DMA((SLOTS,)),
        ],
        compiler_params=params(12),
        name="finish",
    )(order, owner_slot, sums, *roots, *folded, *blocks)[:2]


def swap(value, flip):
    axes = ("pool", "dp")
    count = math.prod(lax.axis_size(axis) for axis in axes)
    return lax.ppermute(value, axes, [(i, i ^ flip) for i in range(count)])


def rounds():
    peer_bits = lax.axis_size("dp").bit_length() - 1
    bits = [1 << i for i in range(peer_bits + lax.axis_size("pool").bit_length() - 1)]
    return bits[peer_bits:][::-1] + bits[:peer_bits]


def add(*values):
    return sum(value.astype(F32) for value in values).astype(BF16)


def per_device(activations, gradient, owner_slot):
    peer_count = lax.axis_size("dp")
    my_index = lax.axis_index("dp")
    group_index = lax.axis_index("pool")
    tokens_all = activations.shape[0] * peer_count
    order = (my_index % QUAD) ^ jnp.arange(QUAD, dtype=jnp.int32)
    order = jnp.concatenate([order, jnp.stack([group_index, my_index * SLOTS])])

    a, b, c, d = statistics(order, activations)
    b, c, d = swap(b, 1), swap(c, 2), swap(d, 3)
    blocks, grams, squares = gram(order, gradient, a)
    mine = add(a, b, c, d)
    flip = QUAD
    other = swap(mine, flip)
    grams = list(grams)
    while 2 * flip < peer_count:
        mine = add(mine, other)
        flip *= 2
        other = swap(mine, flip)

    across = swap(grams[3], 1)
    across, grams[1] = lax.optimization_barrier((across, grams[1]))
    from_y = swap(grams[1], 1)
    from_z = swap(add(grams[2], across), 2)
    root = newton(tokens_all, squares, mine, other)
    folded = [root, swap(root, 1), swap(root, 2)]
    blocks, roots = list(blocks), []

    def precondition(place):
        blocks[place], root = multiply(folded[place], blocks[place], folded[place])
        roots.append(root)

    sums = norm(root, grams[0], from_y, from_z, squares)
    early, arrivals = {0:[0],3:[1],4:[2]}, {2:[1,2],4:[3]}
    for step, flip in enumerate(rounds()):
        received = swap(sums, flip)
        if step == 3:
            folded[2], _ = lax.optimization_barrier((folded[2], sums))
            folded.append(swap(folded[2], 1))
        for place in early.get(step, ()):
            precondition(place)
            blocks[place], received = lax.optimization_barrier((blocks[place], received))
        for place in arrivals.get(step, ()):
            folded[place], received = lax.optimization_barrier((folded[place], received))
        sums = sums + received
    update, owned = finish(order, owner_slot, sums, roots, folded[EARLY:], blocks)
    return (update, owned[None])


def solution(mesh):
    in_specs = (P("dp", "pool"), P("pool", "dp"), P())
    out_specs = (P("pool", "dp"), P("pool", "dp", None, None))
    return jax.shard_map(
        per_device, mesh=mesh, in_specs=in_specs, out_specs=out_specs, check_vma=False
    )
```

```python
import functools
import math

import jax
import jax.numpy as jnp
from jax import lax
from jax.experimental import pallas as pl
from jax.experimental.pallas import tpu as pltpu
from jax.sharding import PartitionSpec as P

BLK = 512
HALF = BLK // 2
FOLD = BLK + 16
ITERS = 3
SLOTS = 2
QUAD = 4
EARLY = 3
BAND = 128
ROWS = 8
LANES = 128

damping = 0.01
F32 = jnp.float32
BF16 = jnp.bfloat16
SMEM = pl.BlockSpec(memory_space=pltpu.SMEM)
VMEM = pl.BlockSpec(memory_space=pltpu.VMEM)
ANY = pl.BlockSpec(memory_space=pl.ANY)


def params(mib):
    return pltpu.CompilerParams(vmem_limit_bytes=mib * 2**20)


def dot(left, right, dims=((1,), (0,))):
    return lax.dot_general(left, right, (dims, ((), ())), preferred_element_type=F32)


def places():
    row = lax.broadcasted_iota(jnp.int32, (HALF, HALF), 0)
    col = lax.broadcasted_iota(jnp.int32, (HALF, HALF), 1)
    return row, col


def fold(first, last):
    row, col = places()
    body = jnp.where(row <= col, first, last)
    diagonal = jnp.sum(jnp.where(row == col, last, 0.0), axis=0, keepdims=True)
    return body, jnp.broadcast_to(diagonal, (FOLD - BLK, HALF))


def unfold(body, diagonal):
    row, col = places()
    turned = body.T
    first = jnp.where(row <= col, body, turned)
    last = jnp.where(row > col, body, jnp.where(row < col, turned, diagonal))
    return first, last


def stat_kernel(order, x_ref, *out):
    for place in (1, 2, 3, 0):
        start = pl.multiple_of(order[place] * BLK, BLK)
        left = x_ref[:, pl.ds(start, HALF)]
        right = x_ref[:, pl.ds(pl.multiple_of(start + HALF, HALF), HALF)]
        along = ((0,), (0,))
        out[place][:HALF] = dot(left, right, along).astype(BF16)
        body, diagonal = fold(dot(left, left, along), dot(right, right, along))
        out[place][HALF:BLK] = body.astype(BF16)
        out[place][BLK:] = diagonal.astype(BF16)


def statistics(order, activations):
    return pl.pallas_call(
        stat_kernel,
        out_shape=[jax.ShapeDtypeStruct((FOLD, HALF), BF16)] * QUAD,
        in_specs=[SMEM, VMEM],
        out_specs=[VMEM] * QUAD,
        compiler_params=params(12),
        name="statistics",
    )(order, activations)


def chunks(width, size):
    start = 0
    while width - start >= 2 * size:
        yield pl.ds(start, size)
        start += size
    yield pl.ds(start, width - start)


def gram_kernel(order, after, g_ref, *refs):
    held, folded = refs[:QUAD], refs[QUAD : 2 * QUAD]
    norm_ref, left, last, arrived = refs[2 * QUAD :]
    parts = list(chunks(g_ref.shape[1], 1792))

    def copy(place, index):
        rows = pl.ds(pl.multiple_of(order[place] * BLK, BLK), BLK)
        return pltpu.make_async_copy(
            g_ref.at[rows, parts[index]], held[place].at[:, parts[index]], arrived.at[place, index]
        )

    for place in range(QUAD):
        for index in range(len(parts)):
            copy(place, index).start()
    norm_ref[...] = jnp.zeros_like(norm_ref)
    row, col = places()
    for place in range(QUAD):
        for index in range(len(parts)):
            copy(place, index).wait()
        whole = held[place][...]
        across = ((1,), (1,))
        left[...] = dot(whole, whole[:HALF], across)
        last[...] = dot(whole[HALF:], whole[HALF:], across)
        squares = jnp.where(row == col, left[:HALF] + last[...], 0.0)
        norm_ref[...] += jnp.sum(squares, axis=0, keepdims=True)
        body, diagonal = fold(left[:HALF], last[...])
        folded[place][:HALF] = left[HALF:].astype(BF16)
        folded[place][HALF:BLK] = body.astype(BF16)
        folded[place][BLK:] = diagonal.astype(BF16)


def gram(order, gradient, after):
    rows, columns = gradient.shape
    parts = len(list(chunks(columns, 1792)))
    results = pl.pallas_call(
        gram_kernel,
        out_shape=[pltpu.VMEM((BLK, columns), BF16)] * QUAD
        + [jax.ShapeDtypeStruct((FOLD, HALF), BF16)] * QUAD
        + [jax.ShapeDtypeStruct((1, HALF), F32)],
        in_specs=[SMEM, ANY, ANY],
        out_specs=[VMEM] * (2 * QUAD + 1),
        scratch_shapes=[
            pltpu.VMEM((BLK, HALF), F32),
            pltpu.VMEM((HALF, HALF), F32),
            pltpu.SemaphoreType.DMA((QUAD, parts)),
        ],
        compiler_params=params(12),
        cost_estimate=pl.CostEstimate(
            flops=2 * rows * columns * BLK, bytes_accessed=2 * rows * columns, transcendentals=0
        ),
        name="gram",
    )(order, after, pltpu.with_memory_space_constraint(gradient, pltpu.HBM))
    return results[:QUAD], results[QUAD : 2 * QUAD], results[-1]


def product(left, right):
    return dot(left.astype(BF16), right.astype(BF16))


def newton_kernel(tokens, after, mine, other, root, held):
    total = (mine[...].astype(F32) + other[...].astype(F32)) / tokens
    cross = total[:HALF]
    first, last = unfold(total[HALF:BLK], total[BLK : BLK + 1])
    held[:HALF, :HALF] = first
    held[:HALF, HALF:] = cross
    held[HALF:, :HALF] = cross.T
    held[HALF:, HALF:] = last
    row = lax.broadcasted_iota(jnp.int32, (BLK, BLK), 0)
    col = lax.broadcasted_iota(jnp.int32, (BLK, BLK), 1)
    identity = jnp.where(row == col, 1.0, 0.0).astype(F32)
    matrix = held[...] + damping * identity
    bound = jnp.max(jnp.sum(jnp.abs(matrix), axis=0, keepdims=True), axis=1, keepdims=True)
    scale = 2.0 / bound
    iterate = matrix * scale
    estimate = None
    for step in range(ITERS):
        error = (identity - iterate) * 0.25
        if estimate is None:
            estimate = error
        else:
            estimate = estimate + error + product(estimate, error)
        if step + 1 < ITERS:
            square = 2.0 * error + product(error, error)
            fourth = 2.0 * square + product(square, square)
            iterate = iterate + product(fourth, iterate)
    held[...] = (estimate + identity) * jnp.sqrt(jnp.sqrt(scale))
    root[:HALF] = held[:HALF, HALF:].astype(BF16)
    body, diagonal = fold(held[:HALF, :HALF], held[HALF:, HALF:])
    root[HALF:BLK] = body.astype(BF16)
    root[BLK:] = diagonal.astype(BF16)


def newton(tokens, after, mine, other):
    return pl.pallas_call(
        functools.partial(newton_kernel, tokens),
        out_shape=jax.ShapeDtypeStruct((FOLD, HALF), BF16),
        in_specs=[ANY, VMEM, VMEM],
        out_specs=VMEM,
        scratch_shapes=[pltpu.VMEM((BLK, BLK), F32)],
        compiler_params=params(12),
        cost_estimate=pl.CostEstimate(
            flops=16 * BLK**3, bytes_accessed=8 * BLK * BLK, transcendentals=0
        ),
        name="newton",
    )(after, mine, other)


def unfold_root(folded, root_ref):
    cross = folded[:HALF]
    rest = folded[HALF:].astype(F32)
    first, last = unfold(rest[:HALF], rest[HALF : HALF + 1])
    root_ref[:HALF, :HALF] = first.astype(BF16)
    root_ref[:HALF, HALF:] = cross
    root_ref[HALF:, :HALF] = cross.astype(F32).T.astype(BF16)
    root_ref[HALF:, HALF:] = last.astype(BF16)


def norm_kernel(folded, mine, from_y, from_z, squares, total_ref, root):
    unfold_root(folded, root)
    grams = mine[...].astype(F32) + from_y[...].astype(F32) + from_z[...].astype(F32)
    first = dot(root[:HALF], root[:, :HALF])
    lower = dot(root[HALF:], root[...])
    cross, last = lower[:, :HALF], lower[:, HALF:]
    row, col = places()
    weights = jnp.where(row < col, 2.0 * first, jnp.where(row > col, 2.0 * last, first))
    terms = weights * grams[HALF:BLK] + 2.0 * cross * grams[:HALF]
    terms += jnp.where(row == col, last, 0.0) * grams[BLK : BLK + 1]
    lanes = lambda value: sum(value[:, i : i + LANES] for i in range(0, HALF, LANES))
    new = lanes(jnp.sum(terms, axis=0, keepdims=True))
    row = lax.broadcasted_iota(jnp.int32, total_ref.shape, 0)
    total_ref[...] = jnp.where(row == 0, lanes(squares[...]), jnp.where(row == 1, new, 0.0))


def norm(*operands):
    return pl.pallas_call(
        norm_kernel,
        out_shape=jax.ShapeDtypeStruct((ROWS, LANES), F32),
        in_specs=[VMEM] * 5,
        out_specs=VMEM,
        scratch_shapes=[pltpu.VMEM((BLK, BLK), BF16)],
        compiler_params=params(12),
        name="norm",
    )(*operands)


def multiply_kernel(after, folded, held_ref, u_ref, root_ref):
    unfold_root(folded, root_ref)
    for part in chunks(u_ref.shape[1], BLK):
        u_ref[:, part] = dot(root_ref[...], held_ref[:, part]).astype(BF16)


def multiply(folded, held, after):
    return pl.pallas_call(
        multiply_kernel,
        out_shape=[pltpu.VMEM(held.shape, BF16), jax.ShapeDtypeStruct((BLK, BLK), BF16)],
        in_specs=[ANY, VMEM, VMEM],
        out_specs=[VMEM] * 2,
        input_output_aliases={2: 0},
        compiler_params=params(12),
        cost_estimate=pl.CostEstimate(flops=1880000000, bytes_accessed=1, transcendentals=0),
        name="multiply",
    )(after, folded, held)


def finish_kernel(order, owner_slot, sums, *refs):
    roots, folded, blocks = refs[:EARLY], refs[EARLY:QUAD], refs[QUAD : 2 * QUAD]
    update_ref, owned_ref = refs[2 * QUAD : 2 * QUAD + 2]
    scaled = refs[2 * QUAD + 2 : 3 * QUAD + 2]
    late, empty, sent, stored = refs[3 * QUAD + 2 :]
    both = jnp.sum(sums[...], axis=1, keepdims=True)
    ratio = jnp.sqrt(both[:1] / (both[1:2] + 1e-06))
    columns = blocks[0].shape[1]
    waits = []

    def send(place, rows, columns):
        at = pl.multiple_of(order[place] * BLK + rows.start, rows.size)
        copy = pltpu.make_async_copy(
            scaled[place].at[rows, columns],
            update_ref.at[pl.ds(at, rows.size), columns],
            sent.at[len(waits)],
        )
        copy.start()
        waits.append(copy)

    def store(source, slot):
        return pltpu.make_async_copy(source, owned_ref.at[slot], stored.at[slot])

    def rescale(place, rows):
        scaled[place][rows] = (blocks[place][rows].astype(F32) * ratio).astype(BF16)

    bands = [(place, pl.ds(i, BAND)) for place in range(EARLY) for i in range(0, BLK, BAND)]
    products = [(place, part) for place in range(EARLY, QUAD) for part in chunks(columns, BLK)]
    ahead = 1
    for one in bands[:ahead]:
        rescale(*one)
        send(*one, pl.ds(0, columns))
    bands = bands[ahead:]
    empty[...] = jnp.zeros_like(empty)
    for place in range(EARLY, QUAD):
        unfold_root(folded[place - EARLY], late.at[place - EARLY])
    for slot in range(SLOTS):
        mine = [owner_slot[order[QUAD], order[place]] == order[QUAD + 1] + slot for place in range(QUAD)]
        for place in range(QUAD):
            source = roots[place] if place < EARLY else late.at[place - EARLY]
            pl.when(mine[place])(store(source, slot).start)
        pl.when(jnp.logical_not(functools.reduce(jnp.logical_or, mine)))(store(empty, slot).start)
    for place, part in products:
        product = dot(late[place - EARLY], blocks[place][:, part])
        scaled[place][:, part] = (product * ratio).astype(BF16)
        band, bands = bands[:1], bands[1:]
        for one in band:
            rescale(*one)
            send(*one, pl.ds(0, columns))
        send(place, pl.ds(0, BLK), part)
    for one in bands:
        rescale(*one)
        send(*one, pl.ds(0, columns))
    for copy in waits:
        copy.wait()
    for slot in range(SLOTS):
        store(empty, slot).wait()


def finish(order, owner_slot, sums, roots, folded, blocks):
    columns = blocks[0].shape[1]
    pieces = EARLY * (BLK // BAND) + (QUAD - EARLY) * len(list(chunks(columns, BLK)))
    return pl.pallas_call(
        finish_kernel,
        out_shape=[
            jax.ShapeDtypeStruct((QUAD * BLK, columns), BF16),
            jax.ShapeDtypeStruct((SLOTS, BLK, BLK), BF16),
        ]
        + [pltpu.VMEM((BLK, columns), BF16)] * QUAD,
        in_specs=[SMEM] * 2 + [VMEM] * (1 + 2 * QUAD),
        out_specs=[ANY] * 2 + [VMEM] * QUAD,
        input_output_aliases={3 + QUAD + place: 2 + place for place in range(QUAD)},
        scratch_shapes=[
            pltpu.VMEM((QUAD - EARLY, BLK, BLK), BF16),
            pltpu.VMEM((BLK, BLK), BF16),
            pltpu.SemaphoreType.DMA((pieces,)),
            pltpu.SemaphoreType.DMA((SLOTS,)),
        ],
        compiler_params=params(12),
        name="finish",
    )(order, owner_slot, sums, *roots, *folded, *blocks)[:2]


def swap(value, flip):
    axes = ("pool", "dp")
    count = math.prod(lax.axis_size(axis) for axis in axes)
    return lax.ppermute(value, axes, [(i, i ^ flip) for i in range(count)])


def rounds():
    peer_bits = lax.axis_size("dp").bit_length() - 1
    bits = [1 << i for i in range(peer_bits + lax.axis_size("pool").bit_length() - 1)]
    return bits[peer_bits:][::-1] + [bits[1], bits[0]] + bits[2:peer_bits]


def add(*values):
    return sum(value.astype(F32) for value in values).astype(BF16)


def per_device(activations, gradient, owner_slot):
    peer_count = lax.axis_size("dp")
    my_index = lax.axis_index("dp")
    group_index = lax.axis_index("pool")
    tokens_all = activations.shape[0] * peer_count
    order = (my_index % QUAD) ^ jnp.arange(QUAD, dtype=jnp.int32)
    order = jnp.concatenate([order, jnp.stack([group_index, my_index * SLOTS])])

    a, b, c, d = statistics(order, activations)
    b, c, d = swap(b, 1), swap(c, 2), swap(d, 3)
    blocks, grams, squares = gram(order, gradient, a)
    mine = add(a, b, c, d)
    flip = QUAD
    other = swap(mine, flip)
    grams = list(grams)
    while 2 * flip < peer_count:
        mine = add(mine, other)
        flip *= 2
        other = swap(mine, flip)

    across = swap(grams[3], 1)
    across, grams[1] = lax.optimization_barrier((across, grams[1]))
    from_y = swap(grams[1], 1)
    from_z = swap(add(grams[2], across), 2)
    root = newton(tokens_all, squares, mine, other)
    folded = [root, swap(root, 1), swap(root, 2)]
    blocks, roots = list(blocks), []

    def precondition(place):
        blocks[place], root = multiply(folded[place], blocks[place], folded[place])
        roots.append(root)

    sums = norm(root, grams[0], from_y, from_z, squares)
    early, arrivals = {2:[0],3:[1],4:[2]}, {2:[1,2],4:[3]}
    for step, flip in enumerate(rounds()):
        received = swap(sums, flip)
        if step == 3:
            folded[2], _ = lax.optimization_barrier((folded[2], sums))
            folded.append(swap(folded[2], 1))
        for place in early.get(step, ()):
            precondition(place)
            blocks[place], received = lax.optimization_barrier((blocks[place], received))
        for place in arrivals.get(step, ()):
            folded[place], received = lax.optimization_barrier((folded[place], received))
        sums = sums + received
    update, owned = finish(order, owner_slot, sums, roots, folded[EARLY:], blocks)
    return (update, owned[None])


def solution(mesh):
    in_specs = (P("dp", "pool"), P("pool", "dp"), P())
    out_specs = (P("pool", "dp"), P("pool", "dp", None, None))
    return jax.shard_map(
        per_device, mesh=mesh, in_specs=in_specs, out_specs=out_specs, check_vma=False
    )
```

```python
import functools
import math

import jax
import jax.numpy as jnp
from jax import lax
from jax.experimental import pallas as pl
from jax.experimental.pallas import tpu as pltpu
from jax.sharding import PartitionSpec as P

BLK = 512
HALF = BLK // 2
FOLD = BLK + 16
ITERS = 3
SLOTS = 2
QUAD = 4
EARLY = 3
BAND = 128
ROWS = 8
LANES = 128

damping = 0.01
F32 = jnp.float32
BF16 = jnp.bfloat16
SMEM = pl.BlockSpec(memory_space=pltpu.SMEM)
VMEM = pl.BlockSpec(memory_space=pltpu.VMEM)
ANY = pl.BlockSpec(memory_space=pl.ANY)


def params(mib):
    return pltpu.CompilerParams(vmem_limit_bytes=mib * 2**20)


def dot(left, right, dims=((1,), (0,))):
    return lax.dot_general(left, right, (dims, ((), ())), preferred_element_type=F32)


def places():
    row = lax.broadcasted_iota(jnp.int32, (HALF, HALF), 0)
    col = lax.broadcasted_iota(jnp.int32, (HALF, HALF), 1)
    return row, col


def fold(first, last):
    row, col = places()
    body = jnp.where(row <= col, first, last)
    diagonal = jnp.sum(jnp.where(row == col, last, 0.0), axis=0, keepdims=True)
    return body, jnp.broadcast_to(diagonal, (FOLD - BLK, HALF))


def unfold(body, diagonal):
    row, col = places()
    turned = body.T
    first = jnp.where(row <= col, body, turned)
    last = jnp.where(row > col, body, jnp.where(row < col, turned, diagonal))
    return first, last


def stat_kernel(order, x_ref, *out):
    for place in (1, 2, 3, 0):
        start = pl.multiple_of(order[place] * BLK, BLK)
        left = x_ref[:, pl.ds(start, HALF)]
        right = x_ref[:, pl.ds(pl.multiple_of(start + HALF, HALF), HALF)]
        along = ((0,), (0,))
        out[place][:HALF] = dot(left, right, along).astype(BF16)
        body, diagonal = fold(dot(left, left, along), dot(right, right, along))
        out[place][HALF:BLK] = body.astype(BF16)
        out[place][BLK:] = diagonal.astype(BF16)


def statistics(order, activations):
    return pl.pallas_call(
        stat_kernel,
        out_shape=[jax.ShapeDtypeStruct((FOLD, HALF), BF16)] * QUAD,
        in_specs=[SMEM, VMEM],
        out_specs=[VMEM] * QUAD,
        compiler_params=params(12),
        name="statistics",
    )(order, activations)


def chunks(width, size):
    start = 0
    while width - start >= 2 * size:
        yield pl.ds(start, size)
        start += size
    yield pl.ds(start, width - start)


def gram_kernel(order, after, g_ref, *refs):
    held, folded = refs[:QUAD], refs[QUAD : 2 * QUAD]
    norm_ref, left, last, arrived = refs[2 * QUAD :]
    parts = list(chunks(g_ref.shape[1], 1792))

    def copy(place, index):
        rows = pl.ds(pl.multiple_of(order[place] * BLK, BLK), BLK)
        return pltpu.make_async_copy(
            g_ref.at[rows, parts[index]], held[place].at[:, parts[index]], arrived.at[place, index]
        )

    for place in range(QUAD):
        for index in range(len(parts)):
            copy(place, index).start()
    norm_ref[...] = jnp.zeros_like(norm_ref)
    row, col = places()
    for place in range(QUAD):
        for index in range(len(parts)):
            copy(place, index).wait()
        whole = held[place][...]
        across = ((1,), (1,))
        left[...] = dot(whole, whole[:HALF], across)
        last[...] = dot(whole[HALF:], whole[HALF:], across)
        squares = jnp.where(row == col, left[:HALF] + last[...], 0.0)
        norm_ref[...] += jnp.sum(squares, axis=0, keepdims=True)
        body, diagonal = fold(left[:HALF], last[...])
        folded[place][:HALF] = left[HALF:].astype(BF16)
        folded[place][HALF:BLK] = body.astype(BF16)
        folded[place][BLK:] = diagonal.astype(BF16)


def gram(order, gradient, after):
    rows, columns = gradient.shape
    parts = len(list(chunks(columns, 1792)))
    results = pl.pallas_call(
        gram_kernel,
        out_shape=[pltpu.VMEM((BLK, columns), BF16)] * QUAD
        + [jax.ShapeDtypeStruct((FOLD, HALF), BF16)] * QUAD
        + [jax.ShapeDtypeStruct((1, HALF), F32)],
        in_specs=[SMEM, ANY, ANY],
        out_specs=[VMEM] * (2 * QUAD + 1),
        scratch_shapes=[
            pltpu.VMEM((BLK, HALF), F32),
            pltpu.VMEM((HALF, HALF), F32),
            pltpu.SemaphoreType.DMA((QUAD, parts)),
        ],
        compiler_params=params(12),
        cost_estimate=pl.CostEstimate(
            flops=2 * rows * columns * BLK, bytes_accessed=2 * rows * columns, transcendentals=0
        ),
        name="gram",
    )(order, after, pltpu.with_memory_space_constraint(gradient, pltpu.HBM))
    return results[:QUAD], results[QUAD : 2 * QUAD], results[-1]


def product(left, right):
    return dot(left.astype(BF16), right.astype(BF16))


def newton_kernel(tokens, after, mine, other, root, held):
    total = (mine[...].astype(F32) + other[...].astype(F32)) / tokens
    cross = total[:HALF]
    first, last = unfold(total[HALF:BLK], total[BLK : BLK + 1])
    held[:HALF, :HALF] = first
    held[:HALF, HALF:] = cross
    held[HALF:, :HALF] = cross.T
    held[HALF:, HALF:] = last
    row = lax.broadcasted_iota(jnp.int32, (BLK, BLK), 0)
    col = lax.broadcasted_iota(jnp.int32, (BLK, BLK), 1)
    identity = jnp.where(row == col, 1.0, 0.0).astype(F32)
    matrix = held[...] + damping * identity
    bound = jnp.max(jnp.sum(jnp.abs(matrix), axis=0, keepdims=True), axis=1, keepdims=True)
    scale = 2.0 / bound
    iterate = matrix * scale
    estimate = None
    for step in range(ITERS):
        error = (identity - iterate) * 0.25
        if estimate is None:
            estimate = error
        else:
            estimate = estimate + error + product(estimate, error)
        if step + 1 < ITERS:
            square = 2.0 * error + product(error, error)
            fourth = 2.0 * square + product(square, square)
            iterate = iterate + product(fourth, iterate)
    held[...] = (estimate + identity) * jnp.sqrt(jnp.sqrt(scale))
    root[:HALF] = held[:HALF, HALF:].astype(BF16)
    body, diagonal = fold(held[:HALF, :HALF], held[HALF:, HALF:])
    root[HALF:BLK] = body.astype(BF16)
    root[BLK:] = diagonal.astype(BF16)


def newton(tokens, after, mine, other):
    return pl.pallas_call(
        functools.partial(newton_kernel, tokens),
        out_shape=jax.ShapeDtypeStruct((FOLD, HALF), BF16),
        in_specs=[ANY, VMEM, VMEM],
        out_specs=VMEM,
        scratch_shapes=[pltpu.VMEM((BLK, BLK), F32)],
        compiler_params=params(12),
        cost_estimate=pl.CostEstimate(
            flops=16 * BLK**3, bytes_accessed=8 * BLK * BLK, transcendentals=0
        ),
        name="newton",
    )(after, mine, other)


def unfold_root(folded, root_ref):
    cross = folded[:HALF]
    rest = folded[HALF:].astype(F32)
    first, last = unfold(rest[:HALF], rest[HALF : HALF + 1])
    root_ref[:HALF, :HALF] = first.astype(BF16)
    root_ref[:HALF, HALF:] = cross
    root_ref[HALF:, :HALF] = cross.astype(F32).T.astype(BF16)
    root_ref[HALF:, HALF:] = last.astype(BF16)


def norm_kernel(folded, mine, from_y, from_z, squares, total_ref, root):
    unfold_root(folded, root)
    grams = mine[...].astype(F32) + from_y[...].astype(F32) + from_z[...].astype(F32)
    first = dot(root[:HALF], root[:, :HALF])
    lower = dot(root[HALF:], root[...])
    cross, last = lower[:, :HALF], lower[:, HALF:]
    row, col = places()
    weights = jnp.where(row < col, 2.0 * first, jnp.where(row > col, 2.0 * last, first))
    terms = weights * grams[HALF:BLK] + 2.0 * cross * grams[:HALF]
    terms += jnp.where(row == col, last, 0.0) * grams[BLK : BLK + 1]
    lanes = lambda value: sum(value[:, i : i + LANES] for i in range(0, HALF, LANES))
    new = lanes(jnp.sum(terms, axis=0, keepdims=True))
    row = lax.broadcasted_iota(jnp.int32, total_ref.shape, 0)
    total_ref[...] = jnp.where(row == 0, lanes(squares[...]), jnp.where(row == 1, new, 0.0))


def norm(*operands):
    return pl.pallas_call(
        norm_kernel,
        out_shape=jax.ShapeDtypeStruct((ROWS, LANES), F32),
        in_specs=[VMEM] * 5,
        out_specs=VMEM,
        scratch_shapes=[pltpu.VMEM((BLK, BLK), BF16)],
        compiler_params=params(12),
        name="norm",
    )(*operands)


def multiply_kernel(after, folded, held_ref, u_ref, root_ref):
    unfold_root(folded, root_ref)
    for part in chunks(u_ref.shape[1], BLK):
        u_ref[:, part] = dot(root_ref[...], held_ref[:, part]).astype(BF16)


def multiply(folded, held, after):
    return pl.pallas_call(
        multiply_kernel,
        out_shape=[pltpu.VMEM(held.shape, BF16), jax.ShapeDtypeStruct((BLK, BLK), BF16)],
        in_specs=[ANY, VMEM, VMEM],
        out_specs=[VMEM] * 2,
        input_output_aliases={2: 0},
        compiler_params=params(12),
        cost_estimate=pl.CostEstimate(flops=1880000000, bytes_accessed=1, transcendentals=0),
        name="multiply",
    )(after, folded, held)


def finish_kernel(order, owner_slot, sums, *refs):
    roots, folded, blocks = refs[:EARLY], refs[EARLY:QUAD], refs[QUAD : 2 * QUAD]
    update_ref, owned_ref = refs[2 * QUAD : 2 * QUAD + 2]
    scaled = refs[2 * QUAD + 2 : 3 * QUAD + 2]
    late, empty, sent, stored = refs[3 * QUAD + 2 :]
    both = jnp.sum(sums[...], axis=1, keepdims=True)
    ratio = jnp.sqrt(both[:1] / (both[1:2] + 1e-06))
    columns = blocks[0].shape[1]
    waits = []

    def send(place, rows, columns):
        at = pl.multiple_of(order[place] * BLK + rows.start, rows.size)
        copy = pltpu.make_async_copy(
            scaled[place].at[rows, columns],
            update_ref.at[pl.ds(at, rows.size), columns],
            sent.at[len(waits)],
        )
        copy.start()
        waits.append(copy)

    def store(source, slot):
        return pltpu.make_async_copy(source, owned_ref.at[slot], stored.at[slot])

    def rescale(place, rows):
        scaled[place][rows] = (blocks[place][rows].astype(F32) * ratio).astype(BF16)

    bands = [(place, pl.ds(i, BAND)) for place in range(EARLY) for i in range(0, BLK, BAND)]
    products = [(place, part) for place in range(EARLY, QUAD) for part in chunks(columns, BLK)]
    ahead = 1
    for one in bands[:ahead]:
        rescale(*one)
        send(*one, pl.ds(0, columns))
    bands = bands[ahead:]
    empty[...] = jnp.zeros_like(empty)
    for place in range(EARLY, QUAD):
        unfold_root(folded[place - EARLY], late.at[place - EARLY])
    for slot in range(SLOTS):
        mine = [owner_slot[order[QUAD], order[place]] == order[QUAD + 1] + slot for place in range(QUAD)]
        for place in range(QUAD):
            source = roots[place] if place < EARLY else late.at[place - EARLY]
            pl.when(mine[place])(store(source, slot).start)
        pl.when(jnp.logical_not(functools.reduce(jnp.logical_or, mine)))(store(empty, slot).start)
    for place, part in products:
        product = dot(late[place - EARLY], blocks[place][:, part])
        scaled[place][:, part] = (product * ratio).astype(BF16)
        band, bands = bands[:1], bands[1:]
        for one in band:
            rescale(*one)
            send(*one, pl.ds(0, columns))
        send(place, pl.ds(0, BLK), part)
    for one in bands:
        rescale(*one)
        send(*one, pl.ds(0, columns))
    for copy in waits:
        copy.wait()
    for slot in range(SLOTS):
        store(empty, slot).wait()


def finish(order, owner_slot, sums, roots, folded, blocks):
    columns = blocks[0].shape[1]
    pieces = EARLY * (BLK // BAND) + (QUAD - EARLY) * len(list(chunks(columns, BLK)))
    return pl.pallas_call(
        finish_kernel,
        out_shape=[
            jax.ShapeDtypeStruct((QUAD * BLK, columns), BF16),
            jax.ShapeDtypeStruct((SLOTS, BLK, BLK), BF16),
        ]
        + [pltpu.VMEM((BLK, columns), BF16)] * QUAD,
        in_specs=[SMEM] * 2 + [VMEM] * (1 + 2 * QUAD),
        out_specs=[ANY] * 2 + [VMEM] * QUAD,
        input_output_aliases={3 + QUAD + place: 2 + place for place in range(QUAD)},
        scratch_shapes=[
            pltpu.VMEM((QUAD - EARLY, BLK, BLK), BF16),
            pltpu.VMEM((BLK, BLK), BF16),
            pltpu.SemaphoreType.DMA((pieces,)),
            pltpu.SemaphoreType.DMA((SLOTS,)),
        ],
        compiler_params=params(12),
        name="finish",
    )(order, owner_slot, sums, *roots, *folded, *blocks)[:2]


def swap(value, flip):
    axes = ("pool", "dp")
    count = math.prod(lax.axis_size(axis) for axis in axes)
    return lax.ppermute(value, axes, [(i, i ^ flip) for i in range(count)])


def rounds():
    peer_bits = lax.axis_size("dp").bit_length() - 1
    bits = [1 << i for i in range(peer_bits + lax.axis_size("pool").bit_length() - 1)]
    first = [bits[2], bits[-1], bits[2] + bits[-1]] if peer_bits > 2 else [bits[-1]]
    return [first] + [[bit] for bit in (bits[0], *bits[peer_bits:-1], bits[1], *bits[3:peer_bits])]


def add(*values):
    return sum(value.astype(F32) for value in values).astype(BF16)


def per_device(activations, gradient, owner_slot):
    peer_count = lax.axis_size("dp")
    my_index = lax.axis_index("dp")
    group_index = lax.axis_index("pool")
    tokens_all = activations.shape[0] * peer_count
    order = (my_index % QUAD) ^ jnp.arange(QUAD, dtype=jnp.int32)
    order = jnp.concatenate([order, jnp.stack([group_index, my_index * SLOTS])])

    a, b, c, d = statistics(order, activations)
    b, c, d = swap(b, 1), swap(c, 2), swap(d, 3)
    blocks, grams, squares = gram(order, gradient, a)
    mine = add(a, b, c, d)
    flip = QUAD
    other = swap(mine, flip)
    grams = list(grams)
    while 2 * flip < peer_count:
        mine = add(mine, other)
        flip *= 2
        other = swap(mine, flip)

    across = swap(grams[3], 1)
    across, grams[1] = lax.optimization_barrier((across, grams[1]))
    from_y = swap(grams[1], 1)
    from_z = swap(add(grams[2], across), 2)
    root = newton(tokens_all, squares, mine, other)
    folded = [root, swap(root, 1), swap(root, 2)]
    blocks, roots = list(blocks), []

    def precondition(place):
        blocks[place], root = multiply(folded[place], blocks[place], folded[place])
        roots.append(root)

    sums = norm(root, grams[0], from_y, from_z, squares)
    early, arrivals = {0:[0],1:[1],3:[2]}, {0:[1,2],3:[3]}
    for step, flips in enumerate(rounds()):
        received = [swap(sums, flip) for flip in flips]
        if step == 1:
            folded[2], _ = lax.optimization_barrier((folded[2], sums))
            folded.append(swap(folded[2], 1))
        for place in early.get(step, ()):
            precondition(place)
            blocks[place], *received = lax.optimization_barrier((blocks[place], *received))
        for place in arrivals.get(step, ()):
            folded[place], *received = lax.optimization_barrier((folded[place], *received))
        sums = sums + sum(received)
    update, owned = finish(order, owner_slot, sums, roots, folded[EARLY:], blocks)
    return (update, owned[None])


def solution(mesh):
    in_specs = (P("dp", "pool"), P("pool", "dp"), P())
    out_specs = (P("pool", "dp"), P("pool", "dp", None, None))
    return jax.shard_map(
        per_device, mesh=mesh, in_specs=in_specs, out_specs=out_specs, check_vma=False
    )
```

```python
import functools
import math

import jax
import jax.numpy as jnp
from jax import lax
from jax.experimental import pallas as pl
from jax.experimental.pallas import tpu as pltpu
from jax.sharding import PartitionSpec as P

BLK = 512
HALF = BLK // 2
FOLD = BLK + 16
ITERS = 3
SLOTS = 2
QUAD = 4
EARLY = 3
BAND = 128
ROWS = 8
LANES = 128

damping = 0.01
F32 = jnp.float32
BF16 = jnp.bfloat16
SMEM = pl.BlockSpec(memory_space=pltpu.SMEM)
VMEM = pl.BlockSpec(memory_space=pltpu.VMEM)
ANY = pl.BlockSpec(memory_space=pl.ANY)


def params(mib):
    return pltpu.CompilerParams(vmem_limit_bytes=mib * 2**20)


def dot(left, right, dims=((1,), (0,))):
    return lax.dot_general(left, right, (dims, ((), ())), preferred_element_type=F32)


def places():
    row = lax.broadcasted_iota(jnp.int32, (HALF, HALF), 0)
    col = lax.broadcasted_iota(jnp.int32, (HALF, HALF), 1)
    return row, col


def fold(first, last):
    row, col = places()
    body = jnp.where(row <= col, first, last)
    diagonal = jnp.sum(jnp.where(row == col, last, 0.0), axis=0, keepdims=True)
    return body, jnp.broadcast_to(diagonal, (FOLD - BLK, HALF))


def unfold(body, diagonal):
    row, col = places()
    turned = body.T
    first = jnp.where(row <= col, body, turned)
    last = jnp.where(row > col, body, jnp.where(row < col, turned, diagonal))
    return first, last


def stat_kernel(order, x_ref, *out):
    for place in (1, 2, 3, 0):
        start = pl.multiple_of(order[place] * BLK, BLK)
        left = x_ref[:, pl.ds(start, HALF)]
        right = x_ref[:, pl.ds(pl.multiple_of(start + HALF, HALF), HALF)]
        along = ((0,), (0,))
        out[place][:HALF] = dot(left, right, along).astype(BF16)
        body, diagonal = fold(dot(left, left, along), dot(right, right, along))
        out[place][HALF:BLK] = body.astype(BF16)
        out[place][BLK:] = diagonal.astype(BF16)


def statistics(order, activations):
    return pl.pallas_call(
        stat_kernel,
        out_shape=[jax.ShapeDtypeStruct((FOLD, HALF), BF16)] * QUAD,
        in_specs=[SMEM, VMEM],
        out_specs=[VMEM] * QUAD,
        compiler_params=params(12),
        name="statistics",
    )(order, activations)


def chunks(width, size):
    start = 0
    while width - start >= 2 * size:
        yield pl.ds(start, size)
        start += size
    yield pl.ds(start, width - start)


def gram_kernel(places_held, order, after, g_ref, *refs):
    count = len(places_held)
    held, folded = refs[:count], refs[count : 2 * count]
    norm_ref, left, last, arrived = refs[2 * count :]
    parts = list(chunks(g_ref.shape[1], 1792))

    def copy(place, index):
        rows = pl.ds(pl.multiple_of(order[places_held[place]] * BLK, BLK), BLK)
        return pltpu.make_async_copy(
            g_ref.at[rows, parts[index]], held[place].at[:, parts[index]], arrived.at[place, index]
        )

    for place in range(count):
        for index in range(len(parts)):
            copy(place, index).start()
    norm_ref[...] = jnp.zeros_like(norm_ref)
    row, col = places()
    for place in range(count):
        for index in range(len(parts)):
            copy(place, index).wait()
        whole = held[place][...]
        across = ((1,), (1,))
        left[...] = dot(whole, whole[:HALF], across)
        last[...] = dot(whole[HALF:], whole[HALF:], across)
        squares = jnp.where(row == col, left[:HALF] + last[...], 0.0)
        norm_ref[...] += jnp.sum(squares, axis=0, keepdims=True)
        body, diagonal = fold(left[:HALF], last[...])
        folded[place][:HALF] = left[HALF:].astype(BF16)
        folded[place][HALF:BLK] = body.astype(BF16)
        folded[place][BLK:] = diagonal.astype(BF16)


def gram(places_held, order, gradient, after):
    count, columns = len(places_held), gradient.shape[1]
    rows = count * BLK
    parts = len(list(chunks(columns, 1792)))
    results = pl.pallas_call(
        functools.partial(gram_kernel, places_held),
        out_shape=[pltpu.VMEM((BLK, columns), BF16)] * count
        + [jax.ShapeDtypeStruct((FOLD, HALF), BF16)] * count
        + [jax.ShapeDtypeStruct((1, HALF), F32)],
        in_specs=[SMEM, ANY, ANY],
        out_specs=[VMEM] * (2 * count + 1),
        scratch_shapes=[
            pltpu.VMEM((BLK, HALF), F32),
            pltpu.VMEM((HALF, HALF), F32),
            pltpu.SemaphoreType.DMA((count, parts)),
        ],
        compiler_params=params(12),
        cost_estimate=pl.CostEstimate(
            flops=2 * rows * columns * BLK, bytes_accessed=2 * rows * columns, transcendentals=0
        ),
        name="gram",
    )(order, after, pltpu.with_memory_space_constraint(gradient, pltpu.HBM))
    return list(results[:count]), list(results[count : 2 * count]), results[-1]


def product(left, right):
    return dot(left.astype(BF16), right.astype(BF16))


def newton_kernel(tokens, after, mine, other, root, held):
    total = (mine[...].astype(F32) + other[...].astype(F32)) / tokens
    cross = total[:HALF]
    first, last = unfold(total[HALF:BLK], total[BLK : BLK + 1])
    held[:HALF, :HALF] = first
    held[:HALF, HALF:] = cross
    held[HALF:, :HALF] = cross.T
    held[HALF:, HALF:] = last
    row = lax.broadcasted_iota(jnp.int32, (BLK, BLK), 0)
    col = lax.broadcasted_iota(jnp.int32, (BLK, BLK), 1)
    identity = jnp.where(row == col, 1.0, 0.0).astype(F32)
    matrix = held[...] + damping * identity
    bound = jnp.max(jnp.sum(jnp.abs(matrix), axis=0, keepdims=True), axis=1, keepdims=True)
    scale = 2.0 / bound
    iterate = matrix * scale
    estimate = None
    for step in range(ITERS):
        error = (identity - iterate) * 0.25
        if estimate is None:
            estimate = error
        else:
            estimate = estimate + error + product(estimate, error)
        if step + 1 < ITERS:
            square = 2.0 * error + product(error, error)
            fourth = 2.0 * square + product(square, square)
            iterate = iterate + product(fourth, iterate)
    held[...] = (estimate + identity) * jnp.sqrt(jnp.sqrt(scale))
    root[:HALF] = held[:HALF, HALF:].astype(BF16)
    body, diagonal = fold(held[:HALF, :HALF], held[HALF:, HALF:])
    root[HALF:BLK] = body.astype(BF16)
    root[BLK:] = diagonal.astype(BF16)


def newton(tokens, after, mine, other):
    return pl.pallas_call(
        functools.partial(newton_kernel, tokens),
        out_shape=jax.ShapeDtypeStruct((FOLD, HALF), BF16),
        in_specs=[ANY, VMEM, VMEM],
        out_specs=VMEM,
        scratch_shapes=[pltpu.VMEM((BLK, BLK), F32)],
        compiler_params=params(12),
        cost_estimate=pl.CostEstimate(
            flops=16 * BLK**3, bytes_accessed=8 * BLK * BLK, transcendentals=0
        ),
        name="newton",
    )(after, mine, other)


def unfold_root(folded, root_ref):
    cross = folded[:HALF]
    rest = folded[HALF:].astype(F32)
    first, last = unfold(rest[:HALF], rest[HALF : HALF + 1])
    root_ref[:HALF, :HALF] = first.astype(BF16)
    root_ref[:HALF, HALF:] = cross
    root_ref[HALF:, :HALF] = cross.astype(F32).T.astype(BF16)
    root_ref[HALF:, HALF:] = last.astype(BF16)


def norm_kernel(folded, mine, from_y, from_z, squares, total_ref, root):
    unfold_root(folded, root)
    grams = mine[...].astype(F32) + from_y[...].astype(F32) + from_z[...].astype(F32)
    first = dot(root[:HALF], root[:, :HALF])
    lower = dot(root[HALF:], root[...])
    cross, last = lower[:, :HALF], lower[:, HALF:]
    row, col = places()
    weights = jnp.where(row < col, 2.0 * first, jnp.where(row > col, 2.0 * last, first))
    terms = weights * grams[HALF:BLK] + 2.0 * cross * grams[:HALF]
    terms += jnp.where(row == col, last, 0.0) * grams[BLK : BLK + 1]
    lanes = lambda value: sum(value[:, i : i + LANES] for i in range(0, HALF, LANES))
    new = lanes(jnp.sum(terms, axis=0, keepdims=True))
    row = lax.broadcasted_iota(jnp.int32, total_ref.shape, 0)
    total_ref[...] = jnp.where(row == 0, lanes(squares[...]), jnp.where(row == 1, new, 0.0))


def norm(*operands):
    return pl.pallas_call(
        norm_kernel,
        out_shape=jax.ShapeDtypeStruct((ROWS, LANES), F32),
        in_specs=[VMEM] * 5,
        out_specs=VMEM,
        scratch_shapes=[pltpu.VMEM((BLK, BLK), BF16)],
        compiler_params=params(12),
        name="norm",
    )(*operands)


def multiply_kernel(after, folded, held_ref, u_ref, root_ref):
    unfold_root(folded, root_ref)
    for part in chunks(u_ref.shape[1], BLK):
        u_ref[:, part] = dot(root_ref[...], held_ref[:, part]).astype(BF16)


def multiply(folded, held, after):
    return pl.pallas_call(
        multiply_kernel,
        out_shape=[pltpu.VMEM(held.shape, BF16), jax.ShapeDtypeStruct((BLK, BLK), BF16)],
        in_specs=[ANY, VMEM, VMEM],
        out_specs=[VMEM] * 2,
        input_output_aliases={2: 0},
        compiler_params=params(12),
        cost_estimate=pl.CostEstimate(flops=1880000000, bytes_accessed=1, transcendentals=0),
        name="multiply",
    )(after, folded, held)


def finish_kernel(order, owner_slot, sums, *refs):
    roots, folded, blocks = refs[:EARLY], refs[EARLY:QUAD], refs[QUAD : 2 * QUAD]
    update_ref, owned_ref = refs[2 * QUAD : 2 * QUAD + 2]
    scaled = refs[2 * QUAD + 2 : 3 * QUAD + 2]
    late, empty, sent, stored = refs[3 * QUAD + 2 :]
    both = jnp.sum(sums[...], axis=1, keepdims=True)
    ratio = jnp.sqrt(both[:1] / (both[1:2] + 1e-06))
    columns = blocks[0].shape[1]
    waits = []

    def send(place, rows, columns):
        at = pl.multiple_of(order[place] * BLK + rows.start, rows.size)
        copy = pltpu.make_async_copy(
            scaled[place].at[rows, columns],
            update_ref.at[pl.ds(at, rows.size), columns],
            sent.at[len(waits)],
        )
        copy.start()
        waits.append(copy)

    def store(source, slot):
        return pltpu.make_async_copy(source, owned_ref.at[slot], stored.at[slot])

    def rescale(place, rows):
        scaled[place][rows] = (blocks[place][rows].astype(F32) * ratio).astype(BF16)

    bands = [(place, pl.ds(i, BAND)) for place in range(EARLY) for i in range(0, BLK, BAND)]
    products = [(place, part) for place in range(EARLY, QUAD) for part in chunks(columns, BLK)]
    ahead = 1
    for one in bands[:ahead]:
        rescale(*one)
        send(*one, pl.ds(0, columns))
    bands = bands[ahead:]
    empty[...] = jnp.zeros_like(empty)
    for place in range(EARLY, QUAD):
        unfold_root(folded[place - EARLY], late.at[place - EARLY])
    for slot in range(SLOTS):
        mine = [owner_slot[order[QUAD], order[place]] == order[QUAD + 1] + slot for place in range(QUAD)]
        for place in range(QUAD):
            source = roots[place] if place < EARLY else late.at[place - EARLY]
            pl.when(mine[place])(store(source, slot).start)
        pl.when(jnp.logical_not(functools.reduce(jnp.logical_or, mine)))(store(empty, slot).start)
    for place, part in products:
        product = dot(late[place - EARLY], blocks[place][:, part])
        scaled[place][:, part] = (product * ratio).astype(BF16)
        band, bands = bands[:1], bands[1:]
        for one in band:
            rescale(*one)
            send(*one, pl.ds(0, columns))
        send(place, pl.ds(0, BLK), part)
    for one in bands:
        rescale(*one)
        send(*one, pl.ds(0, columns))
    for copy in waits:
        copy.wait()
    for slot in range(SLOTS):
        store(empty, slot).wait()


def finish(order, owner_slot, sums, roots, folded, blocks):
    columns = blocks[0].shape[1]
    pieces = EARLY * (BLK // BAND) + (QUAD - EARLY) * len(list(chunks(columns, BLK)))
    return pl.pallas_call(
        finish_kernel,
        out_shape=[
            jax.ShapeDtypeStruct((QUAD * BLK, columns), BF16),
            jax.ShapeDtypeStruct((SLOTS, BLK, BLK), BF16),
        ]
        + [pltpu.VMEM((BLK, columns), BF16)] * QUAD,
        in_specs=[SMEM] * 2 + [VMEM] * (1 + 2 * QUAD),
        out_specs=[ANY] * 2 + [VMEM] * QUAD,
        input_output_aliases={3 + QUAD + place: 2 + place for place in range(QUAD)},
        scratch_shapes=[
            pltpu.VMEM((QUAD - EARLY, BLK, BLK), BF16),
            pltpu.VMEM((BLK, BLK), BF16),
            pltpu.SemaphoreType.DMA((pieces,)),
            pltpu.SemaphoreType.DMA((SLOTS,)),
        ],
        compiler_params=params(12),
        name="finish",
    )(order, owner_slot, sums, *roots, *folded, *blocks)[:2]


def swap(value, flip):
    axes = ("pool", "dp")
    count = math.prod(lax.axis_size(axis) for axis in axes)
    return lax.ppermute(value, axes, [(i, i ^ flip) for i in range(count)])


def rounds():
    peer_bits = lax.axis_size("dp").bit_length() - 1
    bits = [1 << i for i in range(peer_bits + lax.axis_size("pool").bit_length() - 1)]
    first = [bits[2], bits[-1], bits[2] + bits[-1]] if peer_bits > 2 else [bits[-1]]
    return [first] + [[bit] for bit in (bits[0], *bits[peer_bits:-1], bits[1], *bits[3:peer_bits])]


def add(*values):
    return sum(value.astype(F32) for value in values).astype(BF16)


def per_device(activations, gradient, owner_slot):
    peer_count = lax.axis_size("dp")
    my_index = lax.axis_index("dp")
    group_index = lax.axis_index("pool")
    tokens_all = activations.shape[0] * peer_count
    order = (my_index % QUAD) ^ jnp.arange(QUAD, dtype=jnp.int32)
    order = jnp.concatenate([order, jnp.stack([group_index, my_index * SLOTS])])

    a, b, c, d = statistics(order, activations)
    b, c, d = swap(b, 1), swap(c, 2), swap(d, 3)
    blocks, grams, squares = gram((1, 2, 3), order, gradient, a)
    mine = add(a, b, c, d)
    own, own_gram, own_squares = gram((0,), order, gradient, mine)
    blocks, grams = own + blocks, own_gram + grams
    flip = QUAD
    other = swap(mine, flip)
    while 2 * flip < peer_count:
        mine = add(mine, other)
        flip *= 2
        other = swap(mine, flip)

    across = swap(grams[3], 1)
    across, grams[1] = lax.optimization_barrier((across, grams[1]))
    from_y = swap(grams[1], 1)
    from_z = swap(add(grams[2], across), 2)
    root = newton(tokens_all, own_squares, mine, other)
    folded = [root, swap(root, 1), swap(root, 2)]
    blocks, roots = list(blocks), []

    def precondition(place):
        blocks[place], root = multiply(folded[place], blocks[place], folded[place])
        roots.append(root)

    sums = norm(root, grams[0], from_y, from_z, squares + own_squares)
    early, arrivals = {0:[0],1:[1],3:[2]}, {0:[1,2],3:[3]}
    for step, flips in enumerate(rounds()):
        received = [swap(sums, flip) for flip in flips]
        if step == 1:
            folded[2], _ = lax.optimization_barrier((folded[2], sums))
            folded.append(swap(folded[2], 1))
        for place in early.get(step, ()):
            precondition(place)
            blocks[place], *received = lax.optimization_barrier((blocks[place], *received))
        for place in arrivals.get(step, ()):
            folded[place], *received = lax.optimization_barrier((folded[place], *received))
        sums = sums + sum(received)
    update, owned = finish(order, owner_slot, sums, roots, folded[EARLY:], blocks)
    return (update, owned[None])


def solution(mesh):
    in_specs = (P("dp", "pool"), P("pool", "dp"), P())
    out_specs = (P("pool", "dp"), P("pool", "dp", None, None))
    return jax.shard_map(
        per_device, mesh=mesh, in_specs=in_specs, out_specs=out_specs, check_vma=False
    )
```
